32 devices in a mesh: tok: 4 (over y, core), head: 8 (over z, x).
Axes of the slice: x: 2, y: 2, z: 4, core: 2. Of those that a mesh axis runs over, the one named last changes fastest.
Arguments:
- tokens: bfloat16 [2048, 4096], P('tok', 'head'), may hold values from -32 to 32
- w_query: bfloat16 [4096, 4096], P(None, 'head'), may hold values from -0.09375 to 0.09375
- w_key: bfloat16 [4096, 4096], P(None, 'head'), may hold values from -0.09375 to 0.09375
- w_value: bfloat16 [4096, 4096], P(None, 'head'), may hold values from -0.09375 to 0.09375
- w_out: bfloat16 [4096, 4096], P('head'), may hold values from -0.09375 to 0.09375
- fast_gate: float32 [32, 128, 256], P('head'), may hold values from -0.5 to 0.5
- fast_up: float32 [32, 128, 256], P('head'), may hold values from -0.5 to 0.5
- fast_down: float32 [32, 256, 128], P('head'), may hold values from -0.375 to 0.375
- token_rate: float32 [2048, 32], P('tok', 'head'), may hold values from 0.05 to 1
- head_step: float32 [32], P('head'), may hold values from 0.2 to 1
Outputs:
- mixed: bfloat16 [2048, 4096], P(('tok', 'head'))
The draws below stay inside these ranges and needn't reach their ends.
All inputs are finite; a program needn't handle non-finite values.
Results may differ from the reference program's by a relative error of at most 0.022.
Values may be sent and summed in bfloat16 or wider, within the bound.
No kernel may reach another device: no remote copies, remote signals or barrier semaphores. Data moves between devices by JAX's collectives and lax.ppermute only.
A program may use at most 64 MiB of HBM per device.

```python
import math
import jax
import jax.numpy as jnp
from jax import lax

HEADS = 32
HEAD_DIM = 128
FAST_HID = 256
WINDOW = 512
TOK_DEV = 512
D = 4096
TOKENS = 2048


def draw_tokens(key, part):
    first_key = jax.random.fold_in(key, 11)
    base = jnp.clip(jax.random.normal(first_key, (TOKENS, D), jnp.float32), -4.0, 4.0)
    return base.astype(jnp.bfloat16)


def level_of(own_key, shape, pieces, least, largest):
    def one(position, shards_of):
        draws = jax.random.uniform(jax.random.fold_in(jax.random.fold_in(own_key, 6), position), (shards_of,), jnp.float32, least / len(pieces), largest / len(pieces))
        return jnp.repeat(jnp.exp(draws), shape[position] // shards_of).reshape((-1,) + (1,) * (len(shape) - position - 1))

    level = one(*pieces[0])
    for cut in pieces[1:]:
        level = level * one(*cut)
    return level


def bell_draw(own_key, extent, width, most, cuts=(), kind=jnp.bfloat16):
    values = jax.random.normal(own_key, extent, jnp.float32) * width
    if len(cuts) > 0:
        values = level_of(own_key, extent, cuts, -0.22, 0.18) * values
    return jnp.clip(values, min=-most, max=most).astype(kind)


def setup_inputs(seed: int = 0) -> dict:
    arg_keys = jax.random.split(jax.random.key(seed), 11)
    return {
        "tokens": draw_tokens(jax.random.fold_in(arg_keys[10], 71), 0),
        "w_query": bell_draw(arg_keys[1], (D, D), D ** -0.5, 0.09375, ((1, 8),)),
        "w_key": bell_draw(arg_keys[2], (D, D), D ** -0.5, 0.09375, ((1, 8),)),
        "w_value": bell_draw(arg_keys[3], (D, D), D ** -0.5, 0.09375, ((1, 8),)),
        "w_out": bell_draw(arg_keys[4], (D, D), D ** -0.5, 0.09375, ((0, 8),)),
        "fast_gate": bell_draw(arg_keys[5], (HEADS, HEAD_DIM, FAST_HID), HEAD_DIM ** -0.5, 0.5, ((0, 8),), jnp.float32),
        "fast_up": bell_draw(arg_keys[6], (HEADS, HEAD_DIM, FAST_HID), HEAD_DIM ** -0.5, 0.5, ((0, 8),), jnp.float32),
        "fast_down": bell_draw(arg_keys[7], (HEADS, FAST_HID, HEAD_DIM), FAST_HID ** -0.5, 0.375, ((0, 8),), jnp.float32),
        "token_rate": jnp.clip(jnp.exp(math.log(1.0) - 2.9957323 * jax.random.uniform(arg_keys[8], (TOKENS, HEADS), jnp.float32) ** level_of(arg_keys[8], (TOKENS, HEADS), ((0, 4), (1, 8)), -0.2, 0.2)), 0.05, 1.0),
        "head_step": jnp.clip(jnp.exp(math.log(1.0) - 1.609438 * jax.random.uniform(arg_keys[9], (HEADS,), jnp.float32) ** level_of(arg_keys[9], (HEADS,), ((0, 8),), -0.2, 0.2)), 0.2, 1.0),
    }


def rms(values):
    return values * lax.rsqrt(lax.optimization_barrier(jnp.mean(values * values, axis=-1, keepdims=True)) + 1e-06)

def matmul(left, right):
    return jnp.dot(left, right, precision=lax.Precision.HIGHEST)

def fast_apply(inputs, gate, upper, down):
    gate_pre = matmul(inputs, gate)
    return matmul(jax.nn.silu(gate_pre) * matmul(inputs, upper), down)

def renew(matrix, grad, step, fan_in):
    mean_sq = jnp.mean(grad * grad)
    return matrix - step * grad * lax.rsqrt(mean_sq + 1e-06) * fan_in ** (-0.5)

def one_head(items):
    query_h, key_h, value_h, rate_h, gate, upper, down, step = items
    knorm = rms(key_h.astype(jnp.float32))
    qnorm = rms(query_h.astype(jnp.float32))
    target = -rate_h[:, None] * value_h.astype(jnp.float32)
    gate_pre = matmul(knorm, gate)
    up_pre = matmul(knorm, upper)
    sigma = jax.nn.sigmoid(gate_pre)
    active = gate_pre * sigma
    hidden = active * up_pre
    grad_down = matmul(hidden.T, target)
    back = matmul(target, down.T)
    grad_up = matmul(knorm.T, back * active)
    grad_gate = matmul(knorm.T, back * up_pre * sigma * (1.0 + gate_pre * (1.0 - sigma)))
    new_gate = renew(gate, grad_gate, step, HEAD_DIM)
    new_up = renew(upper, grad_up, step, HEAD_DIM)
    new_down = renew(down, grad_down, step, FAST_HID)
    return fast_apply(qnorm, new_gate, new_up, new_down)

def reference(tokens, w_query, w_key, w_value, w_out, fast_gate, fast_up, fast_down, token_rate, head_step):
    shape = (TOKENS, HEADS, HEAD_DIM)
    query = jnp.dot(tokens, w_query, preferred_element_type=jnp.float32).astype(jnp.bfloat16).reshape(shape)
    key = jnp.dot(tokens, w_key, preferred_element_type=jnp.float32).astype(jnp.bfloat16).reshape(shape)
    value = jnp.dot(tokens, w_value, preferred_element_type=jnp.float32).astype(jnp.bfloat16).reshape(shape)
    padding = jnp.zeros((WINDOW, HEADS, HEAD_DIM), jnp.bfloat16)
    key_pad = jnp.concatenate([padding, key], axis=0)
    value_pad = jnp.concatenate([padding, value], axis=0)

    def block(index):
        first = index * TOK_DEV
        query_b = lax.dynamic_slice_in_dim(query, first, TOK_DEV, 0).astype(jnp.float32)
        key_b = lax.dynamic_slice_in_dim(key_pad, first, TOK_DEV + WINDOW, 0).astype(jnp.float32)
        value_b = lax.dynamic_slice_in_dim(value_pad, first, TOK_DEV + WINDOW, 0).astype(jnp.float32)
        query_pos = first + jnp.arange(TOK_DEV, dtype=jnp.int32)
        key_pos = first - WINDOW + jnp.arange(TOK_DEV + WINDOW, dtype=jnp.int32)
        allowed = (key_pos[None, :] >= 0) & (key_pos[None, :] <= query_pos[:, None]) & (key_pos[None, :] > query_pos[:, None] - WINDOW)
        scores = jnp.einsum('qhd,khd->hqk', query_b, key_b) * HEAD_DIM ** (-0.5)
        scores = jnp.where(allowed[None], scores, jnp.float32(-1e+30))
        top = lax.optimization_barrier(jnp.max(scores, axis=-1, keepdims=True))
        expo = jnp.exp(scores - top)
        weights = (expo / lax.optimization_barrier(jnp.sum(expo, axis=-1, keepdims=True))).astype(jnp.bfloat16)
        return jnp.einsum('hqk,khd->qhd', weights.astype(jnp.float32), value_b)
    attended = lax.map(block, jnp.arange(TOKENS // TOK_DEV, dtype=jnp.int32)).reshape(shape)
    items = (jnp.transpose(query, (1, 0, 2)), jnp.transpose(key, (1, 0, 2)), jnp.transpose(value, (1, 0, 2)), token_rate.T, fast_gate, fast_up, fast_down, head_step)
    fast_out = jnp.transpose(lax.map(one_head, items), (1, 0, 2))
    combined = (attended + fast_out).astype(jnp.bfloat16).reshape(TOKENS, D)
    return jnp.dot(combined, w_out, preferred_element_type=jnp.float32).astype(jnp.bfloat16)
```

```python
import functools

import jax
import jax.numpy as jnp
from jax import lax
from jax.experimental import pallas as pl
from jax.experimental.pallas import tpu as pltpu
from jax.sharding import PartitionSpec as P

WINDOW = 512
CHUNKS = 2
F32 = jnp.float32
BF16 = jnp.bfloat16
LOG2E = 1.4426950408889634


def call(body, grid, in_specs, out_specs, out_shape, scratch=(), prefetch=1, vmem=48):
    return pl.pallas_call(
        body,
        grid_spec=pltpu.PrefetchScalarGridSpec(
            num_scalar_prefetch=prefetch,
            grid=grid,
            in_specs=in_specs,
            out_specs=out_specs,
            scratch_shapes=list(scratch),
        ),
        out_shape=out_shape,
        compiler_params=pltpu.CompilerParams(vmem_limit_bytes=vmem * 1024 * 1024),
    )


def fixed(shape):
    return pl.BlockSpec(shape, lambda *_: (0,) * len(shape))


def mm(left, right, dims=((1,), (0,))):
    return lax.dot_general(left, right, (dims, ((), ())), preferred_element_type=F32)


def sigmoid(x):
    return 0.5 * jnp.tanh(0.5 * x) + 0.5


def ring_order(count):
    return list(range(0, count, 2)) + list(range(count - 1, 0, -2))


def ring_send(value, step):
    order = ring_order(lax.axis_size("head"))
    count = len(order)
    return lax.ppermute(
        value, "head", [(order[i], order[(i + step) % count]) for i in range(count)]
    )


def ring_ids(offsets):
    count = lax.axis_size("head")
    me = lax.axis_index("head")
    place = jnp.where(me % 2 == 0, me // 2, count - 1 - me // 2)
    ids = []
    for offset in offsets:
        at = (place + offset) % count
        ids.append(jnp.where(at < count // 2, 2 * at, 2 * (count - 1 - at) + 1))
    return jnp.stack(ids).astype(jnp.int32)


def gather_pieces(own):
    count = lax.axis_size("head")
    half = own.shape[0] // 2
    pieces = [own]
    up, down = own, own
    for _ in range(1, count // 2):
        up, down = ring_send(up, 1), ring_send(down, -1)
        pieces += [up, down]
    return pieces + [ring_send(up[:half], 1), ring_send(down[half:], -1)]


def project(ids, pieces, weights):
    rows, depth = pieces[0].shape
    width = weights[0].shape[1]
    half = rows // 2
    count = len(pieces) - 1
    parts = len(weights)

    def body(ids_ref, *refs):
        piece_refs = refs[: count + 1]
        weight_refs = refs[count + 1 : count + 1 + parts]
        out_ref, acc = refs[-2:]
        step = pl.program_id(0)

        for index in range(count):

            @pl.when(step == index)
            def _(index=index):
                for part in range(parts):
                    weight = weight_refs[part][...]
                    if index < count - 1:
                        term = mm(piece_refs[index][...], weight)
                        if index == 0:
                            acc[part] = term
                        else:
                            acc[part] += term
                    else:
                        for side in range(2):
                            where = slice(side * half, (side + 1) * half)
                            term = mm(piece_refs[index + side][...], weight)
                            out_ref[part, where] = (acc[part, where] + term).astype(BF16)

    return call(
        body,
        (count,),
        [fixed(piece.shape) for piece in pieces]
        + [pl.BlockSpec((depth, width), lambda k, ids_ref: (ids_ref[k], 0))] * parts,
        fixed((parts, rows, width)),
        jax.ShapeDtypeStruct((parts, rows, width), BF16),
        [pltpu.VMEM((parts, rows, width), F32)],
    )(ids, *pieces, *weights)


def head_grads(base, heads, kv, rate, fast_gate, fast_up, fast_down, before):
    rows = kv.shape[1]
    size, hidden_size = fast_gate.shape[1:]
    lanes = rate.shape[1]

    def body(base_ref, k_ref, v_ref, rate_ref, gate_ref, up_ref, down_ref, *rest):
        out_ref = rest[-1]
        head = base_ref[0] + pl.program_id(0)
        lane = lax.broadcasted_iota(jnp.int32, (rows, lanes), 1)
        mine = jnp.sum(jnp.where(lane == head, rate_ref[...], 0.0), axis=1, keepdims=True)
        key = k_ref[0].astype(F32)
        knorm = key * lax.rsqrt(jnp.mean(key * key, axis=-1, keepdims=True) + 1e-06)
        target = -mine * v_ref[0].astype(F32)
        knorm = knorm.astype(BF16)
        gate_pre = mm(knorm, gate_ref[0].astype(BF16))
        up_pre = mm(knorm, up_ref[0].astype(BF16))
        back = mm(target.astype(BF16), down_ref[0].astype(BF16), ((1,), (1,)))
        sigma = sigmoid(gate_pre)
        active = gate_pre * sigma
        first = (back * up_pre * (sigma + active * (1.0 - sigma))).astype(BF16)
        second = (back * active).astype(BF16)
        third = (active * up_pre).astype(BF16)
        terms = (
            mm(knorm, first, ((0,), (0,))),
            mm(knorm, second, ((0,), (0,))),
            mm(target.astype(BF16), third, ((0,), (0,))),
        )
        for index, term in enumerate(terms):
            if before is not None:
                term = term + rest[0][0, index]
            out_ref[0, index] = term

    def spec(shape):
        return pl.BlockSpec((1,) + shape, lambda h, b: (b[0] + h,) + (0,) * len(shape))

    args = [kv, kv, rate, fast_gate, fast_up, fast_down]
    specs = [
        pl.BlockSpec((1, rows, size), lambda h, b: (0, 0, b[0] + h)),
        pl.BlockSpec((1, rows, size), lambda h, b: (1, 0, b[0] + h)),
        fixed(rate.shape),
        spec((size, hidden_size)),
        spec((size, hidden_size)),
        spec((hidden_size, size)),
    ]
    if before is not None:
        args.append(before)
        specs.append(spec((3, size, hidden_size)))
    return call(
        body,
        (heads,),
        specs,
        pl.BlockSpec((1, 3, size, hidden_size), lambda h, b: (h, 0, 0, 0)),
        jax.ShapeDtypeStruct((heads, 3, size, hidden_size), F32),
    )(base, *args)


def renew(base, kept, received, step, fast_gate, fast_up, fast_down):
    heads, _, size, hidden_size = kept.shape

    def body(base_ref, step_ref, kept_ref, gate_ref, up_ref, down_ref, *rest):
        out_ref = rest[-1]
        pace = step_ref[base_ref[0] + pl.program_id(0)]
        for index in range(3):
            grad = kept_ref[0, index]
            for more in rest[:-1]:
                grad = grad + more[0, index].astype(F32)
            if index < 2:
                matrix = (gate_ref, up_ref)[index][0]
                fan = size
            else:
                matrix = down_ref[0].T
                fan = hidden_size
            mean_sq = jnp.sum(grad * grad, keepdims=True) / (size * hidden_size)
            scale = pace * fan ** (-0.5) * lax.rsqrt(mean_sq + 1e-06)
            out_ref[0, index] = (matrix - scale * grad).astype(BF16)

    def spec(shape):
        return pl.BlockSpec((1,) + shape, lambda h, b, s: (b[0] + h,) + (0,) * len(shape))

    own = pl.BlockSpec((1, 3, size, hidden_size), lambda h, b, s: (h, 0, 0, 0))
    return call(
        body,
        (heads,),
        [own, spec((size, hidden_size)), spec((size, hidden_size)), spec((hidden_size, size))]
        + [own] * len(received),
        own,
        jax.ShapeDtypeStruct(kept.shape, BF16),
        prefetch=2,
    )(base, step, kept, fast_gate, fast_up, fast_down, *received)


def attend(place, queries, kvs, halos, size):
    count = len(queries)
    rows = queries[0].shape[1]
    heads = queries[0].shape[2] // size
    factor = size ** (-0.5) * LOG2E

    def body(place_ref, *refs):
        q_refs = refs[:count]
        k_refs, v_refs = refs[count : 3 * count], refs[3 * count : 5 * count]
        out_ref = refs[-1]
        has_halo = place_ref[0] > 0
        row = lax.broadcasted_iota(jnp.int32, (rows, rows), 0)
        col = lax.broadcasted_iota(jnp.int32, (rows, rows), 1)
        for index in range(count):
            query = q_refs[index][0]
            scores = []
            for source in range(index, index + count + 1):
                part = mm(query, k_refs[source][0], ((1,), (1,))) * factor
                if source == index:
                    part = jnp.where((col > row) & has_halo, part, -1e30)
                elif source == index + count:
                    part = jnp.where(col <= row, part, -1e30)
                elif source < count:
                    part = jnp.where(has_halo, part, -1e30)
                scores.append(part)
            top = functools.reduce(
                jnp.maximum, [jnp.max(part, axis=-1, keepdims=True) for part in scores]
            )
            total, result = 0.0, 0.0
            for part, source in zip(scores, range(index, index + count + 1)):
                expo = jnp.exp2(part - top)
                total = total + jnp.sum(expo, axis=-1, keepdims=True)
                result = result + mm(expo.astype(BF16), v_refs[source][0])
            out_ref[index * rows : (index + 1) * rows] = result / total

    def spec(which):
        return pl.BlockSpec((1, rows, size), lambda h, p: (which, 0, h))

    sources = list(halos) + list(kvs)
    return call(
        body,
        (heads,),
        [spec(0)] * count + [spec(0)] * (2 * count) + [spec(1)] * (2 * count),
        pl.BlockSpec((count * rows, size), lambda h, p: (0, h)),
        jax.ShapeDtypeStruct((count * rows, heads * size), F32),
    )(place, *queries, *sources, *sources)


def apply_fast(side, queries, attended, mine, other):
    count = len(queries)
    rows = queries[0].shape[1]
    heads, _, size, hidden_size = mine.shape

    def body(side_ref, *refs):
        q_refs = refs[:count]
        attended_ref, mine_ref, other_ref, out_ref = refs[count:]
        held = side_ref[0] == pl.program_id(0) // heads
        gate, upper, down = (
            jnp.where(held, mine_ref[0, index], other_ref[0, index]) for index in range(3)
        )
        for index in range(count):
            where = slice(index * rows, (index + 1) * rows)
            query = q_refs[index][0].astype(F32)
            qnorm = query * lax.rsqrt(jnp.mean(query * query, axis=-1, keepdims=True) + 1e-06)
            qnorm = qnorm.astype(BF16)
            gate_pre = mm(qnorm, gate)
            hidden = gate_pre * sigmoid(gate_pre) * mm(qnorm, upper)
            out_ref[where] = (
                attended_ref[where] + mm(hidden.astype(BF16), down, ((1,), (1,)))
            ).astype(BF16)

    block = pl.BlockSpec((count * rows, size), lambda h, s: (0, h))
    matrices = pl.BlockSpec((1, 3, size, hidden_size), lambda h, s: (h % heads, 0, 0, 0))
    return call(
        body,
        (2 * heads,),
        [pl.BlockSpec((1, rows, size), lambda h, s: (0, 0, h))] * count
        + [block, matrices, matrices],
        block,
        jax.ShapeDtypeStruct((count * rows, 2 * heads * size), BF16),
    )(side, *queries, attended, mine, other)


def partial_out(ids, combined, w_out, columns):
    total_rows, depth = combined.shape
    rows = total_rows // lax.axis_size("head")
    count = ids.shape[0]
    width = w_out.shape[1]

    def body(ids_ref, combined_ref, w_ref, out_ref):
        left = jnp.concatenate(
            [
                combined_ref[pl.ds(pl.multiple_of(ids_ref[index] * rows, rows), rows)]
                for index in range(count)
            ],
            axis=0,
        )
        result = mm(left, w_ref[...]).astype(BF16)
        for index in range(count):
            out_ref[index] = result[index * rows : (index + 1) * rows]

    return call(
        body,
        (width // columns,),
        [fixed(combined.shape), pl.BlockSpec((depth, columns), lambda c, i: (0, c))],
        pl.BlockSpec((count, rows, columns), lambda c, i: (0, 0, c)),
        jax.ShapeDtypeStruct((count, rows, width), BF16),
    )(ids, combined, w_out)


def ring_reduce(combined, w_out):
    count = lax.axis_size("head")
    steps = count // 2
    half = w_out.shape[1] // 2
    farthest = partial_out(ring_ids([steps]), combined, w_out, half // 2)[0]
    offsets = [sign * step for step in range(steps - 1, 0, -1) for sign in (1, -1)] + [0]
    parts = partial_out(ring_ids(offsets), combined, w_out, half // 4)
    sides = (slice(0, half), slice(half, None))
    coming = {
        (1, 0): ring_send(farthest[:, sides[0]], 1),
        (-1, 1): ring_send(farthest[:, sides[1]], -1),
    }
    for index, offset in enumerate(offsets[:-1]):
        way = 1 if offset > 0 else -1
        for which in range(2):
            term = parts[index][:, sides[which]]
            if (way, which) in coming:
                term = (term.astype(F32) + coming[way, which].astype(F32)).astype(BF16)
            coming[way, which] = ring_send(term, way)
    own = parts[len(offsets) - 1]
    ends = []
    for which in range(2):
        total = own[:, sides[which]].astype(F32)
        for way in (1, -1):
            if (way, which) in coming:
                total = total + coming[way, which].astype(F32)
        ends.append(total.astype(BF16))
    return jnp.concatenate(ends, axis=1)


def swap(value, bit):
    count = lax.axis_size("tok")
    return lax.ppermute(value, "tok", [(index, index ^ bit) for index in range(count)])


def shards(
    tokens, w_query, w_key, w_value, w_out, fast_gate, fast_up, fast_down, token_rate, head_step
):
    row_count = tokens.shape[0]
    local_heads, head_size, _ = fast_gate.shape
    head_count = lax.axis_size("head")
    tok_count = lax.axis_size("tok")
    rows = row_count // CHUNKS
    steps = head_count // 2
    place = lax.axis_index("tok").astype(jnp.int32)
    side = place % 2
    pair = local_heads // 2
    offsets = [0] + [sign * step for step in range(1, steps) for sign in (-1, 1)] + [steps]
    ids = ring_ids(offsets)
    zero = jnp.zeros((1,), jnp.int32)
    far_base = ((1 - side) * pair).reshape(1)
    near_base = (side * pair).reshape(1)

    chunks = [gather_pieces(tokens[c * rows : (c + 1) * rows]) for c in range(CHUNKS)]
    rates = [token_rate[c * rows : (c + 1) * rows] for c in range(CHUNKS)]
    nets = (fast_gate, fast_up, fast_down)
    kvs, halos, queries = [], [], []
    grads = None
    for c in range(CHUNKS):
        kv = project(ids, chunks[c], (w_key, w_value))
        halos.append(
            lax.ppermute(kv, "tok", [(index, index + 1) for index in range(tok_count - 1)])
        )
        kvs.append(kv)
        if c < CHUNKS - 1:
            grads = head_grads(zero, local_heads, kv, rates[c], *nets, grads)
        else:
            far = head_grads(far_base, pair, kv, rates[c], *nets, grads)
            near = head_grads(near_base, pair, kv, rates[c], *nets, grads)
        queries.append(project(ids, chunks[c], (w_query,)))
    near = near + swap(far.astype(BF16), 1).astype(F32)
    received = []
    for bit in range(1, tok_count.bit_length() - 1):
        travel = near
        for more in received:
            travel = travel + more.astype(F32)
        received.append(swap(travel.astype(BF16), 1 << bit))
    attended = attend(place.reshape(1), queries, kvs, halos, head_size)
    mine = renew(near_base, near, received, head_step, *nets)
    other = swap(mine, 1)
    combined = apply_fast(side.reshape(1), queries, attended, mine, other)
    return ring_reduce(combined, w_out)


def solution(mesh):
    placed = (
        P("tok", "head"),
        P(None, "head"),
        P(None, "head"),
        P(None, "head"),
        P("head", None),
        P("head", None, None),
        P("head", None, None),
        P("head", None, None),
        P("tok", "head"),
        P("head"),
    )
    return jax.shard_map(
        shards, mesh=mesh, in_specs=placed, out_specs=P(("tok", "head"), None), check_vma=False
    )
```

```python
import functools

import jax
import jax.numpy as jnp
from jax import lax
from jax.experimental import pallas as pl
from jax.experimental.pallas import tpu as pltpu
from jax.sharding import PartitionSpec as P

WINDOW = 512
CHUNKS = 2
F32 = jnp.float32
BF16 = jnp.bfloat16
LOG2E = 1.4426950408889634


def call(body, grid, in_specs, out_specs, out_shape, scratch=(), prefetch=1, vmem=8, cost=None):
    return pl.pallas_call(
        body,
        grid_spec=pltpu.PrefetchScalarGridSpec(
            num_scalar_prefetch=prefetch,
            grid=grid,
            in_specs=in_specs,
            out_specs=out_specs,
            scratch_shapes=list(scratch),
        ),
        out_shape=out_shape,
        cost_estimate=cost,
        compiler_params=pltpu.CompilerParams(vmem_limit_bytes=vmem * 1024 * 1024),
    )


def cost(flops, moved, exps=0):
    return pl.CostEstimate(flops=int(flops), bytes_accessed=int(moved), transcendentals=int(exps))


WHOLE = pl.BlockSpec(memory_space=pltpu.VMEM)
AFTER = pl.BlockSpec(memory_space=pl.ANY)


def fixed(shape):
    return pl.BlockSpec(shape, lambda *_: (0,) * len(shape))


def mm(left, right, dims=((1,), (0,))):
    return lax.dot_general(left, right, (dims, ((), ())), preferred_element_type=F32)


def sigmoid(x):
    return 0.5 * jnp.tanh(0.5 * x) + 0.5


def ring_order(count):
    return list(range(0, count, 2)) + list(range(count - 1, 0, -2))


def ring_send(value, step):
    order = ring_order(lax.axis_size("head"))
    count = len(order)
    return lax.ppermute(
        value, "head", [(order[i], order[(i + step) % count]) for i in range(count)]
    )


def ring_ids(offsets):
    count = lax.axis_size("head")
    me = lax.axis_index("head")
    place = jnp.where(me % 2 == 0, me // 2, count - 1 - me // 2)
    ids = []
    for offset in offsets:
        at = (place + offset) % count
        ids.append(jnp.where(at < count // 2, 2 * at, 2 * (count - 1 - at) + 1))
    return jnp.stack(ids).astype(jnp.int32)


def load(arrays, after=(), start=0, stop=None, pieces=8):
    stop = arrays[0].shape[0] if stop is None else stop
    size = (stop - start) // pieces
    count = len(arrays)

    def body(*refs):
        out_refs, sems = refs[count + len(after) : -1], refs[-1]
        copies = [
            pltpu.make_async_copy(
                refs[index].at[pl.ds(start + piece * size, size)],
                out_refs[index].at[pl.ds(piece * size, size)],
                sems.at[index, piece],
            )
            for index in range(count)
            for piece in range(pieces)
        ]
        for copy in copies:
            copy.start()
        for copy in copies:
            copy.wait()

    return pl.pallas_call(
        body,
        in_specs=[pl.BlockSpec(memory_space=pltpu.HBM)] * count + [AFTER] * len(after),
        out_specs=[WHOLE] * count,
        out_shape=[
            jax.ShapeDtypeStruct((stop - start,) + array.shape[1:], array.dtype)
            for array in arrays
        ],
        scratch_shapes=[pltpu.SemaphoreType.DMA((count, pieces))],
        cost_estimate=cost(0, sum(2 * (stop - start) * array.shape[1] for array in arrays)),
        compiler_params=pltpu.CompilerParams(vmem_limit_bytes=1024 * 1024),
    )(*[pltpu.with_memory_space_constraint(array, pltpu.HBM) for array in arrays], *after)


def gather_pieces(own, longer):
    count = lax.axis_size("head")
    pieces, offsets = [own], [0]
    held = {1: own, -1: own}
    for step in range(1, count // 2 + 1):
        for way in (1, -1):
            if step < count // 2 or way == longer:
                held[way] = ring_send(held[way], way)
                pieces.append(held[way])
                offsets.append(-way * step)
    return pieces, offsets


def project(gathered, weights):
    pieces, offsets = gathered
    rows, depth = pieces[0].shape
    full, width = weights[0].shape
    count = len(pieces)
    parts = len(weights)

    def body(ids_ref, *refs):
        piece_refs, weight_refs = refs[:count], refs[count : count + parts]
        out_ref, left = refs[count + parts :]
        for index in range(count):
            column = pl.multiple_of(ids_ref[index] * depth, depth)
            left[:, pl.ds(column, depth)] = piece_refs[index][...]
        for part in range(parts):
            out_ref[part] = mm(left[...], weight_refs[part][...]).astype(BF16)

    return call(
        body,
        (),
        [WHOLE] * (count + parts),
        WHOLE,
        jax.ShapeDtypeStruct((parts, rows, width), BF16),
        [pltpu.VMEM((rows, full), BF16)],
        vmem=24,
        cost=cost(2 * rows * full * width * parts, 2 * full * (rows + width * parts)),
    )(ring_ids(offsets), *pieces, *weights)


def head_grads(base, heads, chunk, kv, rate, fast_gate, fast_up, fast_down, before, after=()):
    rows = kv.shape[1]
    size, hidden_size = fast_gate.shape[1:]
    lanes = rate.shape[0]

    def body(base_ref, k_ref, v_ref, rate_ref, gate_ref, up_ref, down_ref, *rest):
        out_ref = rest[-1]
        head = base_ref[0] + pl.program_id(0)
        lane = lax.broadcasted_iota(jnp.int32, (rows, lanes), 1)
        mine = jnp.sum(jnp.where(lane == head, rate_ref[...].T, 0.0), axis=1, keepdims=True)
        key = k_ref[0].astype(F32)
        knorm = key * lax.rsqrt(jnp.mean(key * key, axis=-1, keepdims=True) + 1e-06)
        target = -mine * v_ref[0].astype(F32)
        knorm = knorm.astype(BF16)
        gate_pre = mm(knorm, gate_ref[0].astype(BF16))
        up_pre = mm(knorm, up_ref[0].astype(BF16))
        back = mm(target.astype(BF16), down_ref[0].astype(BF16), ((1,), (1,)))
        sigma = sigmoid(gate_pre)
        active = gate_pre * sigma
        first = (back * up_pre * (sigma + active * (1.0 - sigma))).astype(BF16)
        second = (back * active).astype(BF16)
        third = (active * up_pre).astype(BF16)
        terms = (
            mm(knorm, first, ((0,), (0,))),
            mm(knorm, second, ((0,), (0,))),
            mm(target.astype(BF16), third, ((0,), (0,))),
        )
        for index, term in enumerate(terms):
            if before is not None:
                term = term + rest[0][0, index]
            out_ref[0, index] = term

    def spec(shape):
        return pl.BlockSpec((1,) + shape, lambda h, b: (b[0] + h,) + (0,) * len(shape))

    args = [kv, kv, rate, fast_gate, fast_up, fast_down]
    specs = [
        pl.BlockSpec((1, rows, size), lambda h, b: (0, 0, b[0] + h)),
        pl.BlockSpec((1, rows, size), lambda h, b: (1, 0, b[0] + h)),
        pl.BlockSpec((lanes, rows), lambda h, b: (0, chunk)),
        spec((size, hidden_size)),
        spec((size, hidden_size)),
        spec((hidden_size, size)),
    ]
    if before is not None:
        args.append(before)
        specs.append(spec((3, size, hidden_size)))
    args += after
    specs += [AFTER] * len(after)
    return call(
        body,
        (heads,),
        specs,
        pl.BlockSpec((1, 3, size, hidden_size), lambda h, b: (h, 0, 0, 0)),
        jax.ShapeDtypeStruct((heads, 3, size, hidden_size), F32),
        cost=cost(
            12 * heads * rows * size * hidden_size,
            8 * heads * 3 * size * hidden_size,
            heads * rows * hidden_size,
        ),
    )(base, *args)


def renew(base, kept, received, step, fast_gate, fast_up, fast_down, after):
    heads, _, size, hidden_size = kept.shape

    def body(base_ref, step_ref, kept_ref, gate_ref, up_ref, down_ref, *rest):
        out_ref = rest[-1]
        pace = step_ref[base_ref[0] + pl.program_id(0)]
        for index in range(3):
            grad = kept_ref[0, index]
            for more in rest[: len(received)]:
                grad = grad + more[0, index].astype(F32)
            if index < 2:
                matrix = (gate_ref, up_ref)[index][0]
                fan = size
            else:
                matrix = down_ref[0].T
                fan = hidden_size
            mean_sq = jnp.sum(grad * grad, keepdims=True) / (size * hidden_size)
            scale = pace * fan ** (-0.5) * lax.rsqrt(mean_sq + 1e-06)
            out_ref[0, index] = (matrix - scale * grad).astype(BF16)

    def spec(shape):
        return pl.BlockSpec((1,) + shape, lambda h, b, s: (b[0] + h,) + (0,) * len(shape))

    own = pl.BlockSpec((1, 3, size, hidden_size), lambda h, b, s: (h, 0, 0, 0))
    return call(
        body,
        (heads,),
        [own, spec((size, hidden_size)), spec((size, hidden_size)), spec((hidden_size, size))]
        + [own] * len(received)
        + [AFTER] * len(after),
        own,
        jax.ShapeDtypeStruct(kept.shape, BF16),
        prefetch=2,
        cost=cost(10 * kept.size, 12 * kept.size),
    )(base, step, kept, fast_gate, fast_up, fast_down, *received, *after)


def attend(place, queries, kvs, halos, size):
    count = len(queries)
    rows = queries[0].shape[1]
    heads = queries[0].shape[2] // size
    factor = size ** (-0.5) * LOG2E

    def body(place_ref, *refs):
        q_refs = refs[:count]
        k_refs, v_refs = refs[count : 3 * count], refs[3 * count : 5 * count]
        out_ref = refs[-1]
        has_halo = place_ref[0] > 0
        row = lax.broadcasted_iota(jnp.int32, (rows, rows), 0)
        col = lax.broadcasted_iota(jnp.int32, (rows, rows), 1)
        for index in range(count):
            query = q_refs[index][0]
            scores = []
            for source in range(index, index + count + 1):
                part = mm(query, k_refs[source][0], ((1,), (1,))) * factor
                if source == index:
                    part = jnp.where((col > row) & has_halo, part, -1e30)
                elif source == index + count:
                    part = jnp.where(col <= row, part, -1e30)
                elif source < count:
                    part = jnp.where(has_halo, part, -1e30)
                scores.append(part)
            top = functools.reduce(
                jnp.maximum, [jnp.max(part, axis=-1, keepdims=True) for part in scores]
            )
            total, result = 0.0, 0.0
            for part, source in zip(scores, range(index, index + count + 1)):
                expo = jnp.exp2(part - top)
                total = total + jnp.sum(expo, axis=-1, keepdims=True)
                result = result + mm(expo.astype(BF16), v_refs[source][0])
            out_ref[index * rows : (index + 1) * rows] = result / total

    def spec(which):
        return pl.BlockSpec((1, rows, size), lambda h, p: (which, 0, h))

    sources = list(halos) + list(kvs)
    return call(
        body,
        (heads,),
        [spec(0)] * count + [spec(0)] * (2 * count) + [spec(1)] * (2 * count),
        pl.BlockSpec((count * rows, size), lambda h, p: (0, h)),
        jax.ShapeDtypeStruct((count * rows, heads * size), F32),
        cost=cost(
            4 * heads * size * count * (count + 1) * rows * rows,
            8 * count * rows * heads * size,
            heads * count * (count + 1) * rows * rows,
        ),
    )(place, *queries, *sources, *sources)


def apply_fast(base, queries, attended, nets):
    count = len(queries)
    rows = queries[0].shape[1]
    heads, _, size, hidden_size = nets.shape

    def body(base_ref, *refs):
        q_refs = refs[:count]
        attended_ref, net_ref, out_ref = refs[count:]
        for index in range(count):
            where = slice(index * rows, (index + 1) * rows)
            query = q_refs[index][0].astype(F32)
            qnorm = query * lax.rsqrt(jnp.mean(query * query, axis=-1, keepdims=True) + 1e-06)
            qnorm = qnorm.astype(BF16)
            gate_pre = mm(qnorm, net_ref[0, 0])
            hidden = gate_pre * sigmoid(gate_pre) * mm(qnorm, net_ref[0, 1])
            out_ref[where] = (
                attended_ref[where] + mm(hidden.astype(BF16), net_ref[0, 2], ((1,), (1,)))
            ).astype(BF16)

    return call(
        body,
        (heads,),
        [pl.BlockSpec((1, rows, size), lambda h, b: (0, 0, b[0] + h))] * count
        + [
            pl.BlockSpec((count * rows, size), lambda h, b: (0, b[0] + h)),
            pl.BlockSpec((1, 3, size, hidden_size), lambda h, b: (h, 0, 0, 0)),
        ],
        pl.BlockSpec((count * rows, size), lambda h, b: (0, h)),
        jax.ShapeDtypeStruct((count * rows, heads * size), BF16),
        cost=cost(
            6 * heads * count * rows * size * hidden_size,
            8 * heads * count * rows * size,
            heads * count * rows * hidden_size,
        ),
    )(base, *queries, attended, nets)


def partial_out(ids, side, near, far, w_out, after=()):
    rows = near.shape[0] // lax.axis_size("head")
    depth = near.shape[1]
    count = ids.shape[0]
    width = w_out.shape[1]
    block = width // 8

    def body(ids_ref, side_ref, near_ref, far_ref, w_ref, *refs):
        out_refs = refs[len(after) :]
        lefts = [
            jnp.concatenate(
                [
                    ref[pl.ds(pl.multiple_of(ids_ref[index] * rows, rows), rows)]
                    for index in range(count)
                ],
                axis=0,
            )
            for ref in (near_ref, far_ref)
        ]
        near_row = pl.multiple_of(side_ref[0] * depth, depth)
        far_row = pl.multiple_of((1 - side_ref[0]) * depth, depth)
        for column in range(0, width, block):
            result = mm(lefts[0], w_ref[pl.ds(near_row, depth), column : column + block])
            result += mm(lefts[1], w_ref[pl.ds(far_row, depth), column : column + block])
            result = result.astype(BF16)
            half, at = divmod(column, width // 2)
            for index in range(count):
                out_refs[2 * index + half][:, at : at + block] = result[
                    index * rows : (index + 1) * rows
                ]

    outs = call(
        body,
        (),
        [WHOLE] * 3 + [AFTER] * len(after),
        [WHOLE] * (2 * count),
        [jax.ShapeDtypeStruct((rows, width // 2), BF16)] * (2 * count),
        prefetch=2,
        vmem=16,
        cost=cost(4 * count * rows * depth * width, 2 * width * (2 * depth + count * rows)),
    )(ids, side, near, far, w_out, *after)
    return [tuple(outs[2 * index : 2 * index + 2]) for index in range(count)]


def ring_reduce(side, near, far, w_out):
    count = lax.axis_size("head")
    steps = count // 2
    signed = [sign * step for step in range(steps - 1, 0, -1) for sign in (1, -1)]
    first, second = [steps] + signed[:2], signed[2:] + [0]
    parts = dict(zip(first, partial_out(ring_ids(first), side, near, far, w_out)))
    coming = {
        (1, 0): ring_send(parts[steps][0], 1),
        (-1, 1): ring_send(parts[steps][1], -1),
    }
    after = tuple(coming.values())
    parts |= dict(zip(second, partial_out(ring_ids(second), side, near, far, w_out, after)))
    for offset in signed:
        way = 1 if offset > 0 else -1
        for which in range(2):
            term = parts[offset][which]
            if (way, which) in coming:
                term = (term.astype(F32) + coming[way, which].astype(F32)).astype(BF16)
            coming[way, which] = ring_send(term, way)
    ends = []
    for which in range(2):
        total = parts[0][which].astype(F32)
        for way in (1, -1):
            if (way, which) in coming:
                total = total + coming[way, which].astype(F32)
        ends.append(total.astype(BF16))
    return jnp.concatenate(ends, axis=1)


def swap(value, bit):
    count = lax.axis_size("tok")
    return lax.ppermute(value, "tok", [(index, index ^ bit) for index in range(count)])


def shards(
    tokens, w_query, w_key, w_value, w_out, fast_gate, fast_up, fast_down, token_rate, head_step
):
    row_count = tokens.shape[0]
    local_heads, head_size, _ = fast_gate.shape
    tok_count = lax.axis_size("tok")
    rows = row_count // CHUNKS
    place = lax.axis_index("tok").astype(jnp.int32)
    pair = local_heads // 2
    side = (place % 2).reshape(1)
    near_base, far_base = side * pair, (1 - side) * pair
    zero = jnp.zeros((1,), jnp.int32)

    chunks, after = [], ()
    for c in range(CHUNKS):
        (own,) = load([tokens], after, c * rows, (c + 1) * rows, 1)
        chunks.append(gather_pieces(own, 1 if c % 2 == 0 else -1))
        if c == 0:
            w_key, w_value = load([w_key, w_value])
            after = (*chunks[0][0][1:3], w_key, w_value)
    rate = token_rate.T
    nets = (fast_gate, fast_up, fast_down)
    kvs, halos, queries = [], [], []
    grads = None
    for c in range(CHUNKS):
        kv = project(chunks[c], (w_key, w_value))
        halos.append(
            lax.ppermute(kv, "tok", [(index, index + 1) for index in range(tok_count - 1)])
        )
        kvs.append(kv)
        if c < CHUNKS - 1:
            grads = head_grads(zero, local_heads, c, kv, rate, *nets, grads)
        else:
            far = head_grads(far_base, pair, c, kv, rate, *nets, grads)
            near = head_grads(near_base, pair, c, kv, rate, *nets, grads, halos[:-1])
        queries.append(project(chunks[c], (w_query,)))
    near = near + swap(far.astype(BF16), 1).astype(F32)
    received = []
    for bit in range(1, tok_count.bit_length() - 1):
        travel = near
        for more in received:
            travel = travel + more.astype(F32)
        received.append(swap(travel.astype(BF16), 1 << bit))
    attended = attend(place.reshape(1), queries, kvs, halos, head_size)
    mine = renew(near_base, near, received, head_step, *nets, (attended,))
    other = swap(mine, 1)
    near = apply_fast(near_base, queries, attended, mine)
    far = apply_fast(far_base, queries, attended, other)
    return ring_reduce(side, near, far, w_out)


def solution(mesh):
    placed = (
        P("tok", "head"),
        P(None, "head"),
        P(None, "head"),
        P(None, "head"),
        P("head", None),
        P("head", None, None),
        P("head", None, None),
        P("head", None, None),
        P("tok", "head"),
        P("head"),
    )
    return jax.shard_map(
        shards, mesh=mesh, in_specs=placed, out_specs=P(("tok", "head"), None), check_vma=False
    )
```

```python
import functools

import jax
import jax.numpy as jnp
from jax import lax
from jax.experimental import pallas as pl
from jax.experimental.pallas import tpu as pltpu
from jax.sharding import PartitionSpec as P

WINDOW = 512
CHUNKS = 2
F32 = jnp.float32
BF16 = jnp.bfloat16
LOG2E = 1.4426950408889634


def call(body, grid, in_specs, out_specs, out_shape, scratch=(), prefetch=1, vmem=8, cost=None):
    return pl.pallas_call(
        body,
        grid_spec=pltpu.PrefetchScalarGridSpec(
            num_scalar_prefetch=prefetch,
            grid=grid,
            in_specs=in_specs,
            out_specs=out_specs,
            scratch_shapes=list(scratch),
        ),
        out_shape=out_shape,
        cost_estimate=cost,
        compiler_params=pltpu.CompilerParams(vmem_limit_bytes=vmem * 1024 * 1024),
    )


def cost(flops, moved, exps=0):
    return pl.CostEstimate(flops=int(flops), bytes_accessed=int(moved), transcendentals=int(exps))


WHOLE = pl.BlockSpec(memory_space=pltpu.VMEM)
AFTER = pl.BlockSpec(memory_space=pl.ANY)


def fixed(shape):
    return pl.BlockSpec(shape, lambda *_: (0,) * len(shape))


def mm(left, right, dims=((1,), (0,))):
    return lax.dot_general(left, right, (dims, ((), ())), preferred_element_type=F32)


def sigmoid(x):
    return 0.5 * jnp.tanh(0.5 * x) + 0.5


def ring_order(count):
    return list(range(0, count, 2)) + list(range(count - 1, 0, -2))


def ring_send(value, step):
    order = ring_order(lax.axis_size("head"))
    count = len(order)
    return lax.ppermute(
        value, "head", [(order[i], order[(i + step) % count]) for i in range(count)]
    )


def ring_ids(offsets):
    count = lax.axis_size("head")
    me = lax.axis_index("head")
    place = jnp.where(me % 2 == 0, me // 2, count - 1 - me // 2)
    ids = []
    for offset in offsets:
        at = (place + offset) % count
        ids.append(jnp.where(at < count // 2, 2 * at, 2 * (count - 1 - at) + 1))
    return jnp.stack(ids).astype(jnp.int32)


def load(arrays, blocks, order):
    count = len(arrays)
    sizes = [array.shape[0] // blocks for array in arrays]

    def body(order_ref, *refs):
        out_refs, sems = refs[count:-1], refs[-1]
        copies = [
            pltpu.make_async_copy(
                refs[index].at[pl.ds(pl.multiple_of(order_ref[block] * size, size), size)],
                out_refs[index].at[pl.ds(block * size, size)],
                sems.at[index, block],
            )
            for index, size in enumerate(sizes)
            for block in range(blocks)
        ]
        for copy in copies:
            copy.start()
        for copy in copies:
            copy.wait()

    return call(
        body,
        (),
        [pl.BlockSpec(memory_space=pltpu.HBM)] * count,
        [WHOLE] * count,
        [jax.ShapeDtypeStruct(array.shape, array.dtype) for array in arrays],
        [pltpu.SemaphoreType.DMA((count, blocks))],
        vmem=1,
        cost=cost(0, sum(4 * array.size for array in arrays)),
    )(order, *[pltpu.with_memory_space_constraint(array, pltpu.HBM) for array in arrays])


def split_rows(tokens):
    rows, width = tokens.shape[0] // CHUNKS, tokens.shape[1]

    def body(in_ref, *refs):
        out_refs, sems = refs[:-1], refs[-1]
        copies = [
            pltpu.make_async_copy(in_ref.at[pl.ds(c * rows, rows)], out_refs[c], sems.at[c])
            for c in range(CHUNKS)
        ]
        for copy in copies:
            copy.start()
        for copy in copies:
            copy.wait()

    return pl.pallas_call(
        body,
        in_specs=[pl.BlockSpec(memory_space=pltpu.HBM)],
        out_specs=[WHOLE] * CHUNKS,
        out_shape=[jax.ShapeDtypeStruct((rows, width), tokens.dtype)] * CHUNKS,
        scratch_shapes=[pltpu.SemaphoreType.DMA((CHUNKS,))],
        cost_estimate=cost(0, 4 * rows * width),
        compiler_params=pltpu.CompilerParams(vmem_limit_bytes=1024 * 1024),
    )(pltpu.with_memory_space_constraint(tokens, pltpu.HBM))


def ring_offsets():
    steps = lax.axis_size("head") // 2
    return [0] + [way * step for step in range(1, steps) for way in (-1, 1)] + [steps]


def gather_pieces(own, longer):
    steps = lax.axis_size("head") // 2
    pieces = [own]
    held = {1: own, -1: own}
    for step in range(1, steps + 1):
        for way in (1, -1):
            if step < steps or way == longer:
                held[way] = ring_send(held[way], way)
                pieces.append(held[way])
    return pieces


def accumulate(chunks, first, last, weights, before=None, lead=0):
    rows, depth = chunks[0][0].shape
    width = weights[0].shape[1]
    parts, span = len(weights), last - first
    total = rows * len(chunks)
    final = last == len(chunks[0])
    dtype = BF16 if final else F32
    pieces = [chunk[index] for chunk in chunks for index in range(first, last)]

    def body(*refs):
        piece_refs = refs[: len(pieces)]
        weight_refs = refs[len(pieces) : len(pieces) + parts]
        out_ref, left = refs[-2:]
        for index, ref in enumerate(piece_refs):
            chunk, piece = divmod(index, span)
            left[chunk * rows : (chunk + 1) * rows, piece * depth : (piece + 1) * depth] = ref[...]
        for part in range(parts):
            term = mm(left[...], weight_refs[part][first * depth : last * depth])
            if before is not None:
                term = term + refs[-3][lead + part]
            out_ref[part] = term.astype(dtype)

    aliased = before is not None and not final
    args = [*pieces, *weights] + ([] if before is None else [before])
    return pl.pallas_call(
        body,
        in_specs=[WHOLE] * len(args),
        out_specs=WHOLE,
        out_shape=jax.ShapeDtypeStruct((parts, total, width), dtype),
        scratch_shapes=[pltpu.VMEM((total, span * depth), BF16)],
        input_output_aliases={len(args) - 1: 0} if aliased else {},
        cost_estimate=cost(
            2 * total * span * depth * width * parts,
            2 * span * depth * (total + width * parts) + 8 * total * width * parts,
        ),
        compiler_params=pltpu.CompilerParams(vmem_limit_bytes=12 * 1024 * 1024),
    )(*args)


def head_grads(base, heads, kv, rate, fast_gate, fast_up, fast_down, before=None):
    rows = kv.shape[1]
    size, hidden_size = fast_gate.shape[1:]
    lanes = rate.shape[0]

    def body(base_ref, k_ref, v_ref, rate_ref, gate_ref, up_ref, down_ref, *rest):
        head = base_ref[0] + pl.program_id(0)
        lane = lax.broadcasted_iota(jnp.int32, (rows, lanes), 1)
        mine = jnp.sum(jnp.where(lane == head, rate_ref[...].T, 0.0), axis=1, keepdims=True)
        key = k_ref[0].astype(F32)
        knorm = key * lax.rsqrt(jnp.mean(key * key, axis=-1, keepdims=True) + 1e-06)
        target = (-mine * v_ref[0].astype(F32)).astype(BF16)
        knorm = knorm.astype(BF16)
        gate_pre = mm(knorm, gate_ref[0].astype(BF16))
        up_pre = mm(knorm, up_ref[0].astype(BF16))
        back = mm(target, down_ref[0].astype(BF16), ((1,), (1,)))
        sigma = sigmoid(gate_pre)
        active = gate_pre * sigma
        first = (back * up_pre * (sigma + active * (1.0 - sigma))).astype(BF16)
        second = (back * active).astype(BF16)
        third = (active * up_pre).astype(BF16)
        terms = (
            mm(knorm, first, ((0,), (0,))),
            mm(knorm, second, ((0,), (0,))),
            mm(target, third, ((0,), (0,))),
        )
        for index, term in enumerate(terms):
            if before is not None:
                term = term + rest[0][0, index]
                rest[-1][0, index] = term.astype(BF16)
                rest[-2][0, index] = term
            else:
                rest[-1][0, index] = term

    def spec(shape):
        return pl.BlockSpec((1,) + shape, lambda h, b: (b[0] + h,) + (0,) * len(shape))

    own = pl.BlockSpec((1, 3, size, hidden_size), lambda h, b: (h, 0, 0, 0))
    args = [kv, kv, rate, fast_gate, fast_up, fast_down]
    specs = [
        pl.BlockSpec((1, rows, size), lambda h, b: (0, 0, b[0] + h)),
        pl.BlockSpec((1, rows, size), lambda h, b: (1, 0, b[0] + h)),
        fixed(rate.shape),
        spec((size, hidden_size)),
        spec((size, hidden_size)),
        spec((hidden_size, size)),
    ]
    kinds = [F32]
    if before is not None:
        args.append(before)
        specs.append(own)
        kinds.append(BF16)
    return call(
        body,
        (heads,),
        specs,
        [own] * len(kinds),
        [jax.ShapeDtypeStruct((heads, 3, size, hidden_size), kind) for kind in kinds],
        cost=cost(
            12 * heads * rows * size * hidden_size,
            8 * heads * 3 * size * hidden_size,
            heads * rows * hidden_size,
        ),
    )(base, *args)


def renew(base, kept, received, step, fast_gate, fast_up, fast_down, after):
    heads, _, size, hidden_size = kept.shape

    def body(base_ref, step_ref, kept_ref, gate_ref, up_ref, down_ref, *rest):
        out_ref = rest[-1]
        pace = step_ref[base_ref[0] + pl.program_id(0)]
        for index in range(3):
            grad = kept_ref[0, index]
            for more in rest[: len(received)]:
                grad = grad + more[0, index].astype(F32)
            if index < 2:
                matrix = (gate_ref, up_ref)[index][0]
                fan = size
            else:
                matrix = down_ref[0].T
                fan = hidden_size
            mean_sq = jnp.sum(grad * grad, keepdims=True) / (size * hidden_size)
            scale = pace * fan ** (-0.5) * lax.rsqrt(mean_sq + 1e-06)
            out_ref[0, index] = (matrix - scale * grad).astype(BF16)

    def spec(shape):
        return pl.BlockSpec((1,) + shape, lambda h, b, s: (b[0] + h,) + (0,) * len(shape))

    own = pl.BlockSpec((1, 3, size, hidden_size), lambda h, b, s: (h, 0, 0, 0))
    return call(
        body,
        (heads,),
        [own, spec((size, hidden_size)), spec((size, hidden_size)), spec((hidden_size, size))]
        + [own] * len(received)
        + [AFTER] * len(after),
        own,
        jax.ShapeDtypeStruct(kept.shape, BF16),
        prefetch=2,
        cost=cost(10 * kept.size, 12 * kept.size),
    )(base, step, kept, fast_gate, fast_up, fast_down, *received, *after)


def attend(place, query, kv, beside, behind, size):
    total = query.shape[1]
    heads = query.shape[2] // size
    rows = total // 2
    factor = size ** (-0.5) * LOG2E

    def body(place_ref, q_ref, k_ref, v_ref, k_beside, v_beside, k_behind, v_behind, out_ref):
        has_halo = place_ref[0] > 0
        odd = place_ref[0] % 2 == 1
        keys = (jnp.where(odd, k_beside[0], k_behind[0]), k_ref[0])
        values = (jnp.where(odd, v_beside[0], v_behind[0]), v_ref[0])
        row = lax.broadcasted_iota(jnp.int32, (rows, rows), 0)
        col = lax.broadcasted_iota(jnp.int32, (rows, rows), 1)

        def block(pair, index):
            side, at = divmod(index, 2)
            return pair[side][at * rows : (at + 1) * rows]

        for index in range(2):
            query_block = q_ref[0, index * rows : (index + 1) * rows]
            scores = []
            for source in range(index, index + 3):
                part = mm(query_block, block(keys, source), ((1,), (1,))) * factor
                if source == index:
                    part = jnp.where((col > row) & has_halo, part, -1e30)
                elif source == index + 2:
                    part = jnp.where(col <= row, part, -1e30)
                elif source < 2:
                    part = jnp.where(has_halo, part, -1e30)
                scores.append(part)
            top = functools.reduce(
                jnp.maximum, [jnp.max(part, axis=-1, keepdims=True) for part in scores]
            )
            sums, result = 0.0, 0.0
            for part, source in zip(scores, range(index, index + 3)):
                expo = jnp.exp2(part - top)
                sums = sums + jnp.sum(expo, axis=-1, keepdims=True)
                result = result + mm(expo.astype(BF16), block(values, source))
            out_ref[index * rows : (index + 1) * rows] = result / sums

    def spec(which):
        return pl.BlockSpec((1, total, size), lambda h, p: (which, 0, h))

    return call(
        body,
        (heads,),
        [spec(0)] + [spec(0), spec(1)] * 3,
        pl.BlockSpec((total, size), lambda h, p: (0, h)),
        jax.ShapeDtypeStruct((total, heads * size), F32),
        cost=cost(
            24 * heads * size * rows * rows,
            8 * total * heads * size,
            6 * heads * rows * rows,
        ),
    )(place, query, kv, kv, beside, beside, behind, behind)


def apply_fast(base, query, attended, nets):
    rows = query.shape[1]
    heads, _, size, hidden_size = nets.shape

    def body(base_ref, q_ref, attended_ref, net_ref, out_ref):
        query = q_ref[0].astype(F32)
        qnorm = query * lax.rsqrt(jnp.mean(query * query, axis=-1, keepdims=True) + 1e-06)
        qnorm = qnorm.astype(BF16)
        gate_pre = mm(qnorm, net_ref[0, 0])
        hidden = gate_pre * sigmoid(gate_pre) * mm(qnorm, net_ref[0, 1])
        fast = mm(hidden.astype(BF16), net_ref[0, 2], ((1,), (1,)))
        out_ref[...] = (attended_ref[...] + fast).astype(BF16)

    return call(
        body,
        (heads,),
        [
            pl.BlockSpec((1, rows, size), lambda h, b: (0, 0, b[0] + h)),
            pl.BlockSpec((rows, size), lambda h, b: (0, b[0] + h)),
            pl.BlockSpec((1, 3, size, hidden_size), lambda h, b: (h, 0, 0, 0)),
        ],
        pl.BlockSpec((rows, size), lambda h, b: (0, h)),
        jax.ShapeDtypeStruct((rows, heads * size), BF16),
        cost=cost(
            6 * heads * rows * size * hidden_size,
            8 * heads * rows * size,
            heads * rows * hidden_size,
        ),
    )(base, query, attended, nets)


def partial_out(ids, side, near, far, w_out, after=()):
    rows = near.shape[0] // lax.axis_size("head")
    depth = near.shape[1]
    count = ids.shape[0]
    width = w_out.shape[1]
    block = width // 8

    def body(ids_ref, side_ref, near_ref, far_ref, w_ref, *refs):
        out_refs = refs[len(after) :]
        lefts = [
            jnp.concatenate(
                [
                    ref[pl.ds(pl.multiple_of(ids_ref[index] * rows, rows), rows)]
                    for index in range(count)
                ],
                axis=0,
            )
            for ref in (near_ref, far_ref)
        ]
        near_row = pl.multiple_of(side_ref[0] * depth, depth)
        far_row = pl.multiple_of((1 - side_ref[0]) * depth, depth)
        for column in range(0, width, block):
            result = mm(lefts[0], w_ref[pl.ds(near_row, depth), column : column + block])
            result += mm(lefts[1], w_ref[pl.ds(far_row, depth), column : column + block])
            result = result.astype(BF16)
            half, at = divmod(column, width // 2)
            for index in range(count):
                out_refs[2 * index + half][:, at : at + block] = result[
                    index * rows : (index + 1) * rows
                ]

    outs = call(
        body,
        (),
        [WHOLE] * 3 + [AFTER] * len(after),
        [WHOLE] * (2 * count),
        [jax.ShapeDtypeStruct((rows, width // 2), BF16)] * (2 * count),
        prefetch=2,
        vmem=16,
        cost=cost(4 * count * rows * depth * width, 2 * width * (2 * depth + count * rows)),
    )(ids, side, near, far, w_out, *after)
    return [tuple(outs[2 * index : 2 * index + 2]) for index in range(count)]


def ring_reduce(side, near, far, w_out):
    count = lax.axis_size("head")
    steps = count // 2
    signed = [sign * step for step in range(steps - 1, 0, -1) for sign in (1, -1)]
    first, second = [steps] + signed[:2], signed[2:] + [0]
    parts = dict(zip(first, partial_out(ring_ids(first), side, near, far, w_out)))
    coming = {}
    ordered = ()
    for which in range(2 * steps - 1):
        step, lane = steps - (which + 1) // 2, which % 2
        if which == 2:
            after = tuple(coming.values())
            later = partial_out(ring_ids(second), side, near, far, w_out, after[:2])
            parts |= dict(zip(second, later))
        terms = []
        for way in (1, -1):
            half = lane if way == 1 else 1 - lane
            term = parts[steps if step == steps else way * step][half]
            if (way, half) in coming:
                term = (term.astype(F32) + coming[way, half].astype(F32)).astype(BF16)
            terms.append(term)
        ordered = lax.optimization_barrier((*terms, *ordered))[:2]
        for way, term in zip((1, -1), ordered):
            coming[way, lane if way == 1 else 1 - lane] = ring_send(term, way)
    ends = []
    for which in range(2):
        total = parts[0][which].astype(F32)
        for way in (1, -1):
            if (way, which) in coming:
                total = total + coming[way, which].astype(F32)
        ends.append(total.astype(BF16))
    return jnp.concatenate(ends, axis=1)


def swap(value, bit):
    count = lax.axis_size("tok")
    return lax.ppermute(value, "tok", [(index, index ^ bit) for index in range(count)])


def shards(
    tokens, w_query, w_key, w_value, w_out, fast_gate, fast_up, fast_down, token_rate, head_step
):
    local_heads, head_size, _ = fast_gate.shape
    tok_count = lax.axis_size("tok")
    place = lax.axis_index("tok").astype(jnp.int32)
    pair = local_heads // 2
    side = (place % 2).reshape(1)
    near_base, far_base = side * pair, (1 - side) * pair
    nets = (fast_gate, fast_up, fast_down)

    own = split_rows(tokens)
    chunks = [gather_pieces(own[c], 1 if c % 2 == 0 else -1) for c in range(CHUNKS)]
    offsets = ring_offsets()
    rate = token_rate.T
    order, rate_beside = lax.optimization_barrier((ring_ids(offsets), swap(rate, 1)))
    weights = load([w_key, w_value, w_query], len(offsets), order)
    sums, done = None, 0
    for step in range(1, len(offsets) // 2):
        sums = accumulate(chunks, done, 2 * step + 1, weights, sums)
        done = 2 * step + 1
    kv = accumulate(chunks, done, len(offsets), weights[:2], sums)
    query = accumulate(chunks, done, len(offsets), weights[2:], sums, 2)

    beside = swap(kv, 1)
    behind = lax.ppermute(kv, "tok", [(index, index + 1) for index in range(1, tok_count - 1, 2)])
    (grads,) = head_grads(near_base, pair, kv, rate, *nets)
    grads, travel = head_grads(near_base, pair, beside, rate_beside, *nets, grads)
    received = []
    for bit in range(1, tok_count.bit_length() - 1):
        if received:
            travel = grads
            for more in received:
                travel = travel + more.astype(F32)
            travel = travel.astype(BF16)
        received.append(swap(travel, 1 << bit))
    attended = attend(place.reshape(1), query, kv, beside, behind, head_size)
    mine = renew(near_base, grads, received, head_step, *nets, (attended,))
    other = swap(mine, 1)
    near = apply_fast(near_base, query, attended, mine)
    far = apply_fast(far_base, query, attended, other)
    return ring_reduce(side, near, far, w_out)


def solution(mesh):
    placed = (
        P("tok", "head"),
        P(None, "head"),
        P(None, "head"),
        P(None, "head"),
        P("head", None),
        P("head", None, None),
        P("head", None, None),
        P("head", None, None),
        P("tok", "head"),
        P("head"),
    )
    return jax.shard_map(
        shards, mesh=mesh, in_specs=placed, out_specs=P(("tok", "head"), None), check_vma=False
    )
```

```python
import functools

import jax
import jax.numpy as jnp
import numpy as np
from jax import lax
from jax.experimental import pallas as pl
from jax.experimental.pallas import tpu as pltpu
from jax.sharding import PartitionSpec as P

WINDOW = 512
CHUNKS = 2
F32 = jnp.float32
BF16 = jnp.bfloat16
LOG2E = 1.4426950408889634


def call(body, in_specs, out_specs, out_shape, scratch=(), vmem=8, cost=None, aliases=None):
    return pl.pallas_call(
        body,
        in_specs=in_specs,
        out_specs=out_specs,
        out_shape=out_shape,
        scratch_shapes=list(scratch),
        input_output_aliases=aliases or {},
        cost_estimate=cost,
        compiler_params=pltpu.CompilerParams(vmem_limit_bytes=vmem * 1024 * 1024),
    )


def cost(flops, moved, exps=0):
    return pl.CostEstimate(flops=int(flops), bytes_accessed=int(moved), transcendentals=int(exps))


WHOLE = pl.BlockSpec(memory_space=pltpu.VMEM)
AFTER = pl.BlockSpec(memory_space=pl.ANY)
NUMBERS = pl.BlockSpec(memory_space=pltpu.SMEM)
IN_HBM = pl.BlockSpec(memory_space=pltpu.HBM)
PLACE, NEAR, FAR, RING = range(4)


def mm(left, right, dims=((1,), (0,))):
    return lax.dot_general(left, right, (dims, ((), ())), preferred_element_type=F32)


def sigmoid(x):
    return 0.5 * jnp.tanh(0.5 * x) + 0.5


def ring_order(count):
    return list(range(0, count, 2)) + list(range(count - 1, 0, -2))


def ring_send(value, step):
    order = ring_order(lax.axis_size("head"))
    count = len(order)
    return lax.ppermute(
        value, "head", [(order[i], order[(i + step) % count]) for i in range(count)]
    )


def ring_offsets():
    steps = lax.axis_size("head") // 2
    return [0] + [way * step for step in range(1, steps) for way in (-1, 1)] + [steps]


def own_numbers(pair):
    order = ring_order(lax.axis_size("head"))
    count = len(order)
    rows = []
    for place in range(lax.axis_size("tok")):
        for head in range(count):
            ring = [order[(order.index(head) + offset) % count] for offset in ring_offsets()]
            rows.append([place, place % 2 * pair, (1 - place % 2) * pair] + ring)
    table = jnp.array(np.array(rows, np.int32))
    return lax.dynamic_index_in_dim(table, lax.axis_index(("tok", "head")), 0, keepdims=False)


def hbm(array):
    return pltpu.with_memory_space_constraint(array, pltpu.HBM)


def run_copies(copies):
    for copy in copies:
        copy.start()
    for copy in copies:
        copy.wait()


def load(numbers, arrays):
    count = len(arrays)
    blocks = len(ring_offsets())
    size = arrays[0].shape[0] // blocks

    def body(numbers_ref, *refs):
        out_refs, sems = refs[count:-1], refs[-1]
        run_copies(
            [
                pltpu.make_async_copy(
                    refs[index].at[
                        pl.ds(pl.multiple_of(numbers_ref[RING + block] * size, size), size)
                    ],
                    out_refs[index].at[pl.ds(block * size, size)],
                    sems.at[index, block],
                )
                for block in range(blocks)
                for index in range(count)
            ]
        )

    return call(
        body,
        [NUMBERS] + [IN_HBM] * count,
        [WHOLE] * count,
        [jax.ShapeDtypeStruct(array.shape, array.dtype) for array in arrays],
        [pltpu.SemaphoreType.DMA((count, blocks))],
        vmem=1,
        cost=cost(0, sum(4 * array.size for array in arrays)),
    )(numbers, *[hbm(array) for array in arrays])


def split_rows(numbers, tokens):
    rows, width = tokens.shape[0] // CHUNKS, tokens.shape[1]

    def body(numbers_ref, in_ref, *refs):
        out_refs, sems = refs[:-1], refs[-1]
        run_copies(
            [
                pltpu.make_async_copy(in_ref.at[pl.ds(c * rows, rows)], out_refs[c], sems.at[c])
                for c in range(CHUNKS)
            ]
        )

    return call(
        body,
        [NUMBERS, IN_HBM],
        [WHOLE] * CHUNKS,
        [jax.ShapeDtypeStruct((rows, width), tokens.dtype)] * CHUNKS,
        [pltpu.SemaphoreType.DMA((CHUNKS,))],
        vmem=1,
        cost=cost(0, 4 * tokens.size),
    )(numbers, hbm(tokens))


def gather_step(held, ways, after):
    moved = {}
    for way in ways:
        value = held[way]
        if after is not None:
            value, _ = lax.optimization_barrier((value, after))
        moved[way] = ring_send(value, way)
    return moved


def accumulate(chunks, first, last, weights, before=None, lead=0):
    rows, depth = chunks[0][0].shape
    width = weights[0].shape[1]
    parts, span = len(weights), last - first
    total = rows * len(chunks)
    final = last == lax.axis_size("head")
    dtype = BF16 if final else F32
    pieces = [chunk[index] for chunk in chunks for index in range(first, last)]

    def body(*refs):
        piece_refs = refs[: len(pieces)]
        weight_refs = refs[len(pieces) : len(pieces) + parts]
        out_ref, left = refs[-2:]
        for index, ref in enumerate(piece_refs):
            chunk, piece = divmod(index, span)
            left[chunk * rows : (chunk + 1) * rows, piece * depth : (piece + 1) * depth] = ref[...]
        for part in range(parts):
            term = mm(left[...], weight_refs[part][first * depth : last * depth])
            if before is not None:
                term = term + refs[-3][lead + part]
            out_ref[part] = term.astype(dtype)

    aliased = before is not None and not final
    args = [*pieces, *weights] + ([] if before is None else [before])
    return call(
        body,
        [WHOLE] * len(args),
        WHOLE,
        jax.ShapeDtypeStruct((parts, total, width), dtype),
        [pltpu.VMEM((total, span * depth), BF16)],
        vmem=12,
        cost=cost(
            2 * total * span * depth * width * parts,
            2 * span * depth * (total + width * parts) + 8 * total * width * parts,
        ),
        aliases={len(args) - 1: 0} if aliased else None,
    )(*args)


def lanes(head, size):
    return pl.ds(pl.multiple_of(head * size, size), size)


def normed(values):
    values = values.astype(F32)
    scale = lax.rsqrt(jnp.mean(values * values, axis=-1, keepdims=True) + 1e-06)
    return (values * scale).astype(BF16)


def head_grads(numbers, kv, rate, fast_gate, fast_up, fast_down, before=None):
    rows = kv.shape[1]
    size, hidden_size = fast_gate.shape[1:]
    count = rate.shape[0]
    heads = count // 2

    def body(numbers_ref, kv_ref, rate_ref, gate_ref, up_ref, down_ref, *rest):
        rates = rate_ref[...].T
        lane = lax.broadcasted_iota(jnp.int32, (rows, count), 1)
        for index in range(heads):
            head = numbers_ref[NEAR] + index
            mine = jnp.sum(jnp.where(lane == head, rates, 0.0), axis=1, keepdims=True)
            knorm = normed(kv_ref[0, :, lanes(head, size)])
            target = (-mine * kv_ref[1, :, lanes(head, size)].astype(F32)).astype(BF16)
            gate_pre = mm(knorm, gate_ref[head].astype(BF16))
            up_pre = mm(knorm, up_ref[head].astype(BF16))
            back = mm(target, down_ref[head].astype(BF16), ((1,), (1,)))
            sigma = sigmoid(gate_pre)
            active = gate_pre * sigma
            first = back * up_pre * (sigma + active * (1.0 - sigma))
            both = jnp.concatenate([first.astype(BF16), (back * active).astype(BF16)], axis=1)
            third = (active * up_pre).astype(BF16)
            pair = mm(knorm, both, ((0,), (0,)))
            terms = (pair[:, :hidden_size], pair[:, hidden_size:], mm(target, third, ((0,), (0,))))
            for part, term in enumerate(terms):
                if before is not None:
                    term = term + rest[0][index, part]
                    rest[-1][index, part] = term.astype(BF16)
                    rest[-2][index, part] = term
                else:
                    rest[-1][index, part] = term

    args = [kv, rate, fast_gate, fast_up, fast_down] + ([] if before is None else [before])
    kinds = [F32] if before is None else [F32, BF16]
    return call(
        body,
        [NUMBERS] + [WHOLE] * len(args),
        [WHOLE] * len(kinds),
        [jax.ShapeDtypeStruct((heads, 3, size, hidden_size), kind) for kind in kinds],
        cost=cost(
            12 * heads * rows * size * hidden_size,
            8 * heads * 3 * size * hidden_size,
            heads * rows * hidden_size,
        ),
    )(numbers, *args)


def renew(numbers, kept, received, step, fast_gate, fast_up, fast_down, after):
    heads, _, size, hidden_size = kept.shape

    def body(numbers_ref, step_ref, kept_ref, gate_ref, up_ref, down_ref, *rest):
        out_ref = rest[-1]
        for index in range(heads):
            head = numbers_ref[NEAR] + index
            for part in range(3):
                grad = kept_ref[index, part]
                for more in rest[: len(received)]:
                    grad = grad + more[index, part].astype(F32)
                if part < 2:
                    matrix = (gate_ref, up_ref)[part][head]
                    fan = size
                else:
                    matrix = down_ref[head].T
                    fan = hidden_size
                mean_sq = jnp.sum(grad * grad, keepdims=True) / (size * hidden_size)
                scale = step_ref[head] * fan ** (-0.5) * lax.rsqrt(mean_sq + 1e-06)
                out_ref[index, part] = (matrix - scale * grad).astype(BF16)

    return call(
        body,
        [NUMBERS, NUMBERS] + [WHOLE] * (4 + len(received)) + [AFTER] * len(after),
        WHOLE,
        jax.ShapeDtypeStruct(kept.shape, BF16),
        cost=cost(10 * kept.size, 12 * kept.size),
    )(numbers, step, kept, fast_gate, fast_up, fast_down, *received, *after)


def attend(numbers, query, kv, beside, behind, size):
    total = query.shape[1]
    heads = query.shape[2] // size
    rows = total // 2
    factor = size ** (-0.5) * LOG2E

    def body(numbers_ref, q_ref, kv_ref, beside_ref, behind_ref, out_ref):
        has_halo = numbers_ref[PLACE] > 0
        odd = numbers_ref[PLACE] % 2 == 1
        row = lax.broadcasted_iota(jnp.int32, (rows, rows), 0)
        col = lax.broadcasted_iota(jnp.int32, (rows, rows), 1)

        def block(which, source, lane):
            side, at = divmod(source, 2)
            where = slice(at * rows, (at + 1) * rows)
            if side == 1:
                return kv_ref[which, where, lane]
            return jnp.where(odd, beside_ref[which, where, lane], behind_ref[which, where, lane])

        for head in range(heads):
            lane = slice(head * size, (head + 1) * size)
            for index in range(2):
                where = slice(index * rows, (index + 1) * rows)
                query_block = q_ref[0, where, lane]
                scores = []
                for source in range(index, index + 3):
                    part = mm(query_block, block(0, source, lane), ((1,), (1,))) * factor
                    if source == index:
                        part = jnp.where((col > row) & has_halo, part, -1e30)
                    elif source == index + 2:
                        part = jnp.where(col <= row, part, -1e30)
                    elif source < 2:
                        part = jnp.where(has_halo, part, -1e30)
                    scores.append(part)
                top = functools.reduce(
                    jnp.maximum, [jnp.max(part, axis=-1, keepdims=True) for part in scores]
                )
                sums, result = 0.0, 0.0
                for part, source in zip(scores, range(index, index + 3)):
                    expo = jnp.exp2(part - top)
                    sums = sums + jnp.sum(expo, axis=-1, keepdims=True)
                    result = result + mm(expo.astype(BF16), block(1, source, lane))
                out_ref[where, lane] = result / sums

    return call(
        body,
        [NUMBERS] + [WHOLE] * 4,
        WHOLE,
        jax.ShapeDtypeStruct((total, heads * size), F32),
        cost=cost(
            24 * heads * size * rows * rows,
            8 * total * heads * size,
            6 * heads * rows * rows,
        ),
    )(numbers, query, kv, beside, behind)


def fast_apply(query, gate, upper, down):
    qnorm = normed(query)
    gate_pre = mm(qnorm, gate)
    hidden = gate_pre * sigmoid(gate_pre) * mm(qnorm, upper)
    return mm(hidden.astype(BF16), down, ((1,), (1,)))


def combine_near(numbers, query, attended, nets):
    rows = query.shape[1]
    heads, _, size, hidden_size = nets.shape

    def body(numbers_ref, q_ref, attended_ref, net_ref, out_ref):
        for index in range(heads):
            lane = lanes(numbers_ref[NEAR] + index, size)
            fast = fast_apply(q_ref[0, :, lane], *(net_ref[index, part] for part in range(3)))
            where = slice(index * size, (index + 1) * size)
            out_ref[:, where] = (attended_ref[:, lane] + fast).astype(BF16)

    return call(
        body,
        [NUMBERS] + [WHOLE] * 3,
        WHOLE,
        jax.ShapeDtypeStruct((rows, heads * size), BF16),
        cost=cost(
            6 * heads * rows * size * hidden_size,
            8 * heads * rows * size,
            heads * rows * hidden_size,
        ),
    )(numbers, query, attended, nets)


def partial_out(numbers, offsets, query, attended, nets, near, w_out, after=()):
    known = ring_offsets()
    rows = near.shape[0] // len(known)
    heads, _, size, hidden_size = nets.shape
    depth = heads * size
    count = len(offsets)
    width = w_out.shape[1]
    block = width // 8

    def body(numbers_ref, q_ref, attended_ref, net_ref, near_ref, w_ref, *refs):
        out_refs, far_ref = refs[len(after) : -1], refs[-1]
        starts = [
            pl.multiple_of(numbers_ref[RING + known.index(offset)] * rows, rows)
            for offset in offsets
        ]

        def take(ref, lane):
            return jnp.concatenate([ref[pl.ds(start, rows), lane] for start in starts], axis=0)

        for index in range(heads):
            lane = lanes(numbers_ref[FAR] + index, size)
            fast = fast_apply(
                take(q_ref.at[0], lane), *(net_ref[index, part] for part in range(3))
            )
            where = slice(index * size, (index + 1) * size)
            far_ref[:, where] = (take(attended_ref, lane) + fast).astype(BF16)
        left = take(near_ref, slice(None))
        near_rows = pl.ds(pl.multiple_of(numbers_ref[NEAR] * size, size), depth)
        far_rows = pl.ds(pl.multiple_of(numbers_ref[FAR] * size, size), depth)
        for column in range(0, width, block):
            result = mm(left, w_ref[near_rows, column : column + block])
            result += mm(far_ref[...], w_ref[far_rows, column : column + block])
            result = result.astype(BF16)
            half, at = divmod(column, width // 2)
            for index in range(count):
                out_refs[2 * index + half][:, at : at + block] = result[
                    index * rows : (index + 1) * rows
                ]

    outs = call(
        body,
        [NUMBERS] + [WHOLE] * 5 + [AFTER] * len(after),
        [WHOLE] * (2 * count),
        [jax.ShapeDtypeStruct((rows, width // 2), BF16)] * (2 * count),
        [pltpu.VMEM((count * rows, depth), BF16)],
        vmem=8,
        cost=cost(4 * count * rows * depth * width, 2 * width * (2 * depth + count * rows)),
    )(numbers, query, attended, nets, near, w_out, *after)
    return {offset: tuple(outs[2 * at : 2 * at + 2]) for at, offset in enumerate(offsets)}


def ring_reduce(numbers, query, attended, nets, near, w_out):
    steps = lax.axis_size("head") // 2
    signed = [sign * step for step in range(steps - 1, 0, -1) for sign in (1, -1)]
    shared = (query, attended, nets, near, w_out)
    parts = partial_out(numbers, [steps] + signed[:2], *shared)
    coming = {}
    ordered = ()
    for which in range(2 * steps - 1):
        step, half = steps - (which + 1) // 2, which % 2
        if which == 2:
            parts |= partial_out(numbers, signed[2:] + [0], *shared, tuple(coming.values())[:2])
        terms = []
        for way in (1, -1):
            side = half if way == 1 else 1 - half
            term = parts[steps if step == steps else way * step][side]
            if (way, side) in coming:
                term = (term.astype(F32) + coming[way, side].astype(F32)).astype(BF16)
            terms.append(term)
        ordered = lax.optimization_barrier((*terms, *ordered))[:2]
        for way, term in zip((1, -1), ordered):
            coming[way, half if way == 1 else 1 - half] = ring_send(term, way)
    sides = {1: 1 - half, -1: half}
    totals = add_pair(
        [parts[0][sides[way]] for way in (1, -1)], [coming.pop((way, sides[way])) for way in (1, -1)]
    )
    totals = {sides[way]: total for way, total in zip((1, -1), totals)}
    ends = [totals[side] for side in range(2)]
    for (_, side), more in coming.items():
        ends[side] = ends[side] + more.astype(F32)
    return jnp.concatenate([end.astype(BF16) for end in ends], axis=1)


def add_pair(own, came):
    def body(*refs):
        for index in range(2):
            refs[4 + index][...] = refs[index][...].astype(F32) + refs[2 + index][...].astype(F32)

    return call(
        body,
        [WHOLE] * 4,
        [WHOLE] * 2,
        [jax.ShapeDtypeStruct(value.shape, F32) for value in own],
        cost=cost(0, 64 * own[0].size),
    )(*own, *came)


def swap(value, bit):
    count = lax.axis_size("tok")
    return lax.ppermute(value, "tok", [(index, index ^ bit) for index in range(count)])


def shards(
    tokens, w_query, w_key, w_value, w_out, fast_gate, fast_up, fast_down, token_rate, head_step
):
    local_heads, head_size, _ = fast_gate.shape
    tok_count = lax.axis_size("tok")
    steps = lax.axis_size("head") // 2
    nets = (fast_gate, fast_up, fast_down)
    numbers = own_numbers(local_heads // 2)
    rate = token_rate.T
    rate_beside = swap(rate, 1)

    own = split_rows(numbers, tokens)
    weights = load(numbers, [w_key, w_value, w_query])
    chunks = [[piece] for piece in own]
    held = [{1: piece, -1: piece} for piece in own]
    sums, done = None, 0
    for step in range(1, steps + 1):
        after = (None, None, weights[0], (sums, rate_beside))[step] if step < 4 else sums
        for c in range(CHUNKS):
            last = (1,) if c % 2 == 0 else (-1,)
            held[c] = gather_step(held[c], (1, -1) if step < steps else last, after)
            chunks[c] += held[c].values()
        if step > 1:
            sums = accumulate([chunk[: 2 * step - 1] for chunk in chunks], done, 2 * step - 1, weights, sums)
            done = 2 * step - 1
    kv = accumulate(chunks, done, 2 * steps, weights[:2], sums)
    query = accumulate(chunks, done, 2 * steps, weights[2:], sums, 2)

    beside = swap(kv, 1)
    behind = lax.ppermute(kv, "tok", [(index, index + 1) for index in range(1, tok_count - 1, 2)])
    (grads,) = head_grads(numbers, kv, rate, *nets)
    grads, travel = head_grads(numbers, beside, rate_beside, *nets, grads)
    received = []
    for bit in range(1, tok_count.bit_length() - 1):
        if received:
            travel = grads
            for more in received:
                travel = travel + more.astype(F32)
            travel = travel.astype(BF16)
        received.append(swap(travel, 1 << bit))
    attended = attend(numbers, query, kv, beside, behind, head_size)
    mine = renew(numbers, grads, received, head_step, *nets, (attended,))
    near = combine_near(numbers, query, attended, mine)
    return ring_reduce(numbers, query, attended, swap(mine, 1), near, w_out)


def solution(mesh):
    placed = (
        P("tok", "head"),
        P(None, "head"),
        P(None, "head"),
        P(None, "head"),
        P("head", None),
        P("head", None, None),
        P("head", None, None),
        P("head", None, None),
        P("tok", "head"),
        P("head"),
    )
    return jax.shard_map(
        shards, mesh=mesh, in_specs=placed, out_specs=P(("tok", "head"), None), check_vma=False
    )
```

```python
import functools

import jax
import jax.numpy as jnp
from jax import lax
from jax.experimental import pallas as pl
from jax.experimental.pallas import tpu as pltpu
from jax.sharding import PartitionSpec as P

WINDOW = 512
CHUNKS = 2
F32 = jnp.float32
BF16 = jnp.bfloat16
LOG2E = 1.4426950408889634


def call(body, in_specs, out_specs, out_shape, scratch=(), vmem=8, cost=None, aliases=None):
    return pl.pallas_call(
        body,
        in_specs=in_specs,
        out_specs=out_specs,
        out_shape=out_shape,
        scratch_shapes=list(scratch),
        input_output_aliases=aliases or {},
        cost_estimate=cost,
        compiler_params=pltpu.CompilerParams(vmem_limit_bytes=vmem * 1024 * 1024),
    )


def cost(flops, moved, exps=0):
    return pl.CostEstimate(flops=int(flops), bytes_accessed=int(moved), transcendentals=int(exps))


WHOLE = pl.BlockSpec(memory_space=pltpu.VMEM)
AFTER = pl.BlockSpec(memory_space=pl.ANY)
SCALARS = pl.BlockSpec(memory_space=pltpu.SMEM)
IN_HBM = pl.BlockSpec(memory_space=pltpu.HBM)


def mm(left, right, dims=((1,), (0,))):
    return lax.dot_general(left, right, (dims, ((), ())), preferred_element_type=F32)


def sigmoid(x):
    return 0.5 * jnp.tanh(0.5 * x) + 0.5


def ring_order(count):
    return list(range(0, count, 2)) + list(range(count - 1, 0, -2))


def ring_send(value, step):
    order = ring_order(lax.axis_size("head"))
    count = len(order)
    return lax.ppermute(
        value, "head", [(order[i], order[(i + step) % count]) for i in range(count)]
    )


def ring_offsets():
    steps = lax.axis_size("head") // 2
    return [0] + [way * step for step in range(1, steps) for way in (-1, 1)] + [steps]


def ring_index(offset):
    count = lax.axis_size("head")
    me = lax.axis_index("head")
    at = lax.rem(jnp.where(me % 2 == 0, me // 2, count - 1 - me // 2) + offset + count, count)
    return jnp.where(at < count // 2, 2 * at, 2 * (count - 1 - at) + 1)


def first_head(heads, other=False):
    side = lax.axis_index("tok") % 2
    return (1 - side if other else side) * heads


def hbm(array):
    return pltpu.with_memory_space_constraint(array, pltpu.HBM)


def run_copies(copies):
    for copy in copies:
        copy.start()
    for copy in copies:
        copy.wait()


def load(arrays):
    count = len(arrays)
    blocks = len(ring_offsets())
    size = arrays[0].shape[0] // blocks

    def body(*refs):
        out_refs, sems = refs[count:-1], refs[-1]
        starts = [pl.multiple_of(ring_index(offset) * size, size) for offset in ring_offsets()]
        run_copies(
            [
                pltpu.make_async_copy(
                    refs[index].at[pl.ds(starts[block], size)],
                    out_refs[index].at[pl.ds(block * size, size)],
                    sems.at[index, block],
                )
                for block in range(blocks)
                for index in range(count)
            ]
        )

    return call(
        body,
        [IN_HBM] * count,
        [WHOLE] * count,
        [jax.ShapeDtypeStruct(array.shape, array.dtype) for array in arrays],
        [pltpu.SemaphoreType.DMA((count, blocks))],
        vmem=1,
        cost=cost(0, sum(4 * array.size for array in arrays)),
    )(*[hbm(array) for array in arrays])


def split_rows(tokens):
    rows, width = tokens.shape[0] // CHUNKS, tokens.shape[1]

    def body(in_ref, *refs):
        out_refs, sems = refs[:-1], refs[-1]
        run_copies(
            [
                pltpu.make_async_copy(in_ref.at[pl.ds(c * rows, rows)], out_refs[c], sems.at[c])
                for c in range(CHUNKS)
            ]
        )

    return call(
        body,
        [IN_HBM],
        [WHOLE] * CHUNKS,
        [jax.ShapeDtypeStruct((rows, width), tokens.dtype)] * CHUNKS,
        [pltpu.SemaphoreType.DMA((CHUNKS,))],
        vmem=1,
        cost=cost(0, 4 * tokens.size),
    )(hbm(tokens))


def gather_step(held, ways, after):
    moved = {}
    for way in ways:
        value = held[way]
        if after is not None:
            value, _ = lax.optimization_barrier((value, after))
        moved[way] = ring_send(value, way)
    return moved


def accumulate(chunks, first, last, weights, before=None, lead=0, shared=False):
    rows, depth = chunks[0][0].shape
    width = weights[0].shape[1]
    parts, span = len(weights), last - first
    total = rows * len(chunks)
    final = last == lax.axis_size("head")
    dtype = BF16 if final else F32
    pieces = [chunk[index] for chunk in chunks for index in range(first, last)]

    def body(*refs):
        piece_refs = refs[: len(pieces)]
        weight_refs = refs[len(pieces) : len(pieces) + parts]
        out_ref, left = refs[-2 - shared], refs[-1]
        for index, ref in enumerate(piece_refs):
            chunk, piece = divmod(index, span)
            left[chunk * rows : (chunk + 1) * rows, piece * depth : (piece + 1) * depth] = ref[...]
        for part in range(parts):
            term = mm(left[...], weight_refs[part][first * depth : last * depth])
            if before is not None:
                term = term + refs[len(args) - 1][lead + part]
            out_ref[part] = term.astype(dtype)
            if shared:
                refs[-2][part] = out_ref[part, :, lanes(1 - lax.axis_index("tok") % 2, width // 2)]

    aliased = before is not None and not final
    args = [*pieces, *weights] + ([] if before is None else [before])
    return call(
        body,
        [WHOLE] * len(args),
        [WHOLE] * (1 + shared),
        [jax.ShapeDtypeStruct((parts, total, size), dtype) for size in (width, width // 2)[: 1 + shared]],
        [pltpu.VMEM((total, span * depth), BF16)],
        vmem=12,
        cost=cost(
            2 * total * span * depth * width * parts,
            2 * span * depth * (total + width * parts) + 8 * total * width * parts,
        ),
        aliases={len(args) - 1: 0} if aliased else None,
    )(*args)


def lanes(head, size):
    return pl.ds(pl.multiple_of(head * size, size), size)


def normed(values):
    values = values.astype(F32)
    scale = lax.rsqrt(jnp.mean(values * values, axis=-1, keepdims=True) + 1e-06)
    return (values * scale).astype(BF16)


def head_grads(kv, rate, fast_gate, fast_up, fast_down, before=None):
    rows = kv.shape[1]
    size, hidden_size = fast_gate.shape[1:]
    count = rate.shape[0]
    heads = count // 2
    whole = kv.shape[2] == count * size

    def body(kv_ref, rate_ref, gate_ref, up_ref, down_ref, *rest):
        rates = rate_ref[...].T
        column = lax.broadcasted_iota(jnp.int32, (rows, count), 1)
        for index in range(heads):
            head = first_head(heads) + index
            mine = jnp.sum(jnp.where(column == head, rates, 0.0), axis=1, keepdims=True)
            lane = lanes(head if whole else index, size)
            knorm = normed(kv_ref[0, :, lane])
            target = (-mine * kv_ref[1, :, lane].astype(F32)).astype(BF16)
            gate_pre = mm(knorm, gate_ref[head].astype(BF16))
            up_pre = mm(knorm, up_ref[head].astype(BF16))
            back = mm(target, down_ref[head].astype(BF16), ((1,), (1,)))
            sigma = sigmoid(gate_pre)
            active = gate_pre * sigma
            first = back * up_pre * (sigma + active * (1.0 - sigma))
            both = jnp.concatenate([first.astype(BF16), (back * active).astype(BF16)], axis=1)
            third = (active * up_pre).astype(BF16)
            pair = mm(knorm, both, ((0,), (0,)))
            terms = (pair[:, :hidden_size], pair[:, hidden_size:], mm(target, third, ((0,), (0,))))
            for part, term in enumerate(terms):
                if before is not None:
                    term = term + rest[0][index, part]
                    rest[-1][index, part] = term.astype(BF16)
                    rest[-2][index, part] = term
                else:
                    rest[-1][index, part] = term

    args = [kv, rate, fast_gate, fast_up, fast_down] + ([] if before is None else [before])
    kinds = [F32] if before is None else [F32, BF16]
    return call(
        body,
        [WHOLE] * len(args),
        [WHOLE] * len(kinds),
        [jax.ShapeDtypeStruct((heads, 3, size, hidden_size), kind) for kind in kinds],
        cost=cost(
            12 * heads * rows * size * hidden_size,
            8 * heads * 3 * size * hidden_size,
            heads * rows * hidden_size,
        ),
    )(*args)


def renew(kept, received, step, fast_gate, fast_up, fast_down, after):
    heads, _, size, hidden_size = kept.shape

    def body(step_ref, kept_ref, gate_ref, up_ref, down_ref, *rest):
        out_ref = rest[-1]
        for index in range(heads):
            head = first_head(heads) + index
            for part in range(3):
                grad = kept_ref[index, part]
                for more in rest[: len(received)]:
                    grad = grad + more[index, part].astype(F32)
                if part < 2:
                    matrix = (gate_ref, up_ref)[part][head]
                    fan = size
                else:
                    matrix = down_ref[head].T
                    fan = hidden_size
                mean_sq = jnp.sum(grad * grad, keepdims=True) / (size * hidden_size)
                scale = step_ref[head] * fan ** (-0.5) * lax.rsqrt(mean_sq + 1e-06)
                out_ref[index, part] = (matrix - scale * grad).astype(BF16)

    return call(
        body,
        [SCALARS] + [WHOLE] * (4 + len(received)) + [AFTER] * len(after),
        WHOLE,
        jax.ShapeDtypeStruct(kept.shape, BF16),
        cost=cost(10 * kept.size, 12 * kept.size),
    )(step, kept, fast_gate, fast_up, fast_down, *received, *after)


def attend_blocks(query, blocks, earlier=None):
    factor = query.shape[-1] ** (-0.5) * LOG2E
    scores = []
    for key, _, allowed in blocks:
        part = mm(query, key, ((1,), (1,))) * factor
        scores.append(part if allowed is None else jnp.where(allowed, part, -1e30))
    tops = [jnp.max(part, axis=-1, keepdims=True) for part in scores]
    result, total = 0.0, 0.0
    if earlier is not None:
        tops.append(earlier[1])
    top = functools.reduce(jnp.maximum, tops)
    if earlier is not None:
        shrink = jnp.exp2(earlier[1] - top)
        result, total = earlier[0] * shrink, earlier[2] * shrink
    for part, (_, value, _) in zip(scores, blocks):
        weight = jnp.exp2(part - top)
        total = total + jnp.sum(weight, axis=-1, keepdims=True)
        result = result + mm(weight.astype(BF16), value)
    return result, top, total


def halves(rows):
    return [slice(index * rows // 2, (index + 1) * rows // 2) for index in range(2)]


def earlier_blocks(ref, index, lane):
    rows = ref.shape[1]
    row = lax.broadcasted_iota(jnp.int32, (rows // 2, rows // 2), 0)
    col = lax.broadcasted_iota(jnp.int32, (rows // 2, rows // 2), 1)
    blocks = [(ref[0, halves(rows)[index], lane], ref[1, halves(rows)[index], lane], col > row)]
    if index == 0:
        blocks.append((ref[0, halves(rows)[1], lane], ref[1, halves(rows)[1], lane], None))
    return blocks


def attend_own(query, kv, size):
    rows = query.shape[1]
    heads = query.shape[2] // size
    row = (rows // 2, rows // 2)

    def body(q_ref, kv_ref, out_ref, stats_ref):
        causal = lax.broadcasted_iota(jnp.int32, row, 1) <= lax.broadcasted_iota(jnp.int32, row, 0)
        for index, where in enumerate(halves(rows)):
            stats = []
            for head in range(heads):
                lane = slice(head * size, (head + 1) * size)
                blocks = [
                    (kv_ref[0, keys, lane], kv_ref[1, keys, lane], causal if at == index else None)
                    for at, keys in enumerate(halves(rows)[: index + 1])
                ]
                result, top, total = attend_blocks(q_ref[0, where, lane], blocks)
                out_ref[where, lane] = result
                stats += [top, total]
            stats_ref[where] = jnp.concatenate(stats, axis=1)

    return call(
        body,
        [WHOLE] * 2,
        [WHOLE] * 2,
        [
            jax.ShapeDtypeStruct((rows, heads * size), F32),
            jax.ShapeDtypeStruct((rows, 2 * heads), F32),
        ],
        cost=cost(3 * heads * size * rows * rows, 8 * rows * heads * size, heads * rows * rows),
    )(query, kv)


def attend_behind(summed, stats, query, behind, size):
    rows = query.shape[1]
    heads = query.shape[2] // size

    def body(sum_ref, stats_ref, q_ref, behind_ref, out_ref):
        needed = lax.axis_index("tok") > 0

        @pl.when(needed)
        def _():
            for index, where in enumerate(halves(rows)):
                for head in range(heads):
                    lane = slice(head * size, (head + 1) * size)
                    top, total = (stats_ref[where, 2 * head + at : 2 * head + at + 1] for at in (0, 1))
                    result, _, total = attend_blocks(
                        q_ref[0, where, lane],
                        earlier_blocks(behind_ref, index, lane),
                        (sum_ref[where, lane], top, total),
                    )
                    out_ref[where, lane] = result / total

        @pl.when(jnp.logical_not(needed))
        def _():
            for head in range(heads):
                lane = slice(head * size, (head + 1) * size)
                out_ref[:, lane] = sum_ref[:, lane] / stats_ref[:, 2 * head + 1 : 2 * head + 2]

    return call(
        body,
        [WHOLE] * 4,
        WHOLE,
        jax.ShapeDtypeStruct(summed.shape, F32),
        cost=cost(3 * heads * size * rows * rows, 8 * rows * heads * size, heads * rows * rows),
    )(summed, stats, query, behind)


def fast_apply(query, gate, upper, down):
    qnorm = normed(query)
    gate_pre = mm(qnorm, gate)
    hidden = gate_pre * sigmoid(gate_pre) * mm(qnorm, upper)
    return mm(hidden.astype(BF16), down, ((1,), (1,)))


def combine_near(query, attended, nets):
    rows = query.shape[1]
    heads, _, size, hidden_size = nets.shape

    def body(q_ref, attended_ref, net_ref, out_ref):
        for index in range(heads):
            lane = lanes(first_head(heads) + index, size)
            fast = fast_apply(q_ref[0, :, lane], *(net_ref[index, part] for part in range(3)))
            where = slice(index * size, (index + 1) * size)
            out_ref[:, where] = (attended_ref[:, lane] + fast).astype(BF16)

    return call(
        body,
        [WHOLE] * 3,
        WHOLE,
        jax.ShapeDtypeStruct((rows, heads * size), BF16),
        cost=cost(
            6 * heads * rows * size * hidden_size,
            8 * heads * rows * size,
            heads * rows * hidden_size,
        ),
    )(query, attended, nets)


def partial_out(offsets, query, attended, nets, near, w_out, after=()):
    rows = near.shape[0] // lax.axis_size("head")
    heads, _, size, hidden_size = nets.shape
    depth = heads * size
    count = len(offsets)
    width = w_out.shape[1]
    block = width // 8

    def body(q_ref, attended_ref, net_ref, near_ref, w_ref, *refs):
        out_refs, far_ref = refs[len(after) : -1], refs[-1]
        starts = [pl.multiple_of(ring_index(offset) * rows, rows) for offset in offsets]

        def take(ref, lane):
            return jnp.concatenate([ref[pl.ds(start, rows), lane] for start in starts], axis=0)

        for index in range(heads):
            lane = lanes(first_head(heads, True) + index, size)
            fast = fast_apply(
                take(q_ref.at[0], lane), *(net_ref[index, part] for part in range(3))
            )
            where = slice(index * size, (index + 1) * size)
            far_ref[:, where] = (take(attended_ref, lane) + fast).astype(BF16)
        left = take(near_ref, slice(None))
        near_rows = pl.ds(pl.multiple_of(first_head(heads) * size, depth), depth)
        far_rows = pl.ds(pl.multiple_of(first_head(heads, True) * size, depth), depth)
        for column in range(0, width, block):
            result = mm(left, w_ref[near_rows, column : column + block])
            result += mm(far_ref[...], w_ref[far_rows, column : column + block])
            result = result.astype(BF16)
            half, at = divmod(column, width // 2)
            for index in range(count):
                out_refs[2 * index + half][:, at : at + block] = result[
                    index * rows : (index + 1) * rows
                ]

    outs = call(
        body,
        [WHOLE] * 5 + [AFTER] * len(after),
        [WHOLE] * (2 * count),
        [jax.ShapeDtypeStruct((rows, width // 2), BF16)] * (2 * count),
        [pltpu.VMEM((count * rows, depth), BF16)],
        vmem=8,
        cost=cost(4 * count * rows * depth * width, 2 * width * (2 * depth + count * rows)),
    )(query, attended, nets, near, w_out, *after)
    return {offset: tuple(outs[2 * at : 2 * at + 2]) for at, offset in enumerate(offsets)}


def ring_reduce(query, attended, nets, near, w_out):
    steps = lax.axis_size("head") // 2
    signed = [sign * step for step in range(steps - 1, 0, -1) for sign in (1, -1)]
    shared = (query, attended, nets, near, w_out)
    parts = partial_out([steps], *shared) | partial_out(signed[:2], *shared)
    coming = {}
    ordered = ()
    for which in range(2 * steps - 1):
        step, half = steps - (which + 1) // 2, which % 2
        if which == 2:
            parts |= partial_out(signed[2:] + [0], *shared, tuple(coming.values())[:2])
        terms = []
        for way in (1, -1):
            side = half if way == 1 else 1 - half
            term = parts[steps if step == steps else way * step][side]
            if (way, side) in coming:
                term = (term.astype(F32) + coming[way, side].astype(F32)).astype(BF16)
            terms.append(term)
        ordered = lax.optimization_barrier((*terms, *ordered))[:2]
        for way, term in zip((1, -1), ordered):
            coming[way, half if way == 1 else 1 - half] = ring_send(term, way)
    sides = {1: 1 - half, -1: half}
    totals = add_pair(
        [parts[0][sides[way]] for way in (1, -1)], [coming.pop((way, sides[way])) for way in (1, -1)]
    )
    totals = {sides[way]: total for way, total in zip((1, -1), totals)}
    ends = [totals[side] for side in range(2)]
    for (_, side), more in coming.items():
        ends[side] = ends[side] + more.astype(F32)
    return jnp.concatenate([end.astype(BF16) for end in ends], axis=1)


def add_pair(own, came):
    def body(*refs):
        for index in range(2):
            refs[4 + index][...] = refs[index][...].astype(F32) + refs[2 + index][...].astype(F32)

    return call(
        body,
        [WHOLE] * 4,
        [WHOLE] * 2,
        [jax.ShapeDtypeStruct(value.shape, F32) for value in own],
        cost=cost(0, 64 * own[0].size),
    )(*own, *came)


def swap(value, bit):
    count = lax.axis_size("tok")
    return lax.ppermute(value, "tok", [(index, index ^ bit) for index in range(count)])


def shards(
    tokens, w_query, w_key, w_value, w_out, fast_gate, fast_up, fast_down, token_rate, head_step
):
    local_heads, head_size, _ = fast_gate.shape
    tok_count = lax.axis_size("tok")
    steps = lax.axis_size("head") // 2
    nets = (fast_gate, fast_up, fast_down)
    rate = token_rate.T
    rate_beside = swap(rate, 1)

    own = split_rows(tokens)
    weights = load([w_key, w_value, w_query])
    chunks = [[piece] for piece in own]
    held = [{1: piece, -1: piece} for piece in own]
    sums, done = None, 0
    for step in range(1, steps + 1):
        after = (None, None, weights[0], (sums, rate_beside))[step] if step < 4 else sums
        for c in range(CHUNKS):
            last = (1,) if c % 2 == 0 else (-1,)
            held[c] = gather_step(held[c], (1, -1) if step < steps else last, after)
            chunks[c] += held[c].values()
        if step > 1:
            known = [chunk[: 2 * step - 1] for chunk in chunks]
            (sums,) = accumulate(known, done, 2 * step - 1, weights, sums)
            done = 2 * step - 1
    kv, far = accumulate(chunks, done, 2 * steps, weights[:2], sums, shared=True)
    (query,) = accumulate(chunks, done, 2 * steps, weights[2:], sums, 2)

    behind = lax.ppermute(kv, "tok", [(index, index + 1) for index in range(tok_count - 1)])
    beside = swap(far, 1)
    (grads,) = head_grads(kv, rate, *nets)
    grads, travel = head_grads(beside, rate_beside, *nets, grads)
    received = []
    for bit in range(1, tok_count.bit_length() - 1):
        if received:
            travel = grads
            for more in received:
                travel = travel + more.astype(F32)
            travel = travel.astype(BF16)
        received.append(swap(travel, 1 << bit))
    summed, stats = attend_own(query, kv, head_size)
    attended = attend_behind(summed, stats, query, behind, head_size)
    mine = renew(grads, received, head_step, *nets, (attended,))
    near = combine_near(query, attended, mine)
    return ring_reduce(query, attended, swap(mine, 1), near, w_out)


def solution(mesh):
    placed = (
        P("tok", "head"),
        P(None, "head"),
        P(None, "head"),
        P(None, "head"),
        P("head", None),
        P("head", None, None),
        P("head", None, None),
        P("head", None, None),
        P("tok", "head"),
        P("head"),
    )
    return jax.shard_map(
        shards, mesh=mesh, in_specs=placed, out_specs=P(("tok", "head"), None), check_vma=False
    )
```

```python
import functools

import jax
import jax.numpy as jnp
from jax import lax
from jax.experimental import pallas as pl
from jax.experimental.pallas import tpu as pltpu
from jax.sharding import PartitionSpec as P

WINDOW = 512
CHUNKS = 2
F32 = jnp.float32
BF16 = jnp.bfloat16
LOG2E = 1.4426950408889634


def call(body, in_specs, out_specs, out_shape, scratch=(), vmem=8, cost=None, aliases=None):
    return pl.pallas_call(
        body,
        in_specs=in_specs,
        out_specs=out_specs,
        out_shape=out_shape,
        scratch_shapes=list(scratch),
        input_output_aliases=aliases or {},
        cost_estimate=cost,
        compiler_params=pltpu.CompilerParams(vmem_limit_bytes=vmem * 1024 * 1024),
    )


def cost(flops, moved, exps=0):
    return pl.CostEstimate(flops=int(flops), bytes_accessed=int(moved), transcendentals=int(exps))


WHOLE = pl.BlockSpec(memory_space=pltpu.VMEM)
AFTER = pl.BlockSpec(memory_space=pl.ANY)
SCALARS = pl.BlockSpec(memory_space=pltpu.SMEM)
IN_HBM = pl.BlockSpec(memory_space=pltpu.HBM)


def mm(left, right, dims=((1,), (0,))):
    return lax.dot_general(left, right, (dims, ((), ())), preferred_element_type=F32)


def sigmoid(x):
    return 0.5 * jnp.tanh(0.5 * x) + 0.5


def ring_order(count):
    return list(range(0, count, 2)) + list(range(count - 1, 0, -2))


def ring_send(value, step):
    order = ring_order(lax.axis_size("head"))
    count = len(order)
    return lax.ppermute(
        value, "head", [(order[i], order[(i + step) % count]) for i in range(count)]
    )


def ring_offsets():
    steps = lax.axis_size("head") // 2
    return [0] + [way * step for step in range(1, steps) for way in (-1, 1)] + [steps]


def ring_index(offset):
    count = lax.axis_size("head")
    me = lax.axis_index("head")
    at = lax.rem(jnp.where(me % 2 == 0, me // 2, count - 1 - me // 2) + offset + count, count)
    return jnp.where(at < count // 2, 2 * at, 2 * (count - 1 - at) + 1)


def first_head(heads, other=False):
    side = lax.axis_index("tok") % 2
    return (1 - side if other else side) * heads


def hbm(array):
    return pltpu.with_memory_space_constraint(array, pltpu.HBM)


def run_copies(copies):
    for copy in copies:
        copy.start()
    for copy in copies:
        copy.wait()


def load(arrays):
    count = len(arrays)
    blocks = len(ring_offsets())
    size = arrays[0].shape[0] // blocks

    def body(*refs):
        out_refs, sems = refs[count:-1], refs[-1]
        starts = [pl.multiple_of(ring_index(offset) * size, size) for offset in ring_offsets()]
        run_copies(
            [
                pltpu.make_async_copy(
                    refs[index].at[pl.ds(starts[block], size)],
                    out_refs[index].at[pl.ds(block * size, size)],
                    sems.at[index, block],
                )
                for block in range(blocks)
                for index in range(count)
            ]
        )

    return call(
        body,
        [IN_HBM] * count,
        [WHOLE] * count,
        [jax.ShapeDtypeStruct(array.shape, array.dtype) for array in arrays],
        [pltpu.SemaphoreType.DMA((count, blocks))],
        vmem=1,
        cost=cost(0, sum(4 * array.size for array in arrays)),
    )(*[hbm(array) for array in arrays])


def split_rows(tokens):
    rows, width = tokens.shape[0] // CHUNKS, tokens.shape[1]

    def body(in_ref, *refs):
        out_refs, sems = refs[:-1], refs[-1]
        run_copies(
            [
                pltpu.make_async_copy(in_ref.at[pl.ds(c * rows, rows)], out_refs[c], sems.at[c])
                for c in range(CHUNKS)
            ]
        )

    return call(
        body,
        [IN_HBM],
        [WHOLE] * CHUNKS,
        [jax.ShapeDtypeStruct((rows, width), tokens.dtype)] * CHUNKS,
        [pltpu.SemaphoreType.DMA((CHUNKS,))],
        vmem=1,
        cost=cost(0, 4 * tokens.size),
    )(hbm(tokens))


def gather_step(held, ways, after):
    moved = {}
    for way in ways:
        value = held[way]
        if after is not None:
            value, _ = lax.optimization_barrier((value, after))
        moved[way] = ring_send(value, way)
    return moved


def accumulate(chunks, first, last, weights, before=None, lead=0, shared=False):
    rows, depth = chunks[0][0].shape
    width = weights[0].shape[1]
    parts, span = len(weights), last - first
    total = rows * len(chunks)
    final = last == lax.axis_size("head")
    dtype = BF16 if final else F32
    pieces = [chunk[index] for chunk in chunks for index in range(first, last)]

    def body(*refs):
        piece_refs = refs[: len(pieces)]
        weight_refs = refs[len(pieces) : len(pieces) + parts]
        out_ref, left = refs[-2 - 2 * shared], refs[-1]
        for index, ref in enumerate(piece_refs):
            chunk, piece = divmod(index, span)
            left[chunk * rows : (chunk + 1) * rows, piece * depth : (piece + 1) * depth] = ref[...]
        for part in range(parts):
            term = mm(left[...], weight_refs[part][first * depth : last * depth])
            if before is not None:
                term = term + refs[len(args) - 1][lead + part]
            out_ref[part] = term.astype(dtype)
            if shared:
                side = lax.axis_index("tok") % 2
                refs[-3][part] = out_ref[part, :, lanes(1 - side, width // 2)]
                refs[-2][part] = out_ref[part, :, lanes(side, width // 2)]

    aliased = before is not None and not final
    args = [*pieces, *weights] + ([] if before is None else [before])
    return call(
        body,
        [WHOLE] * len(args),
        [WHOLE] * (1 + 2 * shared),
        [
            jax.ShapeDtypeStruct((parts, total, size), dtype)
            for size in (width, width // 2, width // 2)[: 1 + 2 * shared]
        ],
        [pltpu.VMEM((total, span * depth), BF16)],
        vmem=12,
        cost=cost(
            2 * total * span * depth * width * parts,
            2 * span * depth * (total + width * parts) + 8 * total * width * parts,
        ),
        aliases={len(args) - 1: 0} if aliased else None,
    )(*args)


def lanes(head, size):
    return pl.ds(pl.multiple_of(head * size, size), size)


def normed(values):
    values = values.astype(F32)
    scale = lax.rsqrt(jnp.mean(values * values, axis=-1, keepdims=True) + 1e-06)
    return (values * scale).astype(BF16)


def head_grads(kv, rate, fast_gate, fast_up, fast_down, before=None):
    rows = kv.shape[1]
    size, hidden_size = fast_gate.shape[1:]
    count = rate.shape[0]
    heads = count // 2
    whole = kv.shape[2] == count * size

    def body(kv_ref, rate_ref, gate_ref, up_ref, down_ref, *rest):
        rates = rate_ref[...].T
        column = lax.broadcasted_iota(jnp.int32, (rows, count), 1)
        for index in range(heads):
            head = first_head(heads) + index
            mine = jnp.sum(jnp.where(column == head, rates, 0.0), axis=1, keepdims=True)
            lane = lanes(head if whole else index, size)
            knorm = normed(kv_ref[0, :, lane])
            target = (-mine * kv_ref[1, :, lane].astype(F32)).astype(BF16)
            gate_pre = mm(knorm, gate_ref[head].astype(BF16))
            up_pre = mm(knorm, up_ref[head].astype(BF16))
            back = mm(target, down_ref[head].astype(BF16), ((1,), (1,)))
            sigma = sigmoid(gate_pre)
            active = gate_pre * sigma
            first = back * up_pre * (sigma + active * (1.0 - sigma))
            both = jnp.concatenate([first.astype(BF16), (back * active).astype(BF16)], axis=1)
            third = (active * up_pre).astype(BF16)
            pair = mm(knorm, both, ((0,), (0,)))
            terms = (pair[:, :hidden_size], pair[:, hidden_size:], mm(target, third, ((0,), (0,))))
            for part, term in enumerate(terms):
                if before is not None:
                    term = term + rest[0][index, part]
                    rest[-1][index, part] = term.astype(BF16)
                    rest[-2][index, part] = term
                else:
                    rest[-1][index, part] = term

    args = [kv, rate, fast_gate, fast_up, fast_down] + ([] if before is None else [before])
    kinds = [F32] if before is None else [F32, BF16]
    return call(
        body,
        [WHOLE] * len(args),
        [WHOLE] * len(kinds),
        [jax.ShapeDtypeStruct((heads, 3, size, hidden_size), kind) for kind in kinds],
        cost=cost(
            12 * heads * rows * size * hidden_size,
            8 * heads * 3 * size * hidden_size,
            heads * rows * hidden_size,
        ),
    )(*args)


def renew(kept, received, step, fast_gate, fast_up, fast_down, after):
    heads, _, size, hidden_size = kept.shape

    def body(step_ref, kept_ref, gate_ref, up_ref, down_ref, *rest):
        out_ref = rest[-1]
        for index in range(heads):
            head = first_head(heads) + index
            for part in range(3):
                grad = kept_ref[index, part]
                for more in rest[: len(received)]:
                    grad = grad + more[index, part].astype(F32)
                if part < 2:
                    matrix = (gate_ref, up_ref)[part][head]
                    fan = size
                else:
                    matrix = down_ref[head].T
                    fan = hidden_size
                mean_sq = jnp.sum(grad * grad, keepdims=True) / (size * hidden_size)
                scale = step_ref[head] * fan ** (-0.5) * lax.rsqrt(mean_sq + 1e-06)
                out_ref[index, part] = (matrix - scale * grad).astype(BF16)

    return call(
        body,
        [SCALARS] + [WHOLE] * (4 + len(received)) + [AFTER] * len(after),
        WHOLE,
        jax.ShapeDtypeStruct(kept.shape, BF16),
        cost=cost(10 * kept.size, 12 * kept.size),
    )(step, kept, fast_gate, fast_up, fast_down, *received, *after)


def attend_blocks(query, blocks):
    factor = query.shape[-1] ** (-0.5) * LOG2E
    scores = []
    for key, _, allowed in blocks:
        part = mm(query, key, ((1,), (1,))) * factor
        scores.append(part if allowed is None else jnp.where(allowed, part, -1e30))
    tops = [jnp.max(part, axis=-1, keepdims=True) for part in scores]
    top = functools.reduce(jnp.maximum, tops)
    result, total = 0.0, 0.0
    for part, (_, value, _) in zip(scores, blocks):
        weight = jnp.exp2(part - top)
        total = total + jnp.sum(weight, axis=-1, keepdims=True)
        result = result + mm(weight.astype(BF16), value)
    return result, top, total


def halves(rows):
    return [slice(index * rows // 2, (index + 1) * rows // 2) for index in range(2)]


def earlier_blocks(ref, index, lane):
    rows = ref.shape[1]
    row = lax.broadcasted_iota(jnp.int32, (rows // 2, rows // 2), 0)
    col = lax.broadcasted_iota(jnp.int32, (rows // 2, rows // 2), 1)
    blocks = [(ref[0, halves(rows)[index], lane], ref[1, halves(rows)[index], lane], col > row)]
    if index == 0:
        blocks.append((ref[0, halves(rows)[1], lane], ref[1, halves(rows)[1], lane], None))
    return blocks


def attend_chip(query, kv, beside_near, beside_far, size):
    rows = query.shape[1]
    heads = query.shape[2] // size
    row = (rows // 2, rows // 2)

    def body(q_ref, kv_ref, near_ref, far_ref, out_ref, stats_ref):
        place = lax.axis_index("tok")
        odd = place % 2 == 1
        causal = lax.broadcasted_iota(jnp.int32, row, 1) <= lax.broadcasted_iota(jnp.int32, row, 0)

        def one(index, where, head, earlier):
            lane = slice(head * size, (head + 1) * size)
            blocks = [
                (kv_ref[0, keys, lane], kv_ref[1, keys, lane], causal if at == index else None)
                for at, keys in enumerate(halves(rows)[: index + 1])
            ]
            if earlier is not None:
                half, at = divmod(head, heads // 2)
                ref = (far_ref, near_ref)[half]
                blocks += earlier_blocks(ref, index, slice(at * size, (at + 1) * size))
            return lane, attend_blocks(q_ref[0, where, lane], blocks)

        @pl.when(odd)
        def _():
            for index, where in enumerate(halves(rows)):
                for head in range(heads):
                    lane, (result, _, total) = one(index, where, head, True)
                    out_ref[where, lane] = result / total

        @pl.when(jnp.logical_not(odd))
        def _():
            for index, where in enumerate(halves(rows)):
                for head in range(heads):
                    lane, (result, top, total) = one(index, where, head, None)
                    out_ref[where, lane] = result / jnp.where(place == 0, total, 1.0)
                    stats_ref[0, where, lane] = jnp.broadcast_to(top, result.shape)
                    stats_ref[1, where, lane] = jnp.broadcast_to(total, result.shape)

    return call(
        body,
        [WHOLE] * 4,
        [WHOLE] * 2,
        [
            jax.ShapeDtypeStruct((rows, heads * size), F32),
            jax.ShapeDtypeStruct((2, rows, heads * size), F32),
        ],
        cost=cost(3 * heads * size * rows * rows, 8 * rows * heads * size, heads * rows * rows),
    )(query, kv, beside_near, beside_far)


def attend_behind(summed, stats, query, behind, size):
    rows = query.shape[1]
    heads = query.shape[2] // size

    def body(sum_ref, stats_ref, q_ref, behind_ref, out_ref):
        place = lax.axis_index("tok")

        @pl.when((place > 0) & (place % 2 == 0))
        def _():
            for index, where in enumerate(halves(rows)):
                for head in range(heads):
                    lane = slice(head * size, (head + 1) * size)
                    result, top, total = attend_blocks(
                        q_ref[0, where, lane], earlier_blocks(behind_ref, index, lane)
                    )
                    before = stats_ref[0, where, lane]
                    both = jnp.maximum(before, top)
                    old, new = jnp.exp2(before - both), jnp.exp2(top - both)
                    total = stats_ref[1, where, lane] * old + total * new
                    out_ref[where, lane] = (sum_ref[where, lane] * old + result * new) / total

    return call(
        body,
        [WHOLE] * 4,
        WHOLE,
        jax.ShapeDtypeStruct(summed.shape, F32),
        cost=cost(3 * heads * size * rows * rows, 8 * rows * heads * size, heads * rows * rows),
        aliases={0: 0},
    )(summed, stats, query, behind)


def fast_apply(query, gate, upper, down):
    qnorm = normed(query)
    gate_pre = mm(qnorm, gate)
    hidden = gate_pre * sigmoid(gate_pre) * mm(qnorm, upper)
    return mm(hidden.astype(BF16), down, ((1,), (1,)))


def combine_near(query, attended, nets):
    rows = query.shape[1]
    heads, _, size, hidden_size = nets.shape

    def body(q_ref, attended_ref, net_ref, out_ref):
        for index in range(heads):
            lane = lanes(first_head(heads) + index, size)
            fast = fast_apply(q_ref[0, :, lane], *(net_ref[index, part] for part in range(3)))
            where = slice(index * size, (index + 1) * size)
            out_ref[:, where] = (attended_ref[:, lane] + fast).astype(BF16)

    return call(
        body,
        [WHOLE] * 3,
        WHOLE,
        jax.ShapeDtypeStruct((rows, heads * size), BF16),
        cost=cost(
            6 * heads * rows * size * hidden_size,
            8 * heads * rows * size,
            heads * rows * hidden_size,
        ),
    )(query, attended, nets)


def partial_out(offsets, query, attended, nets, near, w_out, after=()):
    rows = near.shape[0] // lax.axis_size("head")
    heads, _, size, hidden_size = nets.shape
    depth = heads * size
    count = len(offsets)
    width = w_out.shape[1]
    block = width // 8

    def body(q_ref, attended_ref, net_ref, near_ref, w_ref, *refs):
        out_refs, far_ref = refs[len(after) : -1], refs[-1]
        starts = [pl.multiple_of(ring_index(offset) * rows, rows) for offset in offsets]

        def take(ref, lane):
            return jnp.concatenate([ref[pl.ds(start, rows), lane] for start in starts], axis=0)

        for index in range(heads):
            lane = lanes(first_head(heads, True) + index, size)
            fast = fast_apply(
                take(q_ref.at[0], lane), *(net_ref[index, part] for part in range(3))
            )
            where = slice(index * size, (index + 1) * size)
            far_ref[:, where] = (take(attended_ref, lane) + fast).astype(BF16)
        left = take(near_ref, slice(None))
        near_rows = pl.ds(pl.multiple_of(first_head(heads) * size, depth), depth)
        far_rows = pl.ds(pl.multiple_of(first_head(heads, True) * size, depth), depth)
        for column in range(0, width, block):
            result = mm(left, w_ref[near_rows, column : column + block])
            result += mm(far_ref[...], w_ref[far_rows, column : column + block])
            result = result.astype(BF16)
            half, at = divmod(column, width // 2)
            for index in range(count):
                out_refs[2 * index + half][:, at : at + block] = result[
                    index * rows : (index + 1) * rows
                ]

    outs = call(
        body,
        [WHOLE] * 5 + [AFTER] * len(after),
        [WHOLE] * (2 * count),
        [jax.ShapeDtypeStruct((rows, width // 2), BF16)] * (2 * count),
        [pltpu.VMEM((count * rows, depth), BF16)],
        vmem=8,
        cost=cost(4 * count * rows * depth * width, 2 * width * (2 * depth + count * rows)),
    )(query, attended, nets, near, w_out, *after)
    return {offset: tuple(outs[2 * at : 2 * at + 2]) for at, offset in enumerate(offsets)}


def ring_reduce(query, attended, nets, near, w_out):
    steps = lax.axis_size("head") // 2
    signed = [sign * step for step in range(steps - 1, 0, -1) for sign in (1, -1)]
    shared = (query, attended, nets, near, w_out)
    parts = partial_out([steps], *shared) | partial_out(signed[:2], *shared)
    coming = {}
    ordered = ()
    for which in range(2 * steps - 1):
        step, half = steps - (which + 1) // 2, which % 2
        if which == 2:
            parts |= partial_out(signed[2:] + [0], *shared, tuple(coming.values())[:2])
        terms = []
        for way in (1, -1):
            side = half if way == 1 else 1 - half
            term = parts[steps if step == steps else way * step][side]
            if (way, side) in coming:
                term = (term.astype(F32) + coming[way, side].astype(F32)).astype(BF16)
            terms.append(term)
        ordered = lax.optimization_barrier((*terms, *ordered))[:2]
        for way, term in zip((1, -1), ordered):
            coming[way, half if way == 1 else 1 - half] = ring_send(term, way)
    sides = {1: 1 - half, -1: half}
    totals = add_pair(
        [parts[0][sides[way]] for way in (1, -1)], [coming.pop((way, sides[way])) for way in (1, -1)]
    )
    totals = {sides[way]: total for way, total in zip((1, -1), totals)}
    ends = [totals[side] for side in range(2)]
    for (_, side), more in coming.items():
        ends[side] = ends[side] + more.astype(F32)
    return jnp.concatenate([end.astype(BF16) for end in ends], axis=1)


def add_pair(own, came):
    def body(*refs):
        for index in range(2):
            refs[4 + index][...] = refs[index][...].astype(F32) + refs[2 + index][...].astype(F32)

    return call(
        body,
        [WHOLE] * 4,
        [WHOLE] * 2,
        [jax.ShapeDtypeStruct(value.shape, F32) for value in own],
        cost=cost(0, 64 * own[0].size),
    )(*own, *came)


def swap(value, bit):
    count = lax.axis_size("tok")
    return lax.ppermute(value, "tok", [(index, index ^ bit) for index in range(count)])


def shards(
    tokens, w_query, w_key, w_value, w_out, fast_gate, fast_up, fast_down, token_rate, head_step
):
    local_heads, head_size, _ = fast_gate.shape
    tok_count = lax.axis_size("tok")
    steps = lax.axis_size("head") // 2
    nets = (fast_gate, fast_up, fast_down)
    rate = token_rate.T
    rate_beside = swap(rate, 1)

    own = split_rows(tokens)
    weights = load([w_key, w_value, w_query])
    chunks = [[piece] for piece in own]
    held = [{1: piece, -1: piece} for piece in own]
    sums, done = None, 0
    for step in range(1, steps + 1):
        after = (None, None, weights[0], (sums, rate_beside))[step] if step < 4 else sums
        for c in range(CHUNKS):
            last = (1,) if c % 2 == 0 else (-1,)
            held[c] = gather_step(held[c], (1, -1) if step < steps else last, after)
            chunks[c] += held[c].values()
        if step > 1:
            known = [chunk[: 2 * step - 1] for chunk in chunks]
            (sums,) = accumulate(known, done, 2 * step - 1, weights, sums)
            done = 2 * step - 1
    kv, far, near = accumulate(chunks, done, 2 * steps, weights[:2], sums, shared=True)
    (query,) = accumulate(chunks, done, 2 * steps, weights[2:], sums, 2)

    behind = lax.ppermute(kv, "tok", [(index, index + 1) for index in range(1, tok_count - 1, 2)])
    beside = swap(far, 1)
    beside_far = lax.ppermute(near, "tok", [(index, index + 1) for index in range(0, tok_count, 2)])
    (grads,) = head_grads(kv, rate, *nets)
    grads, travel = head_grads(beside, rate_beside, *nets, grads)
    received = []
    for bit in range(1, tok_count.bit_length() - 1):
        if received:
            travel = grads
            for more in received:
                travel = travel + more.astype(F32)
            travel = travel.astype(BF16)
        received.append(swap(travel, 1 << bit))
    summed, stats = attend_chip(query, kv, beside, beside_far, head_size)
    attended = attend_behind(summed, stats, query, behind, head_size)
    mine = renew(grads, received, head_step, *nets, (attended,))
    near = combine_near(query, attended, mine)
    return ring_reduce(query, attended, swap(mine, 1), near, w_out)


def solution(mesh):
    placed = (
        P("tok", "head"),
        P(None, "head"),
        P(None, "head"),
        P(None, "head"),
        P("head", None),
        P("head", None, None),
        P("head", None, None),
        P("head", None, None),
        P("tok", "head"),
        P("head"),
    )
    return jax.shard_map(
        shards, mesh=mesh, in_specs=placed, out_specs=P(("tok", "head"), None), check_vma=False
    )
```

```python
import functools

import jax
import jax.numpy as jnp
from jax import lax
from jax.experimental import pallas as pl
from jax.experimental.pallas import tpu as pltpu
from jax.sharding import PartitionSpec as P

WINDOW = 512
CHUNKS = 2
F32 = jnp.float32
BF16 = jnp.bfloat16
LOG2E = 1.4426950408889634


def call(body, in_specs, out_specs, out_shape, scratch=(), vmem=8, cost=None, aliases=None):
    return pl.pallas_call(
        body,
        in_specs=in_specs,
        out_specs=out_specs,
        out_shape=out_shape,
        scratch_shapes=list(scratch),
        input_output_aliases=aliases or {},
        cost_estimate=cost,
        compiler_params=pltpu.CompilerParams(vmem_limit_bytes=vmem * 1024 * 1024),
    )


def cost(flops, moved, exps=0):
    return pl.CostEstimate(flops=int(flops), bytes_accessed=int(moved), transcendentals=int(exps))


WHOLE = pl.BlockSpec(memory_space=pltpu.VMEM)
AFTER = pl.BlockSpec(memory_space=pl.ANY)
SCALARS = pl.BlockSpec(memory_space=pltpu.SMEM)
IN_HBM = pl.BlockSpec(memory_space=pltpu.HBM)


def mm(left, right, dims=((1,), (0,))):
    return lax.dot_general(left, right, (dims, ((), ())), preferred_element_type=F32)


def sigmoid(x):
    return 0.5 * jnp.tanh(0.5 * x) + 0.5


def ring_order(count):
    return list(range(0, count, 2)) + list(range(count - 1, 0, -2))


def ring_send(value, step):
    order = ring_order(lax.axis_size("head"))
    count = len(order)
    return lax.ppermute(
        value, "head", [(order[i], order[(i + step) % count]) for i in range(count)]
    )


def ring_offsets():
    steps = lax.axis_size("head") // 2
    return [0] + [way * step for step in range(1, steps) for way in (-1, 1)] + [steps]


def ring_index(offset):
    count = lax.axis_size("head")
    me = lax.axis_index("head")
    at = lax.rem(jnp.where(me % 2 == 0, me // 2, count - 1 - me // 2) + offset + count, count)
    return jnp.where(at < count // 2, 2 * at, 2 * (count - 1 - at) + 1)


def first_head(heads, other=False):
    side = lax.axis_index("tok") % 2
    return (1 - side if other else side) * heads


def hbm(array):
    return pltpu.with_memory_space_constraint(array, pltpu.HBM)


def run_copies(copies):
    for copy in copies:
        copy.start()
    for copy in copies:
        copy.wait()


def load(arrays):
    count = len(arrays)
    blocks = len(ring_offsets())
    size = arrays[0].shape[0] // blocks

    def body(*refs):
        out_refs, sems = refs[count:-1], refs[-1]
        starts = [pl.multiple_of(ring_index(offset) * size, size) for offset in ring_offsets()]
        run_copies(
            [
                pltpu.make_async_copy(
                    refs[index].at[pl.ds(starts[block], size)],
                    out_refs[index].at[pl.ds(block * size, size)],
                    sems.at[index, block],
                )
                for block in range(blocks)
                for index in range(count)
            ]
        )

    return call(
        body,
        [IN_HBM] * count,
        [WHOLE] * count,
        [jax.ShapeDtypeStruct(array.shape, array.dtype) for array in arrays],
        [pltpu.SemaphoreType.DMA((count, blocks))],
        vmem=1,
        cost=cost(0, sum(4 * array.size for array in arrays)),
    )(*[hbm(array) for array in arrays])


def split_rows(tokens):
    rows, width = tokens.shape[0] // CHUNKS, tokens.shape[1]

    def body(in_ref, *refs):
        out_refs, sems = refs[:-1], refs[-1]
        run_copies(
            [
                pltpu.make_async_copy(in_ref.at[pl.ds(c * rows, rows)], out_refs[c], sems.at[c])
                for c in range(CHUNKS)
            ]
        )

    return call(
        body,
        [IN_HBM],
        [WHOLE] * CHUNKS,
        [jax.ShapeDtypeStruct((rows, width), tokens.dtype)] * CHUNKS,
        [pltpu.SemaphoreType.DMA((CHUNKS,))],
        vmem=1,
        cost=cost(0, 4 * tokens.size),
    )(hbm(tokens))


def gather_step(held, ways, after):
    moved = {}
    for way in ways:
        value = held[way]
        if after is not None:
            value, _ = lax.optimization_barrier((value, after))
        moved[way] = ring_send(value, way)
    return moved


def accumulate(chunks, first, last, weights, before=None, lead=0, shared=False):
    rows, depth = chunks[0][0].shape
    width = weights[0].shape[1]
    parts, span = len(weights), last - first
    total = rows * len(chunks)
    final = last == lax.axis_size("head")
    dtype = BF16 if final else F32
    pieces = [chunk[index] for chunk in chunks for index in range(first, last)]

    def body(*refs):
        piece_refs = refs[: len(pieces)]
        weight_refs = refs[len(pieces) : len(pieces) + parts]
        out_ref, left = refs[-2 - 2 * shared], refs[-1]
        for index, ref in enumerate(piece_refs):
            chunk, piece = divmod(index, span)
            left[chunk * rows : (chunk + 1) * rows, piece * depth : (piece + 1) * depth] = ref[...]
        for part in range(parts):
            term = mm(left[...], weight_refs[part][first * depth : last * depth])
            if before is not None:
                term = term + refs[len(args) - 1][lead + part]
            out_ref[part] = term.astype(dtype)
            if shared:
                side = lax.axis_index("tok") % 2
                refs[-3][part] = out_ref[part, :, lanes(1 - side, width // 2)]
                refs[-2][part] = out_ref[part, :, lanes(side, width // 2)]

    aliased = before is not None and not final
    args = [*pieces, *weights] + ([] if before is None else [before])
    return call(
        body,
        [WHOLE] * len(args),
        [WHOLE] * (1 + 2 * shared),
        [
            jax.ShapeDtypeStruct((parts, total, size), dtype)
            for size in (width, width // 2, width // 2)[: 1 + 2 * shared]
        ],
        [pltpu.VMEM((total, span * depth), BF16)],
        vmem=12,
        cost=cost(
            2 * total * span * depth * width * parts,
            2 * span * depth * (total + width * parts) + 8 * total * width * parts,
        ),
        aliases={len(args) - 1: 0} if aliased else None,
    )(*args)


def lanes(head, size):
    return pl.ds(pl.multiple_of(head * size, size), size)


def normed(values):
    values = values.astype(F32)
    scale = lax.rsqrt(jnp.mean(values * values, axis=-1, keepdims=True) + 1e-06)
    return (values * scale).astype(BF16)


def head_grads(kv, rate, fast_gate, fast_up, fast_down, before=None):
    rows = kv.shape[1]
    size, hidden_size = fast_gate.shape[1:]
    count = rate.shape[0]
    heads = count // 2
    whole = kv.shape[2] == count * size

    def body(kv_ref, rate_ref, gate_ref, up_ref, down_ref, *rest):
        rates = rate_ref[...].T
        column = lax.broadcasted_iota(jnp.int32, (rows, count), 1)
        for index in range(heads):
            head = first_head(heads) + index
            mine = jnp.sum(jnp.where(column == head, rates, 0.0), axis=1, keepdims=True)
            lane = lanes(head if whole else index, size)
            knorm = normed(kv_ref[0, :, lane])
            target = (-mine * kv_ref[1, :, lane].astype(F32)).astype(BF16)
            gate_pre = mm(knorm, gate_ref[head].astype(BF16))
            up_pre = mm(knorm, up_ref[head].astype(BF16))
            back = mm(target, down_ref[head].astype(BF16), ((1,), (1,)))
            sigma = sigmoid(gate_pre)
            active = gate_pre * sigma
            first = back * up_pre * (sigma + active * (1.0 - sigma))
            both = jnp.concatenate([first.astype(BF16), (back * active).astype(BF16)], axis=1)
            third = (active * up_pre).astype(BF16)
            pair = mm(knorm, both, ((0,), (0,)))
            terms = (pair[:, :hidden_size], pair[:, hidden_size:], mm(target, third, ((0,), (0,))))
            for part, term in enumerate(terms):
                if before is not None:
                    term = term + rest[0][index, part]
                    rest[-1][index, part] = term.astype(BF16)
                    rest[-2][index, part] = term
                else:
                    rest[-1][index, part] = term

    args = [kv, rate, fast_gate, fast_up, fast_down] + ([] if before is None else [before])
    kinds = [F32] if before is None else [F32, BF16]
    return call(
        body,
        [WHOLE] * len(args),
        [WHOLE] * len(kinds),
        [jax.ShapeDtypeStruct((heads, 3, size, hidden_size), kind) for kind in kinds],
        cost=cost(
            12 * heads * rows * size * hidden_size,
            8 * heads * 3 * size * hidden_size,
            heads * rows * hidden_size,
        ),
    )(*args)


def renew(kept, received, step, fast_gate, fast_up, fast_down, after):
    heads, _, size, hidden_size = kept.shape

    def body(step_ref, kept_ref, gate_ref, up_ref, down_ref, *rest):
        out_ref = rest[-1]
        for index in range(heads):
            head = first_head(heads) + index
            for part in range(3):
                grad = kept_ref[index, part]
                for more in rest[: len(received)]:
                    grad = grad + more[index, part].astype(F32)
                if part < 2:
                    matrix = (gate_ref, up_ref)[part][head]
                    fan = size
                else:
                    matrix = down_ref[head].T
                    fan = hidden_size
                mean_sq = jnp.sum(grad * grad, keepdims=True) / (size * hidden_size)
                scale = step_ref[head] * fan ** (-0.5) * lax.rsqrt(mean_sq + 1e-06)
                out_ref[index, part] = (matrix - scale * grad).astype(BF16)

    return call(
        body,
        [SCALARS] + [WHOLE] * (4 + len(received)) + [AFTER] * len(after),
        WHOLE,
        jax.ShapeDtypeStruct(kept.shape, BF16),
        cost=cost(10 * kept.size, 12 * kept.size),
    )(step, kept, fast_gate, fast_up, fast_down, *received, *after)


def attend_blocks(query, blocks):
    factor = query.shape[-1] ** (-0.5) * LOG2E
    scores = []
    for key, _, allowed in blocks:
        part = mm(query, key, ((1,), (1,))) * factor
        scores.append(part if allowed is None else jnp.where(allowed, part, -1e30))
    tops = [jnp.max(part, axis=-1, keepdims=True) for part in scores]
    top = functools.reduce(jnp.maximum, tops)
    result, total = 0.0, 0.0
    for part, (_, value, _) in zip(scores, blocks):
        weight = jnp.exp2(part - top)
        total = total + jnp.sum(weight, axis=-1, keepdims=True)
        result = result + mm(weight.astype(BF16), value)
    return result, top, total


def halves(rows):
    return [slice(index * rows // 2, (index + 1) * rows // 2) for index in range(2)]


def earlier_blocks(ref, index, lane):
    rows = ref.shape[1]
    row = lax.broadcasted_iota(jnp.int32, (rows // 2, rows // 2), 0)
    col = lax.broadcasted_iota(jnp.int32, (rows // 2, rows // 2), 1)
    blocks = [(ref[0, halves(rows)[index], lane], ref[1, halves(rows)[index], lane], col > row)]
    if index == 0:
        blocks.append((ref[0, halves(rows)[1], lane], ref[1, halves(rows)[1], lane], None))
    return blocks


def attend_own(query, kv, size):
    rows = query.shape[1]
    heads = query.shape[2] // size
    row = (rows // 2, rows // 2)

    def body(q_ref, kv_ref, out_ref, stats_ref):
        alone = lax.axis_index("tok") == 0
        causal = lax.broadcasted_iota(jnp.int32, row, 1) <= lax.broadcasted_iota(jnp.int32, row, 0)
        for index, where in enumerate(halves(rows)):
            for head in range(heads):
                lane = slice(head * size, (head + 1) * size)
                blocks = [
                    (kv_ref[0, keys, lane], kv_ref[1, keys, lane], causal if at == index else None)
                    for at, keys in enumerate(halves(rows)[: index + 1])
                ]
                result, top, total = attend_blocks(q_ref[0, where, lane], blocks)
                out_ref[where, lane] = result / jnp.where(alone, total, 1.0)
                stats_ref[0, where, lane] = jnp.broadcast_to(top, result.shape)
                stats_ref[1, where, lane] = jnp.broadcast_to(total, result.shape)

    return call(
        body,
        [WHOLE] * 2,
        [WHOLE] * 2,
        [
            jax.ShapeDtypeStruct((rows, heads * size), F32),
            jax.ShapeDtypeStruct((2, rows, heads * size), F32),
        ],
        cost=cost(3 * heads * size * rows * rows, 8 * rows * heads * size, heads * rows * rows),
    )(query, kv)


def attend_earlier(summed, stats, query, sources, other, size, after=()):
    rows = query.shape[1]
    heads = sources[0].shape[2] // size

    def body(sum_ref, stats_ref, q_ref, *refs):
        out_ref = refs[-1]
        place = lax.axis_index("tok")

        def add(ref):
            for index, where in enumerate(halves(rows)):
                for at in range(heads):
                    lane = lanes(first_head(heads, other) + at, size)
                    result, top, total = attend_blocks(
                        q_ref[0, where, lane],
                        earlier_blocks(ref, index, slice(at * size, (at + 1) * size)),
                    )
                    before = stats_ref[0, where, lane]
                    both = jnp.maximum(before, top)
                    old, new = jnp.exp2(before - both), jnp.exp2(top - both)
                    total = stats_ref[1, where, lane] * old + total * new
                    out_ref[where, lane] = (sum_ref[where, lane] * old + result * new) / total

        if len(sources) == 1:
            pl.when(place > 0)(lambda: add(refs[0]))
        else:
            pl.when((place > 0) & (place % 2 == 0))(lambda: add(refs[0]))
            pl.when(place % 2 == 1)(lambda: add(refs[1]))

    return call(
        body,
        [WHOLE] * (3 + len(sources)) + [AFTER] * len(after),
        WHOLE,
        jax.ShapeDtypeStruct(summed.shape, F32),
        cost=cost(3 * heads * size * rows * rows, 8 * rows * heads * size, heads * rows * rows),
        aliases={0: 0},
    )(summed, stats, query, *sources, *after)


def fast_apply(query, gate, upper, down):
    qnorm = normed(query)
    gate_pre = mm(qnorm, gate)
    hidden = gate_pre * sigmoid(gate_pre) * mm(qnorm, upper)
    return mm(hidden.astype(BF16), down, ((1,), (1,)))


def combine_near(query, attended, nets):
    rows = query.shape[1]
    heads, _, size, hidden_size = nets.shape

    def body(q_ref, attended_ref, net_ref, out_ref):
        for index in range(heads):
            lane = lanes(first_head(heads) + index, size)
            fast = fast_apply(q_ref[0, :, lane], *(net_ref[index, part] for part in range(3)))
            where = slice(index * size, (index + 1) * size)
            out_ref[:, where] = (attended_ref[:, lane] + fast).astype(BF16)

    return call(
        body,
        [WHOLE] * 3,
        WHOLE,
        jax.ShapeDtypeStruct((rows, heads * size), BF16),
        cost=cost(
            6 * heads * rows * size * hidden_size,
            8 * heads * rows * size,
            heads * rows * hidden_size,
        ),
    )(query, attended, nets)


def partial_out(offsets, query, attended, nets, near, w_out, after=()):
    rows = near.shape[0] // lax.axis_size("head")
    heads, _, size, hidden_size = nets.shape
    depth = heads * size
    count = len(offsets)
    width = w_out.shape[1]
    block = width // 8

    def body(q_ref, attended_ref, net_ref, near_ref, w_ref, *refs):
        out_refs, far_ref = refs[len(after) : -1], refs[-1]
        starts = [pl.multiple_of(ring_index(offset) * rows, rows) for offset in offsets]

        def take(ref, lane):
            return jnp.concatenate([ref[pl.ds(start, rows), lane] for start in starts], axis=0)

        for index in range(heads):
            lane = lanes(first_head(heads, True) + index, size)
            fast = fast_apply(
                take(q_ref.at[0], lane), *(net_ref[index, part] for part in range(3))
            )
            where = slice(index * size, (index + 1) * size)
            far_ref[:, where] = (take(attended_ref, lane) + fast).astype(BF16)
        left = take(near_ref, slice(None))
        near_rows = pl.ds(pl.multiple_of(first_head(heads) * size, depth), depth)
        far_rows = pl.ds(pl.multiple_of(first_head(heads, True) * size, depth), depth)
        for column in range(0, width, block):
            result = mm(left, w_ref[near_rows, column : column + block])
            result += mm(far_ref[...], w_ref[far_rows, column : column + block])
            result = result.astype(BF16)
            half, at = divmod(column, width // 2)
            for index in range(count):
                out_refs[2 * index + half][:, at : at + block] = result[
                    index * rows : (index + 1) * rows
                ]

    outs = call(
        body,
        [WHOLE] * 5 + [AFTER] * len(after),
        [WHOLE] * (2 * count),
        [jax.ShapeDtypeStruct((rows, width // 2), BF16)] * (2 * count),
        [pltpu.VMEM((count * rows, depth), BF16)],
        vmem=8,
        cost=cost(4 * count * rows * depth * width, 2 * width * (2 * depth + count * rows)),
    )(query, attended, nets, near, w_out, *after)
    return {offset: tuple(outs[2 * at : 2 * at + 2]) for at, offset in enumerate(offsets)}


def ring_reduce(query, attended, nets, near, w_out):
    steps = lax.axis_size("head") // 2
    signed = [sign * step for step in range(steps - 1, 0, -1) for sign in (1, -1)]
    shared = (query, attended, nets, near, w_out)
    parts = partial_out([steps], *shared) | partial_out(signed[:2], *shared)
    coming = {}
    ordered = ()
    for which in range(2 * steps - 1):
        step, half = steps - (which + 1) // 2, which % 2
        if which == 2:
            parts |= partial_out(signed[2:] + [0], *shared, tuple(coming.values())[:2])
        terms = []
        for way in (1, -1):
            side = half if way == 1 else 1 - half
            term = parts[steps if step == steps else way * step][side]
            if (way, side) in coming:
                term = (term.astype(F32) + coming[way, side].astype(F32)).astype(BF16)
            terms.append(term)
        ordered = lax.optimization_barrier((*terms, *ordered))[:2]
        for way, term in zip((1, -1), ordered):
            coming[way, half if way == 1 else 1 - half] = ring_send(term, way)
    sides = {1: 1 - half, -1: half}
    totals = add_pair(
        [parts[0][sides[way]] for way in (1, -1)], [coming.pop((way, sides[way])) for way in (1, -1)]
    )
    totals = {sides[way]: total for way, total in zip((1, -1), totals)}
    ends = [totals[side] for side in range(2)]
    for (_, side), more in coming.items():
        ends[side] = ends[side] + more.astype(F32)
    return jnp.concatenate([end.astype(BF16) for end in ends], axis=1)


def add_pair(own, came):
    def body(*refs):
        for index in range(2):
            refs[4 + index][...] = refs[index][...].astype(F32) + refs[2 + index][...].astype(F32)

    return call(
        body,
        [WHOLE] * 4,
        [WHOLE] * 2,
        [jax.ShapeDtypeStruct(value.shape, F32) for value in own],
        cost=cost(0, 64 * own[0].size),
    )(*own, *came)


def swap(value, bit):
    count = lax.axis_size("tok")
    return lax.ppermute(value, "tok", [(index, index ^ bit) for index in range(count)])


def shards(
    tokens, w_query, w_key, w_value, w_out, fast_gate, fast_up, fast_down, token_rate, head_step
):
    local_heads, head_size, _ = fast_gate.shape
    tok_count = lax.axis_size("tok")
    steps = lax.axis_size("head") // 2
    nets = (fast_gate, fast_up, fast_down)
    rate = token_rate.T
    rate_beside = swap(rate, 1)

    own = split_rows(tokens)
    weights = load([w_key, w_value, w_query])
    chunks = [[piece] for piece in own]
    held = [{1: piece, -1: piece} for piece in own]
    sums, done = None, 0
    for step in range(1, steps + 1):
        after = {2: weights[0], 3: (sums, rate_beside)}.get(step)
        for c in range(CHUNKS):
            last = (1,) if c % 2 == 0 else (-1,)
            held[c] = gather_step(held[c], (1, -1) if step < steps else last, after)
            chunks[c] += held[c].values()
        if step > 1:
            known = [chunk[: 2 * step - 1] for chunk in chunks]
            (sums,) = accumulate(known, done, 2 * step - 1, weights, sums)
            done = 2 * step - 1
    kv, far, near = accumulate(chunks, done, 2 * steps, weights[:2], sums, shared=True)
    (query,) = accumulate(chunks, done, 2 * steps, weights[2:], sums, 2)

    behind = lax.ppermute(far, "tok", [(index, index + 1) for index in range(1, tok_count - 1, 2)])
    beside = swap(far, 1)
    (grads,) = head_grads(kv, rate, *nets)
    grads, travel = head_grads(beside, rate_beside, *nets, grads)
    received = []
    for bit in range(1, tok_count.bit_length() - 1):
        if received:
            travel = grads
            for more in received:
                travel = travel + more.astype(F32)
            travel = travel.astype(BF16)
        received.append(swap(travel, 1 << bit))
    attended, stats = attend_own(query, kv, head_size)
    near, _ = lax.optimization_barrier((near, attended))
    behind_far = lax.ppermute(near, "tok", [(index, index + 1) for index in range(tok_count - 1)])
    attended = attend_earlier(attended, stats, query, (behind, beside), False, head_size)
    mine = renew(grads, received, head_step, *nets, (attended,))
    near = combine_near(query, attended, mine)
    attended = attend_earlier(attended, stats, query, (behind_far,), True, head_size, (near,))
    return ring_reduce(query, attended, swap(mine, 1), near, w_out)


def solution(mesh):
    placed = (
        P("tok", "head"),
        P(None, "head"),
        P(None, "head"),
        P(None, "head"),
        P("head", None),
        P("head", None, None),
        P("head", None, None),
        P("head", None, None),
        P("tok", "head"),
        P("head"),
    )
    return jax.shard_map(
        shards, mesh=mesh, in_specs=placed, out_specs=P(("tok", "head"), None), check_vma=False
    )
```

```python
import functools

import jax
import jax.numpy as jnp
from jax import lax
from jax.experimental import pallas as pl
from jax.experimental.pallas import tpu as pltpu
from jax.sharding import PartitionSpec as P

WINDOW = 512
CHUNKS = 2
F32 = jnp.float32
BF16 = jnp.bfloat16
LOG2E = 1.4426950408889634


def call(body, in_specs, out_specs, out_shape, scratch=(), vmem=8, cost=None, aliases=None):
    return pl.pallas_call(
        body,
        in_specs=in_specs,
        out_specs=out_specs,
        out_shape=out_shape,
        scratch_shapes=list(scratch),
        input_output_aliases=aliases or {},
        cost_estimate=cost,
        compiler_params=pltpu.CompilerParams(vmem_limit_bytes=vmem * 1024 * 1024),
    )


def cost(flops, moved, exps=0):
    return pl.CostEstimate(flops=int(flops), bytes_accessed=int(moved), transcendentals=int(exps))


WHOLE = pl.BlockSpec(memory_space=pltpu.VMEM)
AFTER = pl.BlockSpec(memory_space=pl.ANY)
SCALARS = pl.BlockSpec(memory_space=pltpu.SMEM)
IN_HBM = pl.BlockSpec(memory_space=pltpu.HBM)


def mm(left, right, dims=((1,), (0,))):
    return lax.dot_general(left, right, (dims, ((), ())), preferred_element_type=F32)


def sigmoid(x):
    return 0.5 * jnp.tanh(0.5 * x) + 0.5


def ring_order(count):
    return list(range(0, count, 2)) + list(range(count - 1, 0, -2))


def ring_send(value, step):
    order = ring_order(lax.axis_size("head"))
    count = len(order)
    return lax.ppermute(
        value, "head", [(order[i], order[(i + step) % count]) for i in range(count)]
    )


def ring_offsets():
    steps = lax.axis_size("head") // 2
    return [0] + [way * step for step in range(1, steps) for way in (-1, 1)] + [steps]


def ring_index(offset):
    count = lax.axis_size("head")
    me = lax.axis_index("head")
    at = lax.rem(jnp.where(me % 2 == 0, me // 2, count - 1 - me // 2) + offset + count, count)
    return jnp.where(at < count // 2, 2 * at, 2 * (count - 1 - at) + 1)


def first_head(heads, other=False):
    side = lax.axis_index("tok") % 2
    return (1 - side if other else side) * heads


def hbm(array):
    return pltpu.with_memory_space_constraint(array, pltpu.HBM)


def run_copies(copies):
    for copy in copies:
        copy.start()
    for copy in copies:
        copy.wait()


def load(arrays):
    count = len(arrays)
    blocks = len(ring_offsets())
    size = arrays[0].shape[0] // blocks

    def body(*refs):
        out_refs, sems = refs[count:-1], refs[-1]
        starts = [pl.multiple_of(ring_index(offset) * size, size) for offset in ring_offsets()]
        run_copies(
            [
                pltpu.make_async_copy(
                    refs[index].at[pl.ds(starts[block], size)],
                    out_refs[index].at[pl.ds(block * size, size)],
                    sems.at[index, block],
                )
                for block in range(blocks)
                for index in range(count)
            ]
        )

    return call(
        body,
        [IN_HBM] * count,
        [WHOLE] * count,
        [jax.ShapeDtypeStruct(array.shape, array.dtype) for array in arrays],
        [pltpu.SemaphoreType.DMA((count, blocks))],
        vmem=1,
        cost=cost(0, sum(4 * array.size for array in arrays)),
    )(*[hbm(array) for array in arrays])


def split_rows(tokens):
    rows, width = tokens.shape[0] // CHUNKS, tokens.shape[1]

    def body(in_ref, *refs):
        out_refs, sems = refs[:-1], refs[-1]
        run_copies(
            [
                pltpu.make_async_copy(in_ref.at[pl.ds(c * rows, rows)], out_refs[c], sems.at[c])
                for c in range(CHUNKS)
            ]
        )

    return call(
        body,
        [IN_HBM],
        [WHOLE] * CHUNKS,
        [jax.ShapeDtypeStruct((rows, width), tokens.dtype)] * CHUNKS,
        [pltpu.SemaphoreType.DMA((CHUNKS,))],
        vmem=1,
        cost=cost(0, 4 * tokens.size),
    )(hbm(tokens))


def gather_step(held, ways, after):
    moved = {}
    for way in ways:
        value = held[way]
        if after is not None:
            value, _ = lax.optimization_barrier((value, after))
        moved[way] = ring_send(value, way)
    return moved


def accumulate(chunks, first, last, weights, before=None, lead=0, shared=False):
    rows, depth = chunks[0][0].shape
    width = weights[0].shape[1]
    parts, span = len(weights), last - first
    total = rows * len(chunks)
    final = last == lax.axis_size("head")
    dtype = BF16 if final else F32
    pieces = [chunk[index] for chunk in chunks for index in range(first, last)]

    def body(*refs):
        piece_refs = refs[: len(pieces)]
        weight_refs = refs[len(pieces) : len(pieces) + parts]
        out_ref, left = refs[-2 - 4 * shared], refs[-1]
        for index, ref in enumerate(piece_refs):
            chunk, piece = divmod(index, span)
            left[chunk * rows : (chunk + 1) * rows, piece * depth : (piece + 1) * depth] = ref[...]
        for part in range(parts):
            term = mm(left[...], weight_refs[part][first * depth : last * depth])
            if before is not None:
                term = term + refs[len(args) - 1][lead + part]
            out_ref[part] = term.astype(dtype)
            if shared:
                side = lax.axis_index("tok") % 2
                refs[-5][part] = out_ref[part, :, lanes(1 - side, width // 2)]
                refs[-4][part] = out_ref[part, :, lanes(side, width // 2)]
                refs[-3 + part][0] = refs[-5][part]

    aliased = before is not None and not final
    args = [*pieces, *weights] + ([] if before is None else [before])
    return call(
        body,
        [WHOLE] * len(args),
        [WHOLE] * (1 + 4 * shared),
        [
            jax.ShapeDtypeStruct((count, total, size), dtype)
            for count, size in [(parts, width)] + [(parts, width // 2)] * 2 * shared
            + [(1, width // 2)] * 2 * shared
        ],
        [pltpu.VMEM((total, span * depth), BF16)],
        vmem=12,
        cost=cost(
            2 * total * span * depth * width * parts,
            2 * span * depth * (total + width * parts) + 8 * total * width * parts,
        ),
        aliases={len(args) - 1: 0} if aliased else None,
    )(*args)


def lanes(head, size):
    return pl.ds(pl.multiple_of(head * size, size), size)


def normed(values):
    values = values.astype(F32)
    scale = lax.rsqrt(jnp.mean(values * values, axis=-1, keepdims=True) + 1e-06)
    return (values * scale).astype(BF16)


def head_grads(keys, values, rate, fast_gate, fast_up, fast_down, before=None):
    rows = keys.shape[1]
    size, hidden_size = fast_gate.shape[1:]
    count = rate.shape[0]
    heads = count // 2
    whole = keys.shape[2] == count * size

    def body(key_ref, value_ref, rate_ref, gate_ref, up_ref, down_ref, *rest):
        rates = rate_ref[...].T
        column = lax.broadcasted_iota(jnp.int32, (rows, count), 1)
        for index in range(heads):
            head = first_head(heads) + index
            mine = jnp.sum(jnp.where(column == head, rates, 0.0), axis=1, keepdims=True)
            lane = lanes(head if whole else index, size)
            knorm = normed(key_ref[0, :, lane])
            target = (-mine * value_ref[value_ref.shape[0] - 1, :, lane].astype(F32)).astype(BF16)
            gate_pre = mm(knorm, gate_ref[head].astype(BF16))
            up_pre = mm(knorm, up_ref[head].astype(BF16))
            back = mm(target, down_ref[head].astype(BF16), ((1,), (1,)))
            sigma = sigmoid(gate_pre)
            active = gate_pre * sigma
            first = back * up_pre * (sigma + active * (1.0 - sigma))
            both = jnp.concatenate([first.astype(BF16), (back * active).astype(BF16)], axis=1)
            third = (active * up_pre).astype(BF16)
            pair = mm(knorm, both, ((0,), (0,)))
            terms = (pair[:, :hidden_size], pair[:, hidden_size:], mm(target, third, ((0,), (0,))))
            for part, term in enumerate(terms):
                if before is not None:
                    term = term + rest[0][index, part]
                    rest[-1][index, part] = term.astype(BF16)
                    rest[-2][index, part] = term
                else:
                    rest[-1][index, part] = term

    args = [keys, values, rate, fast_gate, fast_up, fast_down] + ([] if before is None else [before])
    kinds = [F32] if before is None else [F32, BF16]
    return call(
        body,
        [WHOLE] * len(args),
        [WHOLE] * len(kinds),
        [jax.ShapeDtypeStruct((heads, 3, size, hidden_size), kind) for kind in kinds],
        cost=cost(
            12 * heads * rows * size * hidden_size,
            8 * heads * 3 * size * hidden_size,
            heads * rows * hidden_size,
        ),
    )(*args)


def renew(kept, received, step, fast_gate, fast_up, fast_down, after):
    heads, _, size, hidden_size = kept.shape

    def body(step_ref, kept_ref, gate_ref, up_ref, down_ref, *rest):
        out_ref = rest[-1]
        for index in range(heads):
            head = first_head(heads) + index
            for part in range(3):
                grad = kept_ref[index, part]
                for more in rest[: len(received)]:
                    grad = grad + more[index, part].astype(F32)
                if part < 2:
                    matrix = (gate_ref, up_ref)[part][head]
                    fan = size
                else:
                    matrix = down_ref[head].T
                    fan = hidden_size
                mean_sq = jnp.sum(grad * grad, keepdims=True) / (size * hidden_size)
                scale = step_ref[head] * fan ** (-0.5) * lax.rsqrt(mean_sq + 1e-06)
                out_ref[index, part] = (matrix - scale * grad).astype(BF16)

    return call(
        body,
        [SCALARS] + [WHOLE] * (4 + len(received)) + [AFTER] * len(after),
        WHOLE,
        jax.ShapeDtypeStruct(kept.shape, BF16),
        cost=cost(10 * kept.size, 12 * kept.size),
    )(step, kept, fast_gate, fast_up, fast_down, *received, *after)


def attend_blocks(query, blocks):
    factor = query.shape[-1] ** (-0.5) * LOG2E
    scores = []
    for key, _, allowed in blocks:
        part = mm(query, key, ((1,), (1,))) * factor
        scores.append(part if allowed is None else jnp.where(allowed, part, -1e30))
    tops = [jnp.max(part, axis=-1, keepdims=True) for part in scores]
    top = functools.reduce(jnp.maximum, tops)
    result, total = 0.0, 0.0
    for part, (_, value, _) in zip(scores, blocks):
        weight = jnp.exp2(part - top)
        total = total + jnp.sum(weight, axis=-1, keepdims=True)
        result = result + mm(weight.astype(BF16), value)
    return result, top, total


def halves(rows):
    return [slice(index * rows // 2, (index + 1) * rows // 2) for index in range(2)]


def earlier_blocks(keys, values, index, lane):
    rows = keys.shape[1]
    last = values.shape[0] - 1
    row = lax.broadcasted_iota(jnp.int32, (rows // 2, rows // 2), 0)
    col = lax.broadcasted_iota(jnp.int32, (rows // 2, rows // 2), 1)
    blocks = [(keys[0, halves(rows)[index], lane], values[last, halves(rows)[index], lane], col > row)]
    if index == 0:
        blocks.append((keys[0, halves(rows)[1], lane], values[last, halves(rows)[1], lane], None))
    return blocks


def attend_own(query, kv, size, after):
    rows = query.shape[1]
    heads = query.shape[2] // size
    row = (rows // 2, rows // 2)

    def body(q_ref, kv_ref, _, out_ref, stats_ref):
        alone = lax.axis_index("tok") == 0
        causal = lax.broadcasted_iota(jnp.int32, row, 1) <= lax.broadcasted_iota(jnp.int32, row, 0)
        for index, where in enumerate(halves(rows)):
            for head in range(heads):
                lane = slice(head * size, (head + 1) * size)
                blocks = [
                    (kv_ref[0, keys, lane], kv_ref[1, keys, lane], causal if at == index else None)
                    for at, keys in enumerate(halves(rows)[: index + 1])
                ]
                result, top, total = attend_blocks(q_ref[0, where, lane], blocks)
                out_ref[where, lane] = result / jnp.where(alone, total, 1.0)
                stats_ref[0, where, lane] = jnp.broadcast_to(top, result.shape)
                stats_ref[1, where, lane] = jnp.broadcast_to(total, result.shape)

    return call(
        body,
        [WHOLE] * 2 + [AFTER],
        [WHOLE] * 2,
        [
            jax.ShapeDtypeStruct((rows, heads * size), F32),
            jax.ShapeDtypeStruct((2, rows, heads * size), F32),
        ],
        cost=cost(3 * heads * size * rows * rows, 8 * rows * heads * size, heads * rows * rows),
    )(query, kv, after)


def attend_earlier(summed, stats, query, sources, other, size, after=()):
    rows = query.shape[1]
    heads = sources[0][0].shape[2] // size

    def body(sum_ref, stats_ref, q_ref, *refs):
        out_ref = refs[-1]
        place = lax.axis_index("tok")

        def add(keys, values):
            for index, where in enumerate(halves(rows)):
                for at in range(heads):
                    lane = lanes(first_head(heads, other) + at, size)
                    result, top, total = attend_blocks(
                        q_ref[0, where, lane],
                        earlier_blocks(keys, values, index, slice(at * size, (at + 1) * size)),
                    )
                    before = stats_ref[0, where, lane]
                    both = jnp.maximum(before, top)
                    old, new = jnp.exp2(before - both), jnp.exp2(top - both)
                    total = stats_ref[1, where, lane] * old + total * new
                    out_ref[where, lane] = (sum_ref[where, lane] * old + result * new) / total

        if len(sources) == 1:
            pl.when(place > 0)(lambda: add(*refs[:2]))
        else:
            pl.when((place > 0) & (place % 2 == 0))(lambda: add(*refs[:2]))
            pl.when(place % 2 == 1)(lambda: add(*refs[2:4]))

    return call(
        body,
        [WHOLE] * (3 + 2 * len(sources)) + [AFTER] * len(after),
        WHOLE,
        jax.ShapeDtypeStruct(summed.shape, F32),
        cost=cost(3 * heads * size * rows * rows, 8 * rows * heads * size, heads * rows * rows),
        aliases={0: 0},
    )(summed, stats, query, *[ref for pair in sources for ref in pair], *after)


def fast_apply(query, gate, upper, down):
    qnorm = normed(query)
    gate_pre = mm(qnorm, gate)
    hidden = gate_pre * sigmoid(gate_pre) * mm(qnorm, upper)
    return mm(hidden.astype(BF16), down, ((1,), (1,)))


def combine_near(query, attended, nets):
    rows = query.shape[1]
    heads, _, size, hidden_size = nets.shape

    def body(q_ref, attended_ref, net_ref, out_ref):
        for index in range(heads):
            lane = lanes(first_head(heads) + index, size)
            fast = fast_apply(q_ref[0, :, lane], *(net_ref[index, part] for part in range(3)))
            where = slice(index * size, (index + 1) * size)
            out_ref[:, where] = (attended_ref[:, lane] + fast).astype(BF16)

    return call(
        body,
        [WHOLE] * 3,
        WHOLE,
        jax.ShapeDtypeStruct((rows, heads * size), BF16),
        cost=cost(
            6 * heads * rows * size * hidden_size,
            8 * heads * rows * size,
            heads * rows * hidden_size,
        ),
    )(query, attended, nets)


def partial_out(offsets, query, attended, nets, near, w_out, after=()):
    rows = near.shape[0] // lax.axis_size("head")
    heads, _, size, hidden_size = nets.shape
    depth = heads * size
    count = len(offsets)
    width = w_out.shape[1]
    block = width // 8

    def body(q_ref, attended_ref, net_ref, near_ref, w_ref, *refs):
        out_refs, far_ref = refs[len(after) : -1], refs[-1]
        starts = [pl.multiple_of(ring_index(offset) * rows, rows) for offset in offsets]

        def take(ref, lane):
            return jnp.concatenate([ref[pl.ds(start, rows), lane] for start in starts], axis=0)

        for index in range(heads):
            lane = lanes(first_head(heads, True) + index, size)
            fast = fast_apply(
                take(q_ref.at[0], lane), *(net_ref[index, part] for part in range(3))
            )
            where = slice(index * size, (index + 1) * size)
            far_ref[:, where] = (take(attended_ref, lane) + fast).astype(BF16)
        left = take(near_ref, slice(None))
        near_rows = pl.ds(pl.multiple_of(first_head(heads) * size, depth), depth)
        far_rows = pl.ds(pl.multiple_of(first_head(heads, True) * size, depth), depth)
        for column in range(0, width, block):
            result = mm(left, w_ref[near_rows, column : column + block])
            result += mm(far_ref[...], w_ref[far_rows, column : column + block])
            result = result.astype(BF16)
            half, at = divmod(column, width // 2)
            for index in range(count):
                out_refs[2 * index + half][:, at : at + block] = result[
                    index * rows : (index + 1) * rows
                ]

    outs = call(
        body,
        [WHOLE] * 5 + [AFTER] * len(after),
        [WHOLE] * (2 * count),
        [jax.ShapeDtypeStruct((rows, width // 2), BF16)] * (2 * count),
        [pltpu.VMEM((count * rows, depth), BF16)],
        vmem=8,
        cost=cost(4 * count * rows * depth * width, 2 * width * (2 * depth + count * rows)),
    )(query, attended, nets, near, w_out, *after)
    return {offset: tuple(outs[2 * at : 2 * at + 2]) for at, offset in enumerate(offsets)}


def ring_reduce(query, attended, nets, near, w_out):
    steps = lax.axis_size("head") // 2
    signed = [sign * step for step in range(steps - 1, 0, -1) for sign in (1, -1)]
    shared = (query, attended, nets, near, w_out)
    parts = partial_out([steps], *shared) | partial_out(signed[:2], *shared)
    coming = {}
    ordered = ()
    for which in range(2 * steps - 1):
        step, half = steps - (which + 1) // 2, which % 2
        if which % 2 == 0 and 2 <= which <= 2 * (steps - 2):
            later = signed[which : which + 2] + [0] * (which == 2 * (steps - 2))
            parts |= partial_out(later, *shared, tuple(coming.values())[:2])
        terms = []
        for way in (1, -1):
            side = half if way == 1 else 1 - half
            term = parts[steps if step == steps else way * step][side]
            if (way, side) in coming:
                term = (term.astype(F32) + coming[way, side].astype(F32)).astype(BF16)
            terms.append(term)
        ordered = lax.optimization_barrier((*terms, *ordered))[:2]
        for way, term in zip((1, -1), ordered):
            coming[way, half if way == 1 else 1 - half] = ring_send(term, way)
    sides = {1: 1 - half, -1: half}
    totals = add_pair(
        [parts[0][sides[way]] for way in (1, -1)], [coming.pop((way, sides[way])) for way in (1, -1)]
    )
    totals = {sides[way]: total for way, total in zip((1, -1), totals)}
    ends = [totals[side] for side in range(2)]
    for (_, side), more in coming.items():
        ends[side] = ends[side] + more.astype(F32)
    return jnp.concatenate([end.astype(BF16) for end in ends], axis=1)


def add_pair(own, came):
    def body(*refs):
        for index in range(2):
            refs[4 + index][...] = refs[index][...].astype(F32) + refs[2 + index][...].astype(F32)

    return call(
        body,
        [WHOLE] * 4,
        [WHOLE] * 2,
        [jax.ShapeDtypeStruct(value.shape, F32) for value in own],
        cost=cost(0, 64 * own[0].size),
    )(*own, *came)


def swap(value, bit):
    count = lax.axis_size("tok")
    return lax.ppermute(value, "tok", [(index, index ^ bit) for index in range(count)])


def shards(
    tokens, w_query, w_key, w_value, w_out, fast_gate, fast_up, fast_down, token_rate, head_step
):
    local_heads, head_size, _ = fast_gate.shape
    tok_count = lax.axis_size("tok")
    steps = lax.axis_size("head") // 2
    nets = (fast_gate, fast_up, fast_down)
    rate = token_rate.T
    rate_beside = swap(rate, 1)

    own = split_rows(tokens)
    weights = load([w_key, w_value, w_query])
    chunks = [[piece] for piece in own]
    held = [{1: piece, -1: piece} for piece in own]
    sums, done = None, 0
    for step in range(1, steps + 1):
        after = {2: weights[0], 3: (sums, rate_beside)}.get(step)
        for c in range(CHUNKS):
            last = (1,) if c % 2 == 0 else (-1,)
            held[c] = gather_step(held[c], (1, -1) if step < steps else last, after)
            chunks[c] += held[c].values()
        if step > 1:
            known = [chunk[: 2 * step - 1] for chunk in chunks]
            (sums,) = accumulate(known, done, 2 * step - 1, weights, sums)
            done = 2 * step - 1
    kv, far, near, *apart = accumulate(chunks, done, 2 * steps, weights[:2], sums, shared=True)
    (query,) = accumulate(chunks, done, 2 * steps, weights[2:], sums, 2)

    behind = lax.ppermute(far, "tok", [(index, index + 1) for index in range(1, tok_count - 1, 2)])
    beside = [swap(part, 1) for part in apart]
    (grads,) = head_grads(kv, kv, rate, *nets)
    grads, travel = head_grads(*beside, rate_beside, *nets, grads)
    received = []
    for bit in range(1, tok_count.bit_length() - 1):
        if received:
            travel = grads
            for more in received:
                travel = travel + more.astype(F32)
            travel = travel.astype(BF16)
        received.append(swap(travel, 1 << bit))
    attended, stats = attend_own(query, kv, head_size, behind)
    near, _ = lax.optimization_barrier((near, attended))
    behind_far = lax.ppermute(near, "tok", [(index, index + 1) for index in range(tok_count - 1)])
    attended = attend_earlier(attended, stats, query, ((behind, behind), beside), False, head_size)
    mine = renew(grads, received, head_step, *nets, (attended,))
    near = combine_near(query, attended, mine)
    attended = attend_earlier(attended, stats, query, ((behind_far, behind_far),), True, head_size, (near,))
    return ring_reduce(query, attended, swap(mine, 1), near, w_out)


def solution(mesh):
    placed = (
        P("tok", "head"),
        P(None, "head"),
        P(None, "head"),
        P(None, "head"),
        P("head", None),
        P("head", None, None),
        P("head", None, None),
        P("head", None, None),
        P("tok", "head"),
        P("head"),
    )
    return jax.shard_map(
        shards, mesh=mesh, in_specs=placed, out_specs=P(("tok", "head"), None), check_vma=False
    )
```

```python
import functools

import jax
import jax.numpy as jnp
from jax import lax
from jax.experimental import pallas as pl
from jax.experimental.pallas import tpu as pltpu
from jax.sharding import PartitionSpec as P

WINDOW = 512
CHUNKS = 2
F32 = jnp.float32
BF16 = jnp.bfloat16
LOG2E = 1.4426950408889634


def call(body, in_specs, out_specs, out_shape, scratch=(), vmem=8, cost=None, aliases=None):
    return pl.pallas_call(
        body,
        in_specs=in_specs,
        out_specs=out_specs,
        out_shape=out_shape,
        scratch_shapes=list(scratch),
        input_output_aliases=aliases or {},
        cost_estimate=cost,
        compiler_params=pltpu.CompilerParams(vmem_limit_bytes=vmem * 1024 * 1024),
    )


def cost(flops, moved, exps=0):
    return pl.CostEstimate(flops=int(flops), bytes_accessed=int(moved), transcendentals=int(exps))


WHOLE = pl.BlockSpec(memory_space=pltpu.VMEM)
AFTER = pl.BlockSpec(memory_space=pl.ANY)
SCALARS = pl.BlockSpec(memory_space=pltpu.SMEM)
IN_HBM = pl.BlockSpec(memory_space=pltpu.HBM)


def mm(left, right, dims=((1,), (0,))):
    return lax.dot_general(left, right, (dims, ((), ())), preferred_element_type=F32)


def sigmoid(x):
    return 0.5 * jnp.tanh(0.5 * x) + 0.5


def ring_order(count):
    return list(range(0, count, 2)) + list(range(count - 1, 0, -2))


def ring_send(value, step):
    order = ring_order(lax.axis_size("head"))
    count = len(order)
    return lax.ppermute(
        value, "head", [(order[i], order[(i + step) % count]) for i in range(count)]
    )


def ring_offsets():
    steps = lax.axis_size("head") // 2
    return [0] + [way * step for step in range(1, steps) for way in (-1, 1)] + [steps]


def ring_index(offset):
    count = lax.axis_size("head")
    me = lax.axis_index("head")
    at = lax.rem(jnp.where(me % 2 == 0, me // 2, count - 1 - me // 2) + offset + count, count)
    return jnp.where(at < count // 2, 2 * at, 2 * (count - 1 - at) + 1)


def first_head(heads, other=False):
    side = lax.axis_index("tok") % 2
    return (1 - side if other else side) * heads


def hbm(array):
    return pltpu.with_memory_space_constraint(array, pltpu.HBM)


def run_copies(copies, most):
    for index, copy in enumerate(copies):
        if index >= most:
            copies[index - most].wait()
        copy.start()
    for copy in copies[-most:]:
        copy.wait()


def load(arrays):
    count = len(arrays)
    blocks = len(ring_offsets())
    size = arrays[0].shape[0] // blocks

    def body(*refs):
        out_refs, sems = refs[count:-1], refs[-1]
        starts = [pl.multiple_of(ring_index(offset) * size, size) for offset in ring_offsets()]
        run_copies(
            [
                pltpu.make_async_copy(
                    refs[index].at[pl.ds(starts[block], size)],
                    out_refs[index].at[pl.ds(block * size, size)],
                    sems.at[index, block],
                )
                for block in range(blocks)
                for index in range(count)
            ],
            4,
        )

    return call(
        body,
        [IN_HBM] * count,
        [WHOLE] * count,
        [jax.ShapeDtypeStruct(array.shape, array.dtype) for array in arrays],
        [pltpu.SemaphoreType.DMA((count, blocks))],
        vmem=1,
        cost=cost(0, sum(4 * array.size for array in arrays)),
    )(*[hbm(array) for array in arrays])


def split_rows(tokens):
    rows, width = tokens.shape[0] // CHUNKS, tokens.shape[1]

    def body(in_ref, *refs):
        out_refs, sems = refs[:-1], refs[-1]
        run_copies(
            [
                pltpu.make_async_copy(in_ref.at[pl.ds(c * rows, rows)], out_refs[c], sems.at[c])
                for c in range(CHUNKS)
            ],
            CHUNKS,
        )

    return call(
        body,
        [IN_HBM],
        [WHOLE] * CHUNKS,
        [jax.ShapeDtypeStruct((rows, width), tokens.dtype)] * CHUNKS,
        [pltpu.SemaphoreType.DMA((CHUNKS,))],
        vmem=1,
        cost=cost(0, 4 * tokens.size),
    )(hbm(tokens))


def gather_step(held, ways, after):
    moved = {}
    for way in ways:
        value = held[way]
        if after is not None:
            value, _ = lax.optimization_barrier((value, after))
        moved[way] = ring_send(value, way)
    return moved


def accumulate(chunks, first, last, weights, before=None, lead=0, shared=False):
    rows, depth = chunks[0][0].shape
    width = weights[0].shape[1]
    parts, span = len(weights), last - first
    total = rows * len(chunks)
    final = last == lax.axis_size("head")
    dtype = BF16 if final else F32
    pieces = [chunk[index] for chunk in chunks for index in range(first, last)]

    def body(*refs):
        piece_refs = refs[: len(pieces)]
        weight_refs = refs[len(pieces) : len(pieces) + parts]
        out_ref, left = refs[-2 - 2 * shared], refs[-1]
        for index, ref in enumerate(piece_refs):
            chunk, piece = divmod(index, span)
            left[chunk * rows : (chunk + 1) * rows, piece * depth : (piece + 1) * depth] = ref[...]
        for part in range(parts):
            term = mm(left[...], weight_refs[part][first * depth : last * depth])
            if before is not None:
                term = term + refs[len(args) - 1][lead + part]
            out_ref[part] = term.astype(dtype)
            if shared:
                side = lax.axis_index("tok") % 2
                refs[-3][part] = out_ref[part, :, lanes(1 - side, width // 2)]
                refs[-2][part] = out_ref[part, :, lanes(side, width // 2)]

    aliased = before is not None and not final
    args = [*pieces, *weights] + ([] if before is None else [before])
    return call(
        body,
        [WHOLE] * len(args),
        [WHOLE] * (1 + 2 * shared),
        [
            jax.ShapeDtypeStruct((parts, total, size), dtype)
            for size in (width, width // 2, width // 2)[: 1 + 2 * shared]
        ],
        [pltpu.VMEM((total, span * depth), BF16)],
        vmem=12,
        cost=cost(
            2 * total * span * depth * width * parts,
            2 * span * depth * (total + width * parts) + 8 * total * width * parts,
        ),
        aliases={len(args) - 1: 0} if aliased else None,
    )(*args)


def lanes(head, size):
    return pl.ds(pl.multiple_of(head * size, size), size)


def normed(values):
    values = values.astype(F32)
    scale = lax.rsqrt(jnp.mean(values * values, axis=-1, keepdims=True) + 1e-06)
    return (values * scale).astype(BF16)


def head_grads(kv, rate, fast_gate, fast_up, fast_down, before=None):
    rows = kv.shape[1]
    size, hidden_size = fast_gate.shape[1:]
    count = rate.shape[0]
    heads = count // 2
    whole = kv.shape[2] == count * size

    def body(kv_ref, rate_ref, gate_ref, up_ref, down_ref, *rest):
        rates = rate_ref[...].T
        column = lax.broadcasted_iota(jnp.int32, (rows, count), 1)
        for index in range(heads):
            head = first_head(heads) + index
            mine = jnp.sum(jnp.where(column == head, rates, 0.0), axis=1, keepdims=True)
            lane = lanes(head if whole else index, size)
            knorm = normed(kv_ref[0, :, lane])
            target = (-mine * kv_ref[1, :, lane].astype(F32)).astype(BF16)
            gate_pre = mm(knorm, gate_ref[head].astype(BF16))
            up_pre = mm(knorm, up_ref[head].astype(BF16))
            back = mm(target, down_ref[head].astype(BF16), ((1,), (1,)))
            sigma = sigmoid(gate_pre)
            active = gate_pre * sigma
            first = back * up_pre * (sigma + active * (1.0 - sigma))
            both = jnp.concatenate([first.astype(BF16), (back * active).astype(BF16)], axis=1)
            third = (active * up_pre).astype(BF16)
            pair = mm(knorm, both, ((0,), (0,)))
            terms = (pair[:, :hidden_size], pair[:, hidden_size:], mm(target, third, ((0,), (0,))))
            for part, term in enumerate(terms):
                if before is not None:
                    term = term + rest[0][index, part]
                    rest[-1][index, part] = term.astype(BF16)
                    rest[-2][index, part] = term
                else:
                    rest[-1][index, part] = term

    args = [kv, rate, fast_gate, fast_up, fast_down] + ([] if before is None else [before])
    kinds = [F32] if before is None else [F32, BF16]
    return call(
        body,
        [WHOLE] * len(args),
        [WHOLE] * len(kinds),
        [jax.ShapeDtypeStruct((heads, 3, size, hidden_size), kind) for kind in kinds],
        cost=cost(
            12 * heads * rows * size * hidden_size,
            8 * heads * 3 * size * hidden_size,
            heads * rows * hidden_size,
        ),
    )(*args)


def renew(kept, received, step, fast_gate, fast_up, fast_down, after):
    heads, _, size, hidden_size = kept.shape

    def body(step_ref, kept_ref, gate_ref, up_ref, down_ref, *rest):
        out_ref = rest[-1]
        for index in range(heads):
            head = first_head(heads) + index
            for part in range(3):
                grad = kept_ref[index, part]
                for more in rest[: len(received)]:
                    grad = grad + more[index, part].astype(F32)
                if part < 2:
                    matrix = (gate_ref, up_ref)[part][head]
                    fan = size
                else:
                    matrix = down_ref[head].T
                    fan = hidden_size
                mean_sq = jnp.sum(grad * grad, keepdims=True) / (size * hidden_size)
                scale = step_ref[head] * fan ** (-0.5) * lax.rsqrt(mean_sq + 1e-06)
                out_ref[index, part] = (matrix - scale * grad).astype(BF16)

    return call(
        body,
        [SCALARS] + [WHOLE] * (4 + len(received)) + [AFTER] * len(after),
        WHOLE,
        jax.ShapeDtypeStruct(kept.shape, BF16),
        cost=cost(10 * kept.size, 12 * kept.size),
    )(step, kept, fast_gate, fast_up, fast_down, *received, *after)


def attend_blocks(query, blocks):
    factor = query.shape[-1] ** (-0.5) * LOG2E
    scores = []
    for key, _, allowed in blocks:
        part = mm(query, key, ((1,), (1,))) * factor
        scores.append(part if allowed is None else jnp.where(allowed, part, -1e30))
    tops = [jnp.max(part, axis=-1, keepdims=True) for part in scores]
    top = functools.reduce(jnp.maximum, tops)
    result, total = 0.0, 0.0
    for part, (_, value, _) in zip(scores, blocks):
        weight = jnp.exp2(part - top)
        total = total + jnp.sum(weight, axis=-1, keepdims=True)
        result = result + mm(weight.astype(BF16), value)
    return result, top, total


def halves(rows):
    return [slice(index * rows // 2, (index + 1) * rows // 2) for index in range(2)]


def earlier_blocks(ref, index, lane):
    rows = ref.shape[1]
    row = lax.broadcasted_iota(jnp.int32, (rows // 2, rows // 2), 0)
    col = lax.broadcasted_iota(jnp.int32, (rows // 2, rows // 2), 1)
    blocks = [(ref[0, halves(rows)[index], lane], ref[1, halves(rows)[index], lane], col > row)]
    if index == 0:
        blocks.append((ref[0, halves(rows)[1], lane], ref[1, halves(rows)[1], lane], None))
    return blocks


def attend_own(query, kv, size):
    rows = query.shape[1]
    heads = query.shape[2] // size
    row = (rows // 2, rows // 2)

    def body(q_ref, kv_ref, out_ref, stats_ref):
        alone = lax.axis_index("tok") == 0
        causal = lax.broadcasted_iota(jnp.int32, row, 1) <= lax.broadcasted_iota(jnp.int32, row, 0)
        for index, where in enumerate(halves(rows)):
            for head in range(heads):
                lane = slice(head * size, (head + 1) * size)
                blocks = [
                    (kv_ref[0, keys, lane], kv_ref[1, keys, lane], causal if at == index else None)
                    for at, keys in enumerate(halves(rows)[: index + 1])
                ]
                result, top, total = attend_blocks(q_ref[0, where, lane], blocks)
                out_ref[where, lane] = result / jnp.where(alone, total, 1.0)
                stats_ref[0, where, lane] = jnp.broadcast_to(top, result.shape)
                stats_ref[1, where, lane] = jnp.broadcast_to(total, result.shape)

    return call(
        body,
        [WHOLE] * 2,
        [WHOLE] * 2,
        [
            jax.ShapeDtypeStruct((rows, heads * size), F32),
            jax.ShapeDtypeStruct((2, rows, heads * size), F32),
        ],
        cost=cost(3 * heads * size * rows * rows, 8 * rows * heads * size, heads * rows * rows),
    )(query, kv)


def attend_earlier(summed, stats, query, sources, other, size, after=()):
    rows = query.shape[1]
    heads = sources[0].shape[2] // size

    def body(sum_ref, stats_ref, q_ref, *refs):
        out_ref = refs[-1]
        place = lax.axis_index("tok")

        def add(ref):
            for index, where in enumerate(halves(rows)):
                for at in range(heads):
                    lane = lanes(first_head(heads, other) + at, size)
                    result, top, total = attend_blocks(
                        q_ref[0, where, lane],
                        earlier_blocks(ref, index, slice(at * size, (at + 1) * size)),
                    )
                    before = stats_ref[0, where, lane]
                    both = jnp.maximum(before, top)
                    old, new = jnp.exp2(before - both), jnp.exp2(top - both)
                    total = stats_ref[1, where, lane] * old + total * new
                    out_ref[where, lane] = (sum_ref[where, lane] * old + result * new) / total

        if len(sources) == 1:
            pl.when(place > 0)(lambda: add(refs[0]))
        else:
            pl.when((place > 0) & (place % 2 == 0))(lambda: add(refs[0]))
            pl.when(place % 2 == 1)(lambda: add(refs[1]))

    return call(
        body,
        [WHOLE] * (3 + len(sources)) + [AFTER] * len(after),
        WHOLE,
        jax.ShapeDtypeStruct(summed.shape, F32),
        cost=cost(3 * heads * size * rows * rows, 8 * rows * heads * size, heads * rows * rows),
        aliases={0: 0},
    )(summed, stats, query, *sources, *after)


def fast_apply(query, gate, upper, down):
    qnorm = normed(query)
    gate_pre = mm(qnorm, gate)
    hidden = gate_pre * sigmoid(gate_pre) * mm(qnorm, upper)
    return mm(hidden.astype(BF16), down, ((1,), (1,)))


def combine_near(query, attended, nets):
    rows = query.shape[1]
    heads, _, size, hidden_size = nets.shape

    def body(q_ref, attended_ref, net_ref, out_ref):
        for index in range(heads):
            lane = lanes(first_head(heads) + index, size)
            fast = fast_apply(q_ref[0, :, lane], *(net_ref[index, part] for part in range(3)))
            where = slice(index * size, (index + 1) * size)
            out_ref[:, where] = (attended_ref[:, lane] + fast).astype(BF16)

    return call(
        body,
        [WHOLE] * 3,
        WHOLE,
        jax.ShapeDtypeStruct((rows, heads * size), BF16),
        cost=cost(
            6 * heads * rows * size * hidden_size,
            8 * heads * rows * size,
            heads * rows * hidden_size,
        ),
    )(query, attended, nets)


def partial_out(offsets, query, attended, nets, near, w_out, after=()):
    rows = near.shape[0] // lax.axis_size("head")
    heads, _, size, hidden_size = nets.shape
    depth = heads * size
    count = len(offsets)
    width = w_out.shape[1]
    block = width // 8

    def body(q_ref, attended_ref, net_ref, near_ref, w_ref, *refs):
        out_refs, far_ref = refs[len(after) : -1], refs[-1]
        starts = [pl.multiple_of(ring_index(offset) * rows, rows) for offset in offsets]

        def take(ref, lane):
            return jnp.concatenate([ref[pl.ds(start, rows), lane] for start in starts], axis=0)

        for index in range(heads):
            lane = lanes(first_head(heads, True) + index, size)
            fast = fast_apply(
                take(q_ref.at[0], lane), *(net_ref[index, part] for part in range(3))
            )
            where = slice(index * size, (index + 1) * size)
            far_ref[:, where] = (take(attended_ref, lane) + fast).astype(BF16)
        left = take(near_ref, slice(None))
        near_rows = pl.ds(pl.multiple_of(first_head(heads) * size, depth), depth)
        far_rows = pl.ds(pl.multiple_of(first_head(heads, True) * size, depth), depth)
        for column in range(0, width, block):
            result = mm(left, w_ref[near_rows, column : column + block])
            result += mm(far_ref[...], w_ref[far_rows, column : column + block])
            result = result.astype(BF16)
            half, at = divmod(column, width // 2)
            for index in range(count):
                out_refs[2 * index + half][:, at : at + block] = result[
                    index * rows : (index + 1) * rows
                ]

    outs = call(
        body,
        [WHOLE] * 5 + [AFTER] * len(after),
        [WHOLE] * (2 * count),
        [jax.ShapeDtypeStruct((rows, width // 2), BF16)] * (2 * count),
        [pltpu.VMEM((count * rows, depth), BF16)],
        vmem=8,
        cost=cost(4 * count * rows * depth * width, 2 * width * (2 * depth + count * rows)),
    )(query, attended, nets, near, w_out, *after)
    return {offset: tuple(outs[2 * at : 2 * at + 2]) for at, offset in enumerate(offsets)}


def ring_reduce(query, attended, nets, near, w_out):
    steps = lax.axis_size("head") // 2
    signed = [sign * step for step in range(steps - 1, 0, -1) for sign in (1, -1)]
    shared = (query, attended, nets, near, w_out)
    parts = partial_out([steps], *shared) | partial_out(signed[:2], *shared)
    coming = {}
    ordered = ()
    for which in range(2 * steps - 1):
        step, half = steps - (which + 1) // 2, which % 2
        if which % 2 == 0 and 2 <= which <= 2 * (steps - 2):
            later = signed[which : which + 2] + [0] * (which == 2 * (steps - 2))
            parts |= partial_out(later, *shared, tuple(coming.values())[:2])
        terms = []
        for way in (1, -1):
            side = half if way == 1 else 1 - half
            term = parts[steps if step == steps else way * step][side]
            if (way, side) in coming:
                term = (term.astype(F32) + coming[way, side].astype(F32)).astype(BF16)
            terms.append(term)
        ordered = lax.optimization_barrier((*terms, *ordered))[:2]
        for way, term in zip((1, -1), ordered):
            coming[way, half if way == 1 else 1 - half] = ring_send(term, way)
    sides = {1: 1 - half, -1: half}
    totals = add_pair(
        [parts[0][sides[way]] for way in (1, -1)], [coming.pop((way, sides[way])) for way in (1, -1)]
    )
    totals = {sides[way]: total for way, total in zip((1, -1), totals)}
    ends = [totals[side] for side in range(2)]
    for (_, side), more in coming.items():
        ends[side] = ends[side] + more.astype(F32)
    return jnp.concatenate([end.astype(BF16) for end in ends], axis=1)


def add_pair(own, came):
    def body(*refs):
        for index in range(2):
            refs[4 + index][...] = refs[index][...].astype(F32) + refs[2 + index][...].astype(F32)

    return call(
        body,
        [WHOLE] * 4,
        [WHOLE] * 2,
        [jax.ShapeDtypeStruct(value.shape, F32) for value in own],
        cost=cost(0, 64 * own[0].size),
    )(*own, *came)


def swap(value, bit):
    count = lax.axis_size("tok")
    return lax.ppermute(value, "tok", [(index, index ^ bit) for index in range(count)])


def shards(
    tokens, w_query, w_key, w_value, w_out, fast_gate, fast_up, fast_down, token_rate, head_step
):
    local_heads, head_size, _ = fast_gate.shape
    tok_count = lax.axis_size("tok")
    steps = lax.axis_size("head") // 2
    nets = (fast_gate, fast_up, fast_down)
    rate = token_rate.T
    rate_beside = swap(rate, 1)

    own = split_rows(tokens)
    weights = load([w_key, w_value, w_query])
    chunks = [[piece] for piece in own]
    held = [{1: piece, -1: piece} for piece in own]
    sums, done = None, 0
    for step in range(1, steps + 1):
        after = {2: weights[0], 3: (sums, rate_beside)}.get(step)
        for c in range(CHUNKS):
            last = (1,) if c % 2 == 0 else (-1,)
            held[c] = gather_step(held[c], (1, -1) if step < steps else last, after)
            chunks[c] += held[c].values()
        if step > 1:
            known = [chunk[: 2 * step - 1] for chunk in chunks]
            (sums,) = accumulate(known, done, 2 * step - 1, weights, sums)
            done = 2 * step - 1
    kv, far, near = accumulate(chunks, done, 2 * steps, weights[:2], sums, shared=True)
    (query,) = accumulate(chunks, done, 2 * steps, weights[2:], sums, 2)

    behind = lax.ppermute(far, "tok", [(index, index + 1) for index in range(1, tok_count - 1, 2)])
    beside = swap(far, 1)
    (grads,) = head_grads(kv, rate, *nets)
    grads, travel = head_grads(beside, rate_beside, *nets, grads)
    received = []
    for bit in range(1, tok_count.bit_length() - 1):
        if received:
            travel = grads
            for more in received:
                travel = travel + more.astype(F32)
            travel = travel.astype(BF16)
        received.append(swap(travel, 1 << bit))
    attended, stats = attend_own(query, kv, head_size)
    near, _ = lax.optimization_barrier((near, attended))
    behind_far = lax.ppermute(near, "tok", [(index, index + 1) for index in range(tok_count - 1)])
    attended = attend_earlier(attended, stats, query, (behind, beside), False, head_size)
    mine = renew(grads, received, head_step, *nets, (attended,))
    near = combine_near(query, attended, mine)
    attended = attend_earlier(attended, stats, query, (behind_far,), True, head_size, (near,))
    return ring_reduce(query, attended, swap(mine, 1), near, w_out)


def solution(mesh):
    placed = (
        P("tok", "head"),
        P(None, "head"),
        P(None, "head"),
        P(None, "head"),
        P("head", None),
        P("head", None, None),
        P("head", None, None),
        P("head", None, None),
        P("tok", "head"),
        P("head"),
    )
    return jax.shard_map(
        shards, mesh=mesh, in_specs=placed, out_specs=P(("tok", "head"), None), check_vma=False
    )
```

```python
import functools

import jax
import jax.numpy as jnp
from jax import lax
from jax.experimental import pallas as pl
from jax.experimental.pallas import tpu as pltpu
from jax.sharding import PartitionSpec as P

WINDOW = 512
CHUNKS = 2
F32 = jnp.float32
BF16 = jnp.bfloat16
LOG2E = 1.4426950408889634


def call(body, in_specs, out_specs, out_shape, scratch=(), vmem=8, cost=None, aliases=None):
    return pl.pallas_call(
        body,
        in_specs=in_specs,
        out_specs=out_specs,
        out_shape=out_shape,
        scratch_shapes=list(scratch),
        input_output_aliases=aliases or {},
        cost_estimate=cost,
        compiler_params=pltpu.CompilerParams(vmem_limit_bytes=vmem * 1024 * 1024),
    )


def cost(flops, moved, exps=0):
    return pl.CostEstimate(flops=int(flops), bytes_accessed=int(moved), transcendentals=int(exps))


WHOLE = pl.BlockSpec(memory_space=pltpu.VMEM)
AFTER = pl.BlockSpec(memory_space=pl.ANY)
SCALARS = pl.BlockSpec(memory_space=pltpu.SMEM)
IN_HBM = pl.BlockSpec(memory_space=pltpu.HBM)


def mm(left, right, dims=((1,), (0,))):
    return lax.dot_general(left, right, (dims, ((), ())), preferred_element_type=F32)


def sigmoid(x):
    return 0.5 * jnp.tanh(0.5 * x) + 0.5


def ring_order(count):
    return list(range(0, count, 2)) + list(range(count - 1, 0, -2))


def ring_send(value, step):
    order = ring_order(lax.axis_size("head"))
    count = len(order)
    return lax.ppermute(
        value, "head", [(order[i], order[(i + step) % count]) for i in range(count)]
    )


def ring_offsets():
    steps = lax.axis_size("head") // 2
    return [0] + [way * step for step in range(1, steps) for way in (-1, 1)] + [steps]


def ring_index(offset):
    count = lax.axis_size("head")
    me = lax.axis_index("head")
    at = lax.rem(jnp.where(me % 2 == 0, me // 2, count - 1 - me // 2) + offset + count, count)
    return jnp.where(at < count // 2, 2 * at, 2 * (count - 1 - at) + 1)


def first_head(heads, other=False):
    side = lax.axis_index("tok") % 2
    return (1 - side if other else side) * heads


def hbm(array):
    return pltpu.with_memory_space_constraint(array, pltpu.HBM)


def run_copies(copies, most):
    for index, copy in enumerate(copies):
        if index >= most:
            copies[index - most].wait()
        copy.start()
    for copy in copies[-most:]:
        copy.wait()


def load(arrays):
    count = len(arrays)
    blocks = len(ring_offsets())
    size = arrays[0].shape[0] // blocks

    def body(*refs):
        out_refs, sems = refs[count:-1], refs[-1]
        starts = [pl.multiple_of(ring_index(offset) * size, size) for offset in ring_offsets()]
        run_copies(
            [
                pltpu.make_async_copy(
                    refs[index].at[pl.ds(starts[block], size)],
                    out_refs[index].at[pl.ds(block * size, size)],
                    sems.at[index, block],
                )
                for block in range(blocks)
                for index in range(count)
            ],
            count * blocks,
        )

    return call(
        body,
        [IN_HBM] * count,
        [WHOLE] * count,
        [jax.ShapeDtypeStruct(array.shape, array.dtype) for array in arrays],
        [pltpu.SemaphoreType.DMA((count, blocks))],
        vmem=1,
        cost=cost(0, sum(4 * array.size for array in arrays)),
    )(*[hbm(array) for array in arrays])


def split_rows(tokens):
    rows, width = tokens.shape[0] // CHUNKS, tokens.shape[1]

    def body(in_ref, *refs):
        out_refs, sems = refs[:-1], refs[-1]
        run_copies(
            [
                pltpu.make_async_copy(in_ref.at[pl.ds(c * rows, rows)], out_refs[c], sems.at[c])
                for c in range(CHUNKS)
            ],
            CHUNKS,
        )

    return call(
        body,
        [IN_HBM],
        [WHOLE] * CHUNKS,
        [jax.ShapeDtypeStruct((rows, width), tokens.dtype)] * CHUNKS,
        [pltpu.SemaphoreType.DMA((CHUNKS,))],
        vmem=1,
        cost=cost(0, 4 * tokens.size),
    )(hbm(tokens))


def gather_step(held, ways, after):
    moved = {}
    for way in ways:
        value = held[way]
        if after is not None:
            value, _ = lax.optimization_barrier((value, after))
        moved[way] = ring_send(value, way)
    return moved


def accumulate(chunks, first, last, weights, before=None, lead=0, shared=False):
    rows, depth = chunks[0][0].shape
    width = weights[0].shape[1]
    parts, span = len(weights), last - first
    total = rows * len(chunks)
    final = last == lax.axis_size("head")
    dtype = BF16 if final else F32
    pieces = [chunk[index] for chunk in chunks for index in range(first, last)]

    def body(*refs):
        piece_refs = refs[: len(pieces)]
        weight_refs = refs[len(pieces) : len(pieces) + parts]
        out_ref, left = refs[-2 - 2 * shared], refs[-1]
        for index, ref in enumerate(piece_refs):
            chunk, piece = divmod(index, span)
            left[chunk * rows : (chunk + 1) * rows, piece * depth : (piece + 1) * depth] = ref[...]
        for part in range(parts):
            term = mm(left[...], weight_refs[part][first * depth : last * depth])
            if before is not None:
                term = term + refs[len(args) - 1][lead + part]
            out_ref[part] = term.astype(dtype)
            if shared:
                side = lax.axis_index("tok") % 2
                refs[-3][part] = out_ref[part, :, lanes(1 - side, width // 2)]
                refs[-2][part] = out_ref[part, :, lanes(side, width // 2)]

    aliased = before is not None and not final
    args = [*pieces, *weights] + ([] if before is None else [before])
    return call(
        body,
        [WHOLE] * len(args),
        [WHOLE] * (1 + 2 * shared),
        [
            jax.ShapeDtypeStruct((parts, total, size), dtype)
            for size in (width, width // 2, width // 2)[: 1 + 2 * shared]
        ],
        [pltpu.VMEM((total, span * depth), BF16)],
        vmem=12,
        cost=cost(
            2 * total * span * depth * width * parts,
            2 * span * depth * (total + width * parts) + 8 * total * width * parts,
        ),
        aliases={len(args) - 1: 0} if aliased else None,
    )(*args)


def lanes(head, size):
    return pl.ds(pl.multiple_of(head * size, size), size)


def normed(values):
    values = values.astype(F32)
    scale = lax.rsqrt(jnp.mean(values * values, axis=-1, keepdims=True) + 1e-06)
    return (values * scale).astype(BF16)


def head_grads(kv, rate, fast_gate, fast_up, fast_down, before=None):
    rows = kv.shape[1]
    size, hidden_size = fast_gate.shape[1:]
    count = rate.shape[0]
    heads = count // 2
    whole = kv.shape[2] == count * size

    def body(kv_ref, rate_ref, gate_ref, up_ref, down_ref, *rest):
        rates = rate_ref[...].T
        column = lax.broadcasted_iota(jnp.int32, (rows, count), 1)
        for index in range(heads):
            head = first_head(heads) + index
            mine = jnp.sum(jnp.where(column == head, rates, 0.0), axis=1, keepdims=True)
            lane = lanes(head if whole else index, size)
            knorm = normed(kv_ref[0, :, lane])
            target = (-mine * kv_ref[1, :, lane].astype(F32)).astype(BF16)
            gate_pre = mm(knorm, gate_ref[head].astype(BF16))
            up_pre = mm(knorm, up_ref[head].astype(BF16))
            back = mm(target, down_ref[head].astype(BF16), ((1,), (1,)))
            sigma = sigmoid(gate_pre)
            active = gate_pre * sigma
            first = back * up_pre * (sigma + active * (1.0 - sigma))
            both = jnp.concatenate([first.astype(BF16), (back * active).astype(BF16)], axis=1)
            third = (active * up_pre).astype(BF16)
            pair = mm(knorm, both, ((0,), (0,)))
            terms = (pair[:, :hidden_size], pair[:, hidden_size:], mm(target, third, ((0,), (0,))))
            for part, term in enumerate(terms):
                if before is not None:
                    term = term + rest[0][index, part]
                    rest[-1][index, part] = term.astype(BF16)
                    rest[-2][index, part] = term
                else:
                    rest[-1][index, part] = term

    args = [kv, rate, fast_gate, fast_up, fast_down] + ([] if before is None else [before])
    kinds = [F32] if before is None else [F32, BF16]
    return call(
        body,
        [WHOLE] * len(args),
        [WHOLE] * len(kinds),
        [jax.ShapeDtypeStruct((heads, 3, size, hidden_size), kind) for kind in kinds],
        cost=cost(
            12 * heads * rows * size * hidden_size,
            8 * heads * 3 * size * hidden_size,
            heads * rows * hidden_size,
        ),
    )(*args)


def renew(kept, received, step, fast_gate, fast_up, fast_down, after):
    heads, _, size, hidden_size = kept.shape

    def body(step_ref, kept_ref, gate_ref, up_ref, down_ref, *rest):
        out_ref = rest[-1]
        for index in range(heads):
            head = first_head(heads) + index
            for part in range(3):
                grad = kept_ref[index, part]
                for more in rest[: len(received)]:
                    grad = grad + more[index, part].astype(F32)
                if part < 2:
                    matrix = (gate_ref, up_ref)[part][head]
                    fan = size
                else:
                    matrix = down_ref[head].T
                    fan = hidden_size
                mean_sq = jnp.sum(grad * grad, keepdims=True) / (size * hidden_size)
                scale = step_ref[head] * fan ** (-0.5) * lax.rsqrt(mean_sq + 1e-06)
                out_ref[index, part] = (matrix - scale * grad).astype(BF16)

    return call(
        body,
        [SCALARS] + [WHOLE] * (4 + len(received)) + [AFTER] * len(after),
        WHOLE,
        jax.ShapeDtypeStruct(kept.shape, BF16),
        cost=cost(10 * kept.size, 12 * kept.size),
    )(step, kept, fast_gate, fast_up, fast_down, *received, *after)


def attend_blocks(query, blocks):
    factor = query.shape[-1] ** (-0.5) * LOG2E
    scores = []
    for key, _, allowed in blocks:
        part = mm(query, key, ((1,), (1,))) * factor
        scores.append(part if allowed is None else jnp.where(allowed, part, -1e30))
    tops = [jnp.max(part, axis=-1, keepdims=True) for part in scores]
    top = functools.reduce(jnp.maximum, tops)
    result, total = 0.0, 0.0
    for part, (_, value, _) in zip(scores, blocks):
        weight = jnp.exp2(part - top)
        total = total + jnp.sum(weight, axis=-1, keepdims=True)
        result = result + mm(weight.astype(BF16), value)
    return result, top, total


def halves(rows):
    return [slice(index * rows // 2, (index + 1) * rows // 2) for index in range(2)]


def earlier_blocks(ref, index, lane):
    rows = ref.shape[1]
    row = lax.broadcasted_iota(jnp.int32, (rows // 2, rows // 2), 0)
    col = lax.broadcasted_iota(jnp.int32, (rows // 2, rows // 2), 1)
    blocks = [(ref[0, halves(rows)[index], lane], ref[1, halves(rows)[index], lane], col > row)]
    if index == 0:
        blocks.append((ref[0, halves(rows)[1], lane], ref[1, halves(rows)[1], lane], None))
    return blocks


def attend_own(query, kv, size):
    rows = query.shape[1]
    heads = query.shape[2] // size
    row = (rows // 2, rows // 2)

    def body(q_ref, kv_ref, out_ref, stats_ref):
        alone = lax.axis_index("tok") == 0
        causal = lax.broadcasted_iota(jnp.int32, row, 1) <= lax.broadcasted_iota(jnp.int32, row, 0)
        for index, where in enumerate(halves(rows)):
            for head in range(heads):
                lane = slice(head * size, (head + 1) * size)
                blocks = [
                    (kv_ref[0, keys, lane], kv_ref[1, keys, lane], causal if at == index else None)
                    for at, keys in enumerate(halves(rows)[: index + 1])
                ]
                result, top, total = attend_blocks(q_ref[0, where, lane], blocks)
                share = jnp.where(alone, total, 1.0) if head < heads // 2 else 1.0
                out_ref[where, lane] = result / share
                stats_ref[0, where, lane] = jnp.broadcast_to(top, result.shape)
                stats_ref[1, where, lane] = jnp.broadcast_to(total, result.shape)

    return call(
        body,
        [WHOLE] * 2,
        [WHOLE] * 2,
        [
            jax.ShapeDtypeStruct((rows, heads * size), F32),
            jax.ShapeDtypeStruct((2, rows, heads * size), F32),
        ],
        cost=cost(3 * heads * size * rows * rows, 8 * rows * heads * size, heads * rows * rows),
    )(query, kv)


def merged(summed, before, sums, result, top, total):
    both = jnp.maximum(before, top)
    old, new = jnp.exp2(before - both), jnp.exp2(top - both)
    return (summed * old + result * new) / (sums * old + total * new)


def attend_earlier(summed, stats, query, sources, size):
    rows = query.shape[1]
    heads = sources[0].shape[2] // size

    def body(sum_ref, stats_ref, q_ref, behind_ref, beside_ref, out_ref):
        place = lax.axis_index("tok")

        def add(ref):
            for index, where in enumerate(halves(rows)):
                for at in range(heads):
                    lane = lanes(first_head(heads) + at, size)
                    out_ref[where, lane] = merged(
                        sum_ref[where, lane],
                        stats_ref[0, where, lane],
                        stats_ref[1, where, lane],
                        *attend_blocks(
                            q_ref[0, where, lane],
                            earlier_blocks(ref, index, slice(at * size, (at + 1) * size)),
                        ),
                    )

        pl.when((place > 0) & (place % 2 == 0))(lambda: add(behind_ref))
        pl.when(place % 2 == 1)(lambda: add(beside_ref))

    return call(
        body,
        [WHOLE] * 5,
        WHOLE,
        jax.ShapeDtypeStruct(summed.shape, F32),
        cost=cost(3 * heads * size * rows * rows, 8 * rows * heads * size, heads * rows * rows),
        aliases={0: 0},
    )(summed, stats, query, *sources)


def fast_apply(query, gate, upper, down):
    qnorm = normed(query)
    gate_pre = mm(qnorm, gate)
    hidden = gate_pre * sigmoid(gate_pre) * mm(qnorm, upper)
    return mm(hidden.astype(BF16), down, ((1,), (1,)))


def combine_near(query, attended, nets):
    rows = query.shape[1]
    heads, _, size, hidden_size = nets.shape

    def body(q_ref, attended_ref, net_ref, out_ref):
        for index in range(heads):
            lane = lanes(first_head(heads) + index, size)
            fast = fast_apply(q_ref[0, :, lane], *(net_ref[index, part] for part in range(3)))
            where = slice(index * size, (index + 1) * size)
            out_ref[:, where] = (attended_ref[:, lane] + fast).astype(BF16)

    return call(
        body,
        [WHOLE] * 3,
        WHOLE,
        jax.ShapeDtypeStruct((rows, heads * size), BF16),
        cost=cost(
            6 * heads * rows * size * hidden_size,
            8 * heads * rows * size,
            heads * rows * hidden_size,
        ),
    )(query, attended, nets)


def partial_out(offsets, query, attended, stats, behind, nets, near, w_out, after=()):
    rows = near.shape[0] // lax.axis_size("head")
    heads, _, size, hidden_size = nets.shape
    depth = heads * size
    count = len(offsets)
    width = w_out.shape[1]
    block = width // 8

    def body(q_ref, attended_ref, stats_ref, behind_ref, net_ref, near_ref, w_ref, *refs):
        out_refs, far_ref = refs[len(after) : -1], refs[-1]
        starts = [pl.multiple_of(ring_index(offset) * rows, rows) for offset in offsets]

        def take(ref, lane):
            return jnp.concatenate([ref[pl.ds(start, rows), lane] for start in starts], axis=0)

        row = lax.broadcasted_iota(jnp.int32, (rows, behind.shape[1]), 0)
        row = jnp.concatenate([row + start for start in starts], axis=0)
        col = lax.broadcasted_iota(jnp.int32, row.shape, 1)
        within = (col > row) & (lax.axis_index("tok") > 0)
        for index in range(heads):
            lane = lanes(first_head(heads, True) + index, size)
            where = slice(index * size, (index + 1) * size)
            queries = take(q_ref.at[0], lane)
            fast = fast_apply(queries, *(net_ref[index, part] for part in range(3)))
            seen = merged(
                take(attended_ref, lane),
                take(stats_ref.at[0], lane),
                take(stats_ref.at[1], lane),
                *attend_blocks(queries, [(behind_ref[0, :, where], behind_ref[1, :, where], within)]),
            )
            far_ref[:, where] = (seen + fast).astype(BF16)
        left = take(near_ref, slice(None))
        near_rows = pl.ds(pl.multiple_of(first_head(heads) * size, depth), depth)
        far_rows = pl.ds(pl.multiple_of(first_head(heads, True) * size, depth), depth)
        for column in range(0, width, block):
            result = mm(left, w_ref[near_rows, column : column + block])
            result += mm(far_ref[...], w_ref[far_rows, column : column + block])
            result = result.astype(BF16)
            half, at = divmod(column, width // 2)
            for index in range(count):
                out_refs[2 * index + half][:, at : at + block] = result[
                    index * rows : (index + 1) * rows
                ]

    outs = call(
        body,
        [WHOLE] * 7 + [AFTER] * len(after),
        [WHOLE] * (2 * count),
        [jax.ShapeDtypeStruct((rows, width // 2), BF16)] * (2 * count),
        [pltpu.VMEM((count * rows, depth), BF16)],
        vmem=8,
        cost=cost(4 * count * rows * depth * width, 2 * width * (2 * depth + count * rows)),
    )(query, attended, stats, behind, nets, near, w_out, *after)
    return {offset: tuple(outs[2 * at : 2 * at + 2]) for at, offset in enumerate(offsets)}


def ring_reduce(*shared):
    steps = lax.axis_size("head") // 2
    signed = [sign * step for step in range(steps - 1, 0, -1) for sign in (1, -1)]
    parts = partial_out([steps], *shared) | partial_out(signed[:2], *shared)
    coming = {}
    ordered = ()
    for which in range(2 * steps - 1):
        step, half = steps - (which + 1) // 2, which % 2
        if which % 2 == 0 and 2 <= which <= 2 * (steps - 2):
            later = signed[which : which + 2] + [0] * (which == 2 * (steps - 2))
            parts |= partial_out(later, *shared, tuple(coming.values())[:2])
        terms = []
        for way in (1, -1):
            side = half if way == 1 else 1 - half
            term = parts[steps if step == steps else way * step][side]
            if (way, side) in coming:
                term = (term.astype(F32) + coming[way, side].astype(F32)).astype(BF16)
            terms.append(term)
        ordered = lax.optimization_barrier((*terms, *ordered))[:2]
        for way, term in zip((1, -1), ordered):
            coming[way, half if way == 1 else 1 - half] = ring_send(term, way)
    sides = {1: 1 - half, -1: half}
    totals = add_pair(
        [parts[0][sides[way]] for way in (1, -1)], [coming.pop((way, sides[way])) for way in (1, -1)]
    )
    totals = {sides[way]: total for way, total in zip((1, -1), totals)}
    ends = [totals[side] for side in range(2)]
    for (_, side), more in coming.items():
        ends[side] = ends[side] + more.astype(F32)
    return jnp.concatenate([end.astype(BF16) for end in ends], axis=1)


def add_pair(own, came):
    def body(*refs):
        for index in range(2):
            refs[4 + index][...] = refs[index][...].astype(F32) + refs[2 + index][...].astype(F32)

    return call(
        body,
        [WHOLE] * 4,
        [WHOLE] * 2,
        [jax.ShapeDtypeStruct(value.shape, F32) for value in own],
        cost=cost(0, 64 * own[0].size),
    )(*own, *came)


def swap(value, bit):
    count = lax.axis_size("tok")
    return lax.ppermute(value, "tok", [(index, index ^ bit) for index in range(count)])


def shards(
    tokens, w_query, w_key, w_value, w_out, fast_gate, fast_up, fast_down, token_rate, head_step
):
    local_heads, head_size, _ = fast_gate.shape
    tok_count = lax.axis_size("tok")
    steps = lax.axis_size("head") // 2
    nets = (fast_gate, fast_up, fast_down)
    rate = token_rate.T
    rate_beside = swap(rate, 1)

    own = split_rows(tokens)
    weights = load([w_key, w_value, w_query])
    chunks = [[piece] for piece in own]
    held = [{1: piece, -1: piece} for piece in own]
    sums, done = None, 0
    for step in range(1, steps + 1):
        after = {2: weights[0], 3: (sums, rate_beside)}.get(step)
        for c in range(CHUNKS):
            last = (1,) if c % 2 == 0 else (-1,)
            held[c] = gather_step(held[c], (1, -1) if step < steps else last, after)
            chunks[c] += held[c].values()
        if step > 1:
            known = [chunk[: 2 * step - 1] for chunk in chunks]
            (sums,) = accumulate(known, done, 2 * step - 1, weights, sums)
            done = 2 * step - 1
    kv, far, near = accumulate(chunks, done, 2 * steps, weights[:2], sums, shared=True)
    (query,) = accumulate(chunks, done, 2 * steps, weights[2:], sums, 2)

    behind = lax.ppermute(far, "tok", [(index, index + 1) for index in range(1, tok_count - 1, 2)])
    beside = swap(far, 1)
    (grads,) = head_grads(kv, rate, *nets)
    grads, travel = head_grads(beside, rate_beside, *nets, grads)
    received = []
    for bit in range(1, tok_count.bit_length() - 1):
        if received:
            travel = grads
            for more in received:
                travel = travel + more.astype(F32)
            travel = travel.astype(BF16)
        received.append(swap(travel, 1 << bit))
    attended, stats = attend_own(query, kv, head_size)
    attended = attend_earlier(attended, stats, query, (behind, beside), head_size)
    near, _ = lax.optimization_barrier((near, attended))
    behind_far = lax.ppermute(near, "tok", [(index, index + 1) for index in range(tok_count - 1)])
    mine = renew(grads, received, head_step, *nets, (attended,))
    near = combine_near(query, attended, mine)
    return ring_reduce(query, attended, stats, behind_far, swap(mine, 1), near, w_out)


def solution(mesh):
    placed = (
        P("tok", "head"),
        P(None, "head"),
        P(None, "head"),
        P(None, "head"),
        P("head", None),
        P("head", None, None),
        P("head", None, None),
        P("head", None, None),
        P("tok", "head"),
        P("head"),
    )
    return jax.shard_map(
        shards, mesh=mesh, in_specs=placed, out_specs=P(("tok", "head"), None), check_vma=False
    )
```

```python
import functools

import jax
import jax.numpy as jnp
from jax import lax
from jax.experimental import pallas as pl
from jax.experimental.pallas import tpu as pltpu
from jax.sharding import PartitionSpec as P

WINDOW = 512
CHUNKS = 2
F32 = jnp.float32
BF16 = jnp.bfloat16
LOG2E = 1.4426950408889634


def call(body, in_specs, out_specs, out_shape, scratch=(), vmem=8, cost=None, aliases=None):
    return pl.pallas_call(
        body,
        in_specs=in_specs,
        out_specs=out_specs,
        out_shape=out_shape,
        scratch_shapes=list(scratch),
        input_output_aliases=aliases or {},
        cost_estimate=cost,
        compiler_params=pltpu.CompilerParams(vmem_limit_bytes=vmem * 1024 * 1024),
    )


def cost(flops, moved, exps=0):
    return pl.CostEstimate(flops=int(flops), bytes_accessed=int(moved), transcendentals=int(exps))


WHOLE = pl.BlockSpec(memory_space=pltpu.VMEM)
AFTER = pl.BlockSpec(memory_space=pl.ANY)
SCALARS = pl.BlockSpec(memory_space=pltpu.SMEM)
IN_HBM = pl.BlockSpec(memory_space=pltpu.HBM)


def mm(left, right, dims=((1,), (0,))):
    return lax.dot_general(left, right, (dims, ((), ())), preferred_element_type=F32)


def sigmoid(x):
    return 0.5 * jnp.tanh(0.5 * x) + 0.5


def ring_order(count):
    return list(range(0, count, 2)) + list(range(count - 1, 0, -2))


def ring_send(value, step):
    order = ring_order(lax.axis_size("head"))
    count = len(order)
    return lax.ppermute(
        value, "head", [(order[i], order[(i + step) % count]) for i in range(count)]
    )


def ring_offsets():
    steps = lax.axis_size("head") // 2
    return [0] + [way * step for step in range(1, steps) for way in (-1, 1)] + [steps]


def ring_index(offset):
    count = lax.axis_size("head")
    me = lax.axis_index("head")
    at = lax.rem(jnp.where(me % 2 == 0, me // 2, count - 1 - me // 2) + offset + count, count)
    return jnp.where(at < count // 2, 2 * at, 2 * (count - 1 - at) + 1)


def first_head(heads, other=False):
    side = lax.axis_index("tok") % 2
    return (1 - side if other else side) * heads


def hbm(array):
    return pltpu.with_memory_space_constraint(array, pltpu.HBM)


def run_copies(copies, most):
    for index, copy in enumerate(copies):
        if index >= most:
            copies[index - most].wait()
        copy.start()
    for copy in copies[-most:]:
        copy.wait()


def load(arrays):
    count = len(arrays)
    blocks = len(ring_offsets())
    size = arrays[0].shape[0] // blocks

    def body(*refs):
        out_refs, sems = refs[count:-1], refs[-1]
        starts = [pl.multiple_of(ring_index(offset) * size, size) for offset in ring_offsets()]
        run_copies(
            [
                pltpu.make_async_copy(
                    refs[index].at[pl.ds(starts[block], size)],
                    out_refs[index].at[pl.ds(block * size, size)],
                    sems.at[index, block],
                )
                for block in range(blocks)
                for index in range(count)
            ],
            count * blocks,
        )

    return call(
        body,
        [IN_HBM] * count,
        [WHOLE] * count,
        [jax.ShapeDtypeStruct(array.shape, array.dtype) for array in arrays],
        [pltpu.SemaphoreType.DMA((count, blocks))],
        vmem=1,
        cost=cost(0, sum(4 * array.size for array in arrays)),
    )(*[hbm(array) for array in arrays])


def split_rows(tokens):
    rows, width = tokens.shape[0] // CHUNKS, tokens.shape[1]

    def body(in_ref, *refs):
        out_refs, sems = refs[:-1], refs[-1]
        run_copies(
            [
                pltpu.make_async_copy(in_ref.at[pl.ds(c * rows, rows)], out_refs[c], sems.at[c])
                for c in range(CHUNKS)
            ],
            CHUNKS,
        )

    return call(
        body,
        [IN_HBM],
        [WHOLE] * CHUNKS,
        [jax.ShapeDtypeStruct((rows, width), tokens.dtype)] * CHUNKS,
        [pltpu.SemaphoreType.DMA((CHUNKS,))],
        vmem=1,
        cost=cost(0, 4 * tokens.size),
    )(hbm(tokens))


def gather_step(held, ways, after):
    moved = {}
    for way in ways:
        value = held[way]
        if after is not None:
            value, _ = lax.optimization_barrier((value, after))
        moved[way] = ring_send(value, way)
    return moved


def accumulate(chunks, first, last, weights, before=None, lead=0):
    rows, depth = chunks[0][0].shape
    width = weights[0].shape[1]
    parts, span = len(weights), last - first
    total = rows * len(chunks)
    final = last == lax.axis_size("head")
    dtype = BF16 if final else F32
    pieces = [chunk[index] for chunk in chunks for index in range(first, last)]

    def body(*refs):
        piece_refs = refs[: len(pieces)]
        weight_refs = refs[len(pieces) : len(pieces) + parts]
        out_ref, left = refs[-2:]
        for index, ref in enumerate(piece_refs):
            chunk, piece = divmod(index, span)
            left[chunk * rows : (chunk + 1) * rows, piece * depth : (piece + 1) * depth] = ref[...]
        for part in range(parts):
            term = mm(left[...], weight_refs[part][first * depth : last * depth])
            if before is not None:
                term = term + refs[-3][lead + part]
            out_ref[part] = term.astype(dtype)

    aliased = before is not None and not final
    args = [*pieces, *weights] + ([] if before is None else [before])
    return call(
        body,
        [WHOLE] * len(args),
        WHOLE,
        jax.ShapeDtypeStruct((parts, total, width), dtype),
        [pltpu.VMEM((total, span * depth), BF16)],
        vmem=12,
        cost=cost(
            2 * total * span * depth * width * parts,
            2 * span * depth * (total + width * parts) + 8 * total * width * parts,
        ),
        aliases={len(args) - 1: 0} if aliased else None,
    )(*args)


def finish(chunk, piece, weights, sums, filled):
    rows, depth = piece.shape
    width = weights[0].shape[1]
    parts = len(weights)
    where = slice(chunk * rows, (chunk + 1) * rows)

    def body(piece_ref, *refs):
        weight_refs, sum_ref = refs[:parts], refs[parts]
        out_ref, far_ref, near_ref = refs[-3:]
        side = lax.axis_index("tok") % 2
        for part in range(parts):
            term = mm(piece_ref[...], weight_refs[part][-depth:]) + sum_ref[part, where]
            out_ref[part, where] = term.astype(BF16)
            far_ref[part, where] = out_ref[part, where, lanes(1 - side, width // 2)]
            near_ref[part, where] = out_ref[part, where, lanes(side, width // 2)]

    total = sums.shape[1]
    args = [piece, *weights, sums, *filled]
    return call(
        body,
        [WHOLE] * len(args),
        [WHOLE] * 3,
        [
            jax.ShapeDtypeStruct((parts, total, size), BF16)
            for size in (width, width // 2, width // 2)
        ],
        cost=cost(2 * rows * depth * width * parts, 2 * width * parts * (depth + 4 * rows)),
        aliases={len(args) - 3 + index: index for index in range(3)} if filled else None,
    )(*args)


def lanes(head, size):
    return pl.ds(pl.multiple_of(head * size, size), size)


def normed(values):
    values = values.astype(F32)
    scale = lax.rsqrt(jnp.mean(values * values, axis=-1, keepdims=True) + 1e-06)
    return (values * scale).astype(BF16)


def head_grads(kv, rate, fast_gate, fast_up, fast_down, before=None):
    rows = kv.shape[1]
    size, hidden_size = fast_gate.shape[1:]
    count = rate.shape[0]
    heads = count // 2
    whole = kv.shape[2] == count * size

    def body(kv_ref, rate_ref, gate_ref, up_ref, down_ref, *rest):
        rates = rate_ref[...].T
        column = lax.broadcasted_iota(jnp.int32, (rows, count), 1)
        for index in range(heads):
            head = first_head(heads) + index
            mine = jnp.sum(jnp.where(column == head, rates, 0.0), axis=1, keepdims=True)
            lane = lanes(head if whole else index, size)
            knorm = normed(kv_ref[0, :, lane])
            target = (-mine * kv_ref[1, :, lane].astype(F32)).astype(BF16)
            gate_pre = mm(knorm, gate_ref[head].astype(BF16))
            up_pre = mm(knorm, up_ref[head].astype(BF16))
            back = mm(target, down_ref[head].astype(BF16), ((1,), (1,)))
            sigma = sigmoid(gate_pre)
            active = gate_pre * sigma
            first = back * up_pre * (sigma + active * (1.0 - sigma))
            both = jnp.concatenate([first.astype(BF16), (back * active).astype(BF16)], axis=1)
            third = (active * up_pre).astype(BF16)
            pair = mm(knorm, both, ((0,), (0,)))
            terms = (pair[:, :hidden_size], pair[:, hidden_size:], mm(target, third, ((0,), (0,))))
            for part, term in enumerate(terms):
                if before is not None:
                    term = term + rest[0][index, part]
                    rest[-1][index, part] = term.astype(BF16)
                    rest[-2][index, part] = term
                else:
                    rest[-1][index, part] = term

    args = [kv, rate, fast_gate, fast_up, fast_down] + ([] if before is None else [before])
    kinds = [F32] if before is None else [F32, BF16]
    return call(
        body,
        [WHOLE] * len(args),
        [WHOLE] * len(kinds),
        [jax.ShapeDtypeStruct((heads, 3, size, hidden_size), kind) for kind in kinds],
        cost=cost(
            12 * heads * rows * size * hidden_size,
            8 * heads * 3 * size * hidden_size,
            heads * rows * hidden_size,
        ),
    )(*args)


def renew(kept, received, step, fast_gate, fast_up, fast_down, after):
    heads, _, size, hidden_size = kept.shape

    def body(step_ref, kept_ref, gate_ref, up_ref, down_ref, *rest):
        out_ref = rest[-1]
        for index in range(heads):
            head = first_head(heads) + index
            for part in range(3):
                grad = kept_ref[index, part]
                for more in rest[: len(received)]:
                    grad = grad + more[index, part].astype(F32)
                if part < 2:
                    matrix = (gate_ref, up_ref)[part][head]
                    fan = size
                else:
                    matrix = down_ref[head].T
                    fan = hidden_size
                mean_sq = jnp.sum(grad * grad, keepdims=True) / (size * hidden_size)
                scale = step_ref[head] * fan ** (-0.5) * lax.rsqrt(mean_sq + 1e-06)
                out_ref[index, part] = (matrix - scale * grad).astype(BF16)

    return call(
        body,
        [SCALARS] + [WHOLE] * (4 + len(received)) + [AFTER] * len(after),
        WHOLE,
        jax.ShapeDtypeStruct(kept.shape, BF16),
        cost=cost(10 * kept.size, 12 * kept.size),
    )(step, kept, fast_gate, fast_up, fast_down, *received, *after)


def attend_blocks(query, blocks):
    factor = query.shape[-1] ** (-0.5) * LOG2E
    scores = []
    for key, _, allowed in blocks:
        part = mm(query, key, ((1,), (1,))) * factor
        scores.append(part if allowed is None else jnp.where(allowed, part, -1e30))
    tops = [jnp.max(part, axis=-1, keepdims=True) for part in scores]
    top = functools.reduce(jnp.maximum, tops)
    result, total = 0.0, 0.0
    for part, (_, value, _) in zip(scores, blocks):
        weight = jnp.exp2(part - top)
        total = total + jnp.sum(weight, axis=-1, keepdims=True)
        result = result + mm(weight.astype(BF16), value)
    return result, top, total


def halves(rows):
    return [slice(index * rows // 2, (index + 1) * rows // 2) for index in range(2)]


def earlier_blocks(ref, index, lane):
    rows = ref.shape[1]
    row = lax.broadcasted_iota(jnp.int32, (rows // 2, rows // 2), 0)
    col = lax.broadcasted_iota(jnp.int32, (rows // 2, rows // 2), 1)
    blocks = [(ref[0, halves(rows)[index], lane], ref[1, halves(rows)[index], lane], col > row)]
    if index == 0:
        blocks.append((ref[0, halves(rows)[1], lane], ref[1, halves(rows)[1], lane], None))
    return blocks


def attend_own(query, kv, size):
    rows = query.shape[1]
    heads = query.shape[2] // size
    row = (rows // 2, rows // 2)

    def body(q_ref, kv_ref, out_ref, stats_ref):
        alone = lax.axis_index("tok") == 0
        causal = lax.broadcasted_iota(jnp.int32, row, 1) <= lax.broadcasted_iota(jnp.int32, row, 0)
        for index, where in enumerate(halves(rows)):
            for head in range(heads):
                lane = slice(head * size, (head + 1) * size)
                blocks = [
                    (kv_ref[0, keys, lane], kv_ref[1, keys, lane], causal if at == index else None)
                    for at, keys in enumerate(halves(rows)[: index + 1])
                ]
                result, top, total = attend_blocks(q_ref[0, where, lane], blocks)
                share = jnp.where(alone, total, 1.0) if head < heads // 2 else 1.0
                out_ref[where, lane] = result / share
                stats_ref[0, where, lane] = jnp.broadcast_to(top, result.shape)
                stats_ref[1, where, lane] = jnp.broadcast_to(total, result.shape)

    return call(
        body,
        [WHOLE] * 2,
        [WHOLE] * 2,
        [
            jax.ShapeDtypeStruct((rows, heads * size), F32),
            jax.ShapeDtypeStruct((2, rows, heads * size), F32),
        ],
        cost=cost(3 * heads * size * rows * rows, 8 * rows * heads * size, heads * rows * rows),
    )(query, kv)


def merged(summed, before, sums, result, top, total):
    both = jnp.maximum(before, top)
    old, new = jnp.exp2(before - both), jnp.exp2(top - both)
    return (summed * old + result * new) / (sums * old + total * new)


def attend_earlier(summed, stats, query, sources, size):
    rows = query.shape[1]
    heads = sources[0].shape[2] // size

    def body(sum_ref, stats_ref, q_ref, behind_ref, beside_ref, out_ref):
        place = lax.axis_index("tok")

        def add(ref):
            for index, where in enumerate(halves(rows)):
                for at in range(heads):
                    lane = lanes(first_head(heads) + at, size)
                    out_ref[where, lane] = merged(
                        sum_ref[where, lane],
                        stats_ref[0, where, lane],
                        stats_ref[1, where, lane],
                        *attend_blocks(
                            q_ref[0, where, lane],
                            earlier_blocks(ref, index, slice(at * size, (at + 1) * size)),
                        ),
                    )

        pl.when((place > 0) & (place % 2 == 0))(lambda: add(behind_ref))
        pl.when(place % 2 == 1)(lambda: add(beside_ref))

    return call(
        body,
        [WHOLE] * 5,
        WHOLE,
        jax.ShapeDtypeStruct(summed.shape, F32),
        cost=cost(3 * heads * size * rows * rows, 8 * rows * heads * size, heads * rows * rows),
        aliases={0: 0},
    )(summed, stats, query, *sources)


def fast_apply(query, gate, upper, down):
    qnorm = normed(query)
    gate_pre = mm(qnorm, gate)
    hidden = gate_pre * sigmoid(gate_pre) * mm(qnorm, upper)
    return mm(hidden.astype(BF16), down, ((1,), (1,)))


def combine_near(query, attended, nets):
    rows = query.shape[1]
    heads, _, size, hidden_size = nets.shape

    def body(q_ref, attended_ref, net_ref, out_ref):
        for index in range(heads):
            lane = lanes(first_head(heads) + index, size)
            fast = fast_apply(q_ref[0, :, lane], *(net_ref[index, part] for part in range(3)))
            where = slice(index * size, (index + 1) * size)
            out_ref[:, where] = (attended_ref[:, lane] + fast).astype(BF16)

    return call(
        body,
        [WHOLE] * 3,
        WHOLE,
        jax.ShapeDtypeStruct((rows, heads * size), BF16),
        cost=cost(
            6 * heads * rows * size * hidden_size,
            8 * heads * rows * size,
            heads * rows * hidden_size,
        ),
    )(query, attended, nets)


def partial_out(offsets, query, attended, stats, behind, nets, near, w_out, after=()):
    rows = near.shape[0] // lax.axis_size("head")
    heads, _, size, hidden_size = nets.shape
    depth = heads * size
    count = len(offsets)
    width = w_out.shape[1]
    block = width // 8

    def body(q_ref, attended_ref, stats_ref, behind_ref, net_ref, near_ref, w_ref, *refs):
        out_refs, far_ref = refs[len(after) : -1], refs[-1]
        starts = [pl.multiple_of(ring_index(offset) * rows, rows) for offset in offsets]

        def take(ref, lane):
            return jnp.concatenate([ref[pl.ds(start, rows), lane] for start in starts], axis=0)

        row = lax.broadcasted_iota(jnp.int32, (rows, behind.shape[1]), 0)
        row = jnp.concatenate([row + start for start in starts], axis=0)
        col = lax.broadcasted_iota(jnp.int32, row.shape, 1)
        within = (col > row) & (lax.axis_index("tok") > 0)
        for index in range(heads):
            lane = lanes(first_head(heads, True) + index, size)
            where = slice(index * size, (index + 1) * size)
            queries = take(q_ref.at[0], lane)
            fast = fast_apply(queries, *(net_ref[index, part] for part in range(3)))
            seen = merged(
                take(attended_ref, lane),
                take(stats_ref.at[0], lane),
                take(stats_ref.at[1], lane),
                *attend_blocks(queries, [(behind_ref[0, :, where], behind_ref[1, :, where], within)]),
            )
            far_ref[:, where] = (seen + fast).astype(BF16)
        left = take(near_ref, slice(None))
        near_rows = pl.ds(pl.multiple_of(first_head(heads) * size, depth), depth)
        far_rows = pl.ds(pl.multiple_of(first_head(heads, True) * size, depth), depth)
        for column in range(0, width, block):
            result = mm(left, w_ref[near_rows, column : column + block])
            result += mm(far_ref[...], w_ref[far_rows, column : column + block])
            result = result.astype(BF16)
            half, at = divmod(column, width // 2)
            for index in range(count):
                out_refs[2 * index + half][:, at : at + block] = result[
                    index * rows : (index + 1) * rows
                ]

    outs = call(
        body,
        [WHOLE] * 7 + [AFTER] * len(after),
        [WHOLE] * (2 * count),
        [jax.ShapeDtypeStruct((rows, width // 2), BF16)] * (2 * count),
        [pltpu.VMEM((count * rows, depth), BF16)],
        vmem=8,
        cost=cost(4 * count * rows * depth * width, 2 * width * (2 * depth + count * rows)),
    )(query, attended, stats, behind, nets, near, w_out, *after)
    return {offset: tuple(outs[2 * at : 2 * at + 2]) for at, offset in enumerate(offsets)}


def ring_reduce(*shared):
    steps = lax.axis_size("head") // 2
    signed = [sign * step for step in range(steps - 1, 0, -1) for sign in (1, -1)]
    parts = partial_out([steps], *shared) | partial_out(signed[:2], *shared)
    coming = {}
    ordered = ()
    for which in range(2 * steps - 1):
        step, half = steps - (which + 1) // 2, which % 2
        if which % 2 == 0 and 2 <= which <= 2 * (steps - 2):
            later = signed[which : which + 2] + [0] * (which == 2 * (steps - 2))
            parts |= partial_out(later, *shared, tuple(coming.values())[:2])
        terms = []
        for way in (1, -1):
            side = half if way == 1 else 1 - half
            term = parts[steps if step == steps else way * step][side]
            if (way, side) in coming:
                term = (term.astype(F32) + coming[way, side].astype(F32)).astype(BF16)
            terms.append(term)
        ordered = lax.optimization_barrier((*terms, *ordered))[:2]
        for way, term in zip((1, -1), ordered):
            coming[way, half if way == 1 else 1 - half] = ring_send(term, way)
    sides = {1: 1 - half, -1: half}
    totals = add_pair(
        [parts[0][sides[way]] for way in (1, -1)], [coming.pop((way, sides[way])) for way in (1, -1)]
    )
    totals = {sides[way]: total for way, total in zip((1, -1), totals)}
    ends = [totals[side] for side in range(2)]
    for (_, side), more in coming.items():
        ends[side] = ends[side] + more.astype(F32)
    return jnp.concatenate([end.astype(BF16) for end in ends], axis=1)


def add_pair(own, came):
    def body(*refs):
        for index in range(2):
            refs[4 + index][...] = refs[index][...].astype(F32) + refs[2 + index][...].astype(F32)

    return call(
        body,
        [WHOLE] * 4,
        [WHOLE] * 2,
        [jax.ShapeDtypeStruct(value.shape, F32) for value in own],
        cost=cost(0, 64 * own[0].size),
    )(*own, *came)


def swap(value, bit):
    count = lax.axis_size("tok")
    return lax.ppermute(value, "tok", [(index, index ^ bit) for index in range(count)])


def shards(
    tokens, w_query, w_key, w_value, w_out, fast_gate, fast_up, fast_down, token_rate, head_step
):
    local_heads, head_size, _ = fast_gate.shape
    tok_count = lax.axis_size("tok")
    steps = lax.axis_size("head") // 2
    nets = (fast_gate, fast_up, fast_down)
    rate = token_rate.T
    rate_beside = swap(rate, 1)

    own = split_rows(tokens)
    weights = load([w_key, w_value, w_query])
    chunks = [[piece] for piece in own]
    held = [{1: piece, -1: piece} for piece in own]
    sums, done = None, 0
    for step in range(1, steps + 1):
        after = {2: weights[0], 3: (sums, rate_beside)}.get(step)
        for c in range(CHUNKS):
            last = (1,) if c % 2 == 0 else (-1,)
            held[c] = gather_step(held[c], (1, -1) if step < steps else last, after)
            chunks[c] += held[c].values()
        if step > 1:
            known = [chunk[: 2 * step - 1] for chunk in chunks]
            sums = accumulate(known, done, 2 * step - 1, weights, sums)
            done = 2 * step - 1
    filled = ()
    for c in reversed(range(CHUNKS)):
        filled = finish(c, chunks[c][-1], weights[:2], sums, filled)
    kv, far, near = filled
    query = accumulate(chunks, done, 2 * steps, weights[2:], sums, 2)

    behind = lax.ppermute(far, "tok", [(index, index + 1) for index in range(1, tok_count - 1, 2)])
    beside = swap(far, 1)
    (grads,) = head_grads(kv, rate, *nets)
    grads, travel = head_grads(beside, rate_beside, *nets, grads)
    received = []
    for bit in range(1, tok_count.bit_length() - 1):
        if received:
            travel = grads
            for more in received:
                travel = travel + more.astype(F32)
            travel = travel.astype(BF16)
        received.append(swap(travel, 1 << bit))
    attended, stats = attend_own(query, kv, head_size)
    near, _ = lax.optimization_barrier((near, attended))
    behind_far = lax.ppermute(near, "tok", [(index, index + 1) for index in range(tok_count - 1)])
    attended = attend_earlier(attended, stats, query, (behind, beside), head_size)
    mine = renew(grads, received, head_step, *nets, (attended,))
    near = combine_near(query, attended, mine)
    return ring_reduce(query, attended, stats, behind_far, swap(mine, 1), near, w_out)


def solution(mesh):
    placed = (
        P("tok", "head"),
        P(None, "head"),
        P(None, "head"),
        P(None, "head"),
        P("head", None),
        P("head", None, None),
        P("head", None, None),
        P("head", None, None),
        P("tok", "head"),
        P("head"),
    )
    return jax.shard_map(
        shards, mesh=mesh, in_specs=placed, out_specs=P(("tok", "head"), None), check_vma=False
    )
```

```python
import functools

import jax
import jax.numpy as jnp
from jax import lax
from jax.experimental import pallas as pl
from jax.experimental.pallas import tpu as pltpu
from jax.sharding import PartitionSpec as P

WINDOW = 512
CHUNKS = 2
F32 = jnp.float32
BF16 = jnp.bfloat16
LOG2E = 1.4426950408889634


def call(body, in_specs, out_specs, out_shape, scratch=(), vmem=8, cost=None, aliases=None):
    return pl.pallas_call(
        body,
        in_specs=in_specs,
        out_specs=out_specs,
        out_shape=out_shape,
        scratch_shapes=list(scratch),
        input_output_aliases=aliases or {},
        cost_estimate=cost,
        compiler_params=pltpu.CompilerParams(vmem_limit_bytes=vmem * 1024 * 1024),
    )


def cost(flops, moved, exps=0):
    return pl.CostEstimate(flops=int(flops), bytes_accessed=int(moved), transcendentals=int(exps))


WHOLE = pl.BlockSpec(memory_space=pltpu.VMEM)
AFTER = pl.BlockSpec(memory_space=pl.ANY)
SCALARS = pl.BlockSpec(memory_space=pltpu.SMEM)
IN_HBM = pl.BlockSpec(memory_space=pltpu.HBM)


def mm(left, right, dims=((1,), (0,))):
    return lax.dot_general(left, right, (dims, ((), ())), preferred_element_type=F32)


def sigmoid(x):
    return 0.5 * jnp.tanh(0.5 * x) + 0.5


def ring_order(count):
    return list(range(0, count, 2)) + list(range(count - 1, 0, -2))


def ring_send(value, step):
    order = ring_order(lax.axis_size("head"))
    count = len(order)
    return lax.ppermute(
        value, "head", [(order[i], order[(i + step) % count]) for i in range(count)]
    )


def ring_offsets():
    steps = lax.axis_size("head") // 2
    return [0] + [way * step for step in range(1, steps) for way in (-1, 1)] + [steps]


def ring_index(offset):
    count = lax.axis_size("head")
    me = lax.axis_index("head")
    at = lax.rem(jnp.where(me % 2 == 0, me // 2, count - 1 - me // 2) + offset + count, count)
    return jnp.where(at < count // 2, 2 * at, 2 * (count - 1 - at) + 1)


def first_head(heads, other=False):
    side = lax.axis_index("tok") % 2
    return (1 - side if other else side) * heads


def hbm(array):
    return pltpu.with_memory_space_constraint(array, pltpu.HBM)


def run_copies(copies, most):
    for index, copy in enumerate(copies):
        if index >= most:
            copies[index - most].wait()
        copy.start()
    for copy in copies[-most:]:
        copy.wait()


def load(arrays):
    count = len(arrays)
    blocks = len(ring_offsets())
    size = arrays[0].shape[0] // blocks

    def body(*refs):
        out_refs, sems = refs[count:-1], refs[-1]
        starts = [pl.multiple_of(ring_index(offset) * size, size) for offset in ring_offsets()]
        run_copies(
            [
                pltpu.make_async_copy(
                    refs[index].at[pl.ds(starts[block], size)],
                    out_refs[index].at[pl.ds(block * size, size)],
                    sems.at[index, block],
                )
                for block in range(blocks)
                for index in range(count)
            ],
            count * blocks,
        )

    return call(
        body,
        [IN_HBM] * count,
        [WHOLE] * count,
        [jax.ShapeDtypeStruct(array.shape, array.dtype) for array in arrays],
        [pltpu.SemaphoreType.DMA((count, blocks))],
        vmem=1,
        cost=cost(0, sum(4 * array.size for array in arrays)),
    )(*[hbm(array) for array in arrays])


def split_rows(tokens):
    rows, width = tokens.shape[0] // CHUNKS, tokens.shape[1]

    def body(in_ref, *refs):
        out_refs, sems = refs[:-1], refs[-1]
        run_copies(
            [
                pltpu.make_async_copy(in_ref.at[pl.ds(c * rows, rows)], out_refs[c], sems.at[c])
                for c in range(CHUNKS)
            ],
            CHUNKS,
        )

    return call(
        body,
        [IN_HBM],
        [WHOLE] * CHUNKS,
        [jax.ShapeDtypeStruct((rows, width), tokens.dtype)] * CHUNKS,
        [pltpu.SemaphoreType.DMA((CHUNKS,))],
        vmem=1,
        cost=cost(0, 4 * tokens.size),
    )(hbm(tokens))


def gather_step(held, ways, after):
    moved = {}
    for way in ways:
        value = held[way]
        if after is not None:
            value, _ = lax.optimization_barrier((value, after))
        moved[way] = ring_send(value, way)
    return moved


def accumulate(chunks, first, last, weights, before=None, lead=0):
    rows, depth = chunks[0][0].shape
    width = weights[0].shape[1]
    parts, span = len(weights), last - first
    total = rows * len(chunks)
    final = last == lax.axis_size("head")
    dtype = BF16 if final else F32
    pieces = [chunk[index] for chunk in chunks for index in range(first, last)]

    def body(*refs):
        piece_refs = refs[: len(pieces)]
        weight_refs = refs[len(pieces) : len(pieces) + parts]
        out_ref, left = refs[-2:]
        for index, ref in enumerate(piece_refs):
            chunk, piece = divmod(index, span)
            left[chunk * rows : (chunk + 1) * rows, piece * depth : (piece + 1) * depth] = ref[...]
        for part in range(parts):
            term = mm(left[...], weight_refs[part][first * depth : last * depth])
            if before is not None:
                term = term + refs[-3][lead + part]
            out_ref[part] = term.astype(dtype)

    aliased = before is not None and not final
    args = [*pieces, *weights] + ([] if before is None else [before])
    return call(
        body,
        [WHOLE] * len(args),
        WHOLE,
        jax.ShapeDtypeStruct((parts, total, width), dtype),
        [pltpu.VMEM((total, span * depth), BF16)],
        vmem=12,
        cost=cost(
            2 * total * span * depth * width * parts,
            2 * span * depth * (total + width * parts) + 8 * total * width * parts,
        ),
        aliases={len(args) - 1: 0} if aliased else None,
    )(*args)


def finish(chunk, piece, weights, sums, filled):
    rows, depth = piece.shape
    width = weights[0].shape[1]
    parts = len(weights)
    where = slice(chunk * rows, (chunk + 1) * rows)

    def body(piece_ref, *refs):
        weight_refs, sum_ref = refs[:parts], refs[parts]
        out_ref, far_ref, near_ref = refs[-3:]
        side = lax.axis_index("tok") % 2
        for part in range(parts):
            term = mm(piece_ref[...], weight_refs[part][-depth:]) + sum_ref[part, where]
            out_ref[part, where] = term.astype(BF16)
            far_ref[part, where] = out_ref[part, where, lanes(1 - side, width // 2)]
            near_ref[part, where] = out_ref[part, where, lanes(side, width // 2)]

    total = sums.shape[1]
    args = [piece, *weights, sums, *filled]
    return call(
        body,
        [WHOLE] * len(args),
        [WHOLE] * 3,
        [
            jax.ShapeDtypeStruct((parts, total, size), BF16)
            for size in (width, width // 2, width // 2)
        ],
        cost=cost(2 * rows * depth * width * parts, 2 * width * parts * (depth + 4 * rows)),
        aliases={len(args) - 3 + index: index for index in range(3)} if filled else None,
    )(*args)


def lanes(head, size):
    return pl.ds(pl.multiple_of(head * size, size), size)


def normed(values):
    values = values.astype(F32)
    scale = lax.rsqrt(jnp.mean(values * values, axis=-1, keepdims=True) + 1e-06)
    return (values * scale).astype(BF16)


def head_grads(kv, rate, fast_gate, fast_up, fast_down, before=None):
    rows = kv.shape[1]
    size, hidden_size = fast_gate.shape[1:]
    count = rate.shape[0]
    heads = count // 2
    whole = kv.shape[2] == count * size

    def body(kv_ref, rate_ref, gate_ref, up_ref, down_ref, *rest):
        rates = rate_ref[...].T
        column = lax.broadcasted_iota(jnp.int32, (rows, count), 1)
        for index in range(heads):
            head = first_head(heads) + index
            mine = jnp.sum(jnp.where(column == head, rates, 0.0), axis=1, keepdims=True)
            lane = lanes(head if whole else index, size)
            knorm = normed(kv_ref[0, :, lane])
            target = (-mine * kv_ref[1, :, lane].astype(F32)).astype(BF16)
            gate_pre = mm(knorm, gate_ref[head].astype(BF16))
            up_pre = mm(knorm, up_ref[head].astype(BF16))
            back = mm(target, down_ref[head].astype(BF16), ((1,), (1,)))
            sigma = sigmoid(gate_pre)
            active = gate_pre * sigma
            first = back * up_pre * (sigma + active * (1.0 - sigma))
            both = jnp.concatenate([first.astype(BF16), (back * active).astype(BF16)], axis=1)
            third = (active * up_pre).astype(BF16)
            pair = mm(knorm, both, ((0,), (0,)))
            terms = (pair[:, :hidden_size], pair[:, hidden_size:], mm(target, third, ((0,), (0,))))
            for part, term in enumerate(terms):
                if before is not None:
                    term = term + rest[0][index, part]
                    rest[-1][index, part] = term.astype(BF16)
                    rest[-2][index, part] = term
                else:
                    rest[-1][index, part] = term

    args = [kv, rate, fast_gate, fast_up, fast_down] + ([] if before is None else [before])
    kinds = [F32] if before is None else [F32, BF16]
    return call(
        body,
        [WHOLE] * len(args),
        [WHOLE] * len(kinds),
        [jax.ShapeDtypeStruct((heads, 3, size, hidden_size), kind) for kind in kinds],
        cost=cost(
            12 * heads * rows * size * hidden_size,
            8 * heads * 3 * size * hidden_size,
            heads * rows * hidden_size,
        ),
    )(*args)


def renew(kept, received, step, fast_gate, fast_up, fast_down, after):
    heads, _, size, hidden_size = kept.shape

    def body(step_ref, kept_ref, gate_ref, up_ref, down_ref, *rest):
        out_ref = rest[-1]
        for index in range(heads):
            head = first_head(heads) + index
            for part in range(3):
                grad = kept_ref[index, part]
                for more in rest[: len(received)]:
                    grad = grad + more[index, part].astype(F32)
                if part < 2:
                    matrix = (gate_ref, up_ref)[part][head]
                    fan = size
                else:
                    matrix = down_ref[head].T
                    fan = hidden_size
                mean_sq = jnp.sum(grad * grad, keepdims=True) / (size * hidden_size)
                scale = step_ref[head] * fan ** (-0.5) * lax.rsqrt(mean_sq + 1e-06)
                out_ref[index, part] = (matrix - scale * grad).astype(BF16)

    return call(
        body,
        [SCALARS] + [WHOLE] * (4 + len(received)) + [AFTER] * len(after),
        WHOLE,
        jax.ShapeDtypeStruct(kept.shape, BF16),
        cost=cost(10 * kept.size, 12 * kept.size),
    )(step, kept, fast_gate, fast_up, fast_down, *received, *after)


def attend_blocks(query, blocks):
    factor = query.shape[-1] ** (-0.5) * LOG2E
    scores = []
    for key, _, allowed in blocks:
        part = mm(query, key, ((1,), (1,))) * factor
        scores.append(part if allowed is None else jnp.where(allowed, part, -1e30))
    tops = [jnp.max(part, axis=-1, keepdims=True) for part in scores]
    top = functools.reduce(jnp.maximum, tops)
    result, total = 0.0, 0.0
    for part, (_, value, _) in zip(scores, blocks):
        weight = jnp.exp2(part - top)
        total = total + jnp.sum(weight, axis=-1, keepdims=True)
        result = result + mm(weight.astype(BF16), value)
    return result, top, total


def halves(rows):
    return [slice(index * rows // 2, (index + 1) * rows // 2) for index in range(2)]


def earlier_blocks(ref, index, lane):
    rows = ref.shape[1]
    row = lax.broadcasted_iota(jnp.int32, (rows // 2, rows // 2), 0)
    col = lax.broadcasted_iota(jnp.int32, (rows // 2, rows // 2), 1)
    blocks = [(ref[0, halves(rows)[index], lane], ref[1, halves(rows)[index], lane], col > row)]
    if index == 0:
        blocks.append((ref[0, halves(rows)[1], lane], ref[1, halves(rows)[1], lane], None))
    return blocks


def attend_own(query, kv, size):
    rows = query.shape[1]
    heads = query.shape[2] // size
    row = (rows // 2, rows // 2)

    def body(q_ref, kv_ref, out_ref, stats_ref):
        alone = lax.axis_index("tok") == 0
        causal = lax.broadcasted_iota(jnp.int32, row, 1) <= lax.broadcasted_iota(jnp.int32, row, 0)
        for index, where in enumerate(halves(rows)):
            for head in range(heads):
                lane = slice(head * size, (head + 1) * size)
                blocks = [
                    (kv_ref[0, keys, lane], kv_ref[1, keys, lane], causal if at == index else None)
                    for at, keys in enumerate(halves(rows)[: index + 1])
                ]
                result, top, total = attend_blocks(q_ref[0, where, lane], blocks)
                out_ref[where, lane] = result / jnp.where(alone, total, 1.0)
                stats_ref[0, where, lane] = jnp.broadcast_to(top, result.shape)
                stats_ref[1, where, lane] = jnp.broadcast_to(total, result.shape)

    return call(
        body,
        [WHOLE] * 2,
        [WHOLE] * 2,
        [
            jax.ShapeDtypeStruct((rows, heads * size), F32),
            jax.ShapeDtypeStruct((2, rows, heads * size), F32),
        ],
        cost=cost(3 * heads * size * rows * rows, 8 * rows * heads * size, heads * rows * rows),
    )(query, kv)


def attend_earlier(summed, stats, query, sources, other, size, after=()):
    rows = query.shape[1]
    heads = sources[0].shape[2] // size

    def body(sum_ref, stats_ref, q_ref, *refs):
        out_ref = refs[-1]
        place = lax.axis_index("tok")

        def add(ref):
            for index, where in enumerate(halves(rows)):
                for at in range(heads):
                    lane = lanes(first_head(heads, other) + at, size)
                    result, top, total = attend_blocks(
                        q_ref[0, where, lane],
                        earlier_blocks(ref, index, slice(at * size, (at + 1) * size)),
                    )
                    before = stats_ref[0, where, lane]
                    both = jnp.maximum(before, top)
                    old, new = jnp.exp2(before - both), jnp.exp2(top - both)
                    total = stats_ref[1, where, lane] * old + total * new
                    out_ref[where, lane] = (sum_ref[where, lane] * old + result * new) / total

        if len(sources) == 1:
            pl.when(place > 0)(lambda: add(refs[0]))
        else:
            pl.when((place > 0) & (place % 2 == 0))(lambda: add(refs[0]))
            pl.when(place % 2 == 1)(lambda: add(refs[1]))

    return call(
        body,
        [WHOLE] * (3 + len(sources)) + [AFTER] * len(after),
        WHOLE,
        jax.ShapeDtypeStruct(summed.shape, F32),
        cost=cost(3 * heads * size * rows * rows, 8 * rows * heads * size, heads * rows * rows),
        aliases={0: 0},
    )(summed, stats, query, *sources, *after)


def fast_apply(query, gate, upper, down):
    qnorm = normed(query)
    gate_pre = mm(qnorm, gate)
    hidden = gate_pre * sigmoid(gate_pre) * mm(qnorm, upper)
    return mm(hidden.astype(BF16), down, ((1,), (1,)))


def combine_near(query, attended, nets):
    rows = query.shape[1]
    heads, _, size, hidden_size = nets.shape

    def body(q_ref, attended_ref, net_ref, out_ref):
        for index in range(heads):
            lane = lanes(first_head(heads) + index, size)
            fast = fast_apply(q_ref[0, :, lane], *(net_ref[index, part] for part in range(3)))
            where = slice(index * size, (index + 1) * size)
            out_ref[:, where] = (attended_ref[:, lane] + fast).astype(BF16)

    return call(
        body,
        [WHOLE] * 3,
        WHOLE,
        jax.ShapeDtypeStruct((rows, heads * size), BF16),
        cost=cost(
            6 * heads * rows * size * hidden_size,
            8 * heads * rows * size,
            heads * rows * hidden_size,
        ),
    )(query, attended, nets)


def partial_out(offsets, query, attended, nets, near, w_out, after=()):
    rows = near.shape[0] // lax.axis_size("head")
    heads, _, size, hidden_size = nets.shape
    depth = heads * size
    count = len(offsets)
    width = w_out.shape[1]
    block = width // 8

    def body(q_ref, attended_ref, net_ref, near_ref, w_ref, *refs):
        out_refs, far_ref = refs[len(after) : -1], refs[-1]
        starts = [pl.multiple_of(ring_index(offset) * rows, rows) for offset in offsets]

        def take(ref, lane):
            return jnp.concatenate([ref[pl.ds(start, rows), lane] for start in starts], axis=0)

        for index in range(heads):
            lane = lanes(first_head(heads, True) + index, size)
            fast = fast_apply(
                take(q_ref.at[0], lane), *(net_ref[index, part] for part in range(3))
            )
            where = slice(index * size, (index + 1) * size)
            far_ref[:, where] = (take(attended_ref, lane) + fast).astype(BF16)
        left = take(near_ref, slice(None))
        near_rows = pl.ds(pl.multiple_of(first_head(heads) * size, depth), depth)
        far_rows = pl.ds(pl.multiple_of(first_head(heads, True) * size, depth), depth)
        for column in range(0, width, block):
            result = mm(left, w_ref[near_rows, column : column + block])
            result += mm(far_ref[...], w_ref[far_rows, column : column + block])
            result = result.astype(BF16)
            half, at = divmod(column, width // 2)
            for index in range(count):
                out_refs[2 * index + half][:, at : at + block] = result[
                    index * rows : (index + 1) * rows
                ]

    outs = call(
        body,
        [WHOLE] * 5 + [AFTER] * len(after),
        [WHOLE] * (2 * count),
        [jax.ShapeDtypeStruct((rows, width // 2), BF16)] * (2 * count),
        [pltpu.VMEM((count * rows, depth), BF16)],
        vmem=8,
        cost=cost(4 * count * rows * depth * width, 2 * width * (2 * depth + count * rows)),
    )(query, attended, nets, near, w_out, *after)
    return {offset: tuple(outs[2 * at : 2 * at + 2]) for at, offset in enumerate(offsets)}


def ring_reduce(query, attended, nets, near, w_out):
    steps = lax.axis_size("head") // 2
    signed = [sign * step for step in range(steps - 1, 0, -1) for sign in (1, -1)]
    shared = (query, attended, nets, near, w_out)
    parts = partial_out([steps], *shared) | partial_out(signed[:2], *shared)
    coming = {}
    ordered = ()
    for which in range(2 * steps - 1):
        step, half = steps - (which + 1) // 2, which % 2
        if which % 2 == 0 and 2 <= which <= 2 * (steps - 2):
            later = signed[which : which + 2] + [0] * (which == 2 * (steps - 2))
            parts |= partial_out(later, *shared, tuple(coming.values())[:2])
        terms = []
        for way in (1, -1):
            side = half if way == 1 else 1 - half
            term = parts[steps if step == steps else way * step][side]
            if (way, side) in coming:
                term = (term.astype(F32) + coming[way, side].astype(F32)).astype(BF16)
            terms.append(term)
        ordered = lax.optimization_barrier((*terms, *ordered))[:2]
        for way, term in zip((1, -1), ordered):
            coming[way, half if way == 1 else 1 - half] = ring_send(term, way)
    sides = {1: 1 - half, -1: half}
    totals = add_pair(
        [parts[0][sides[way]] for way in (1, -1)], [coming.pop((way, sides[way])) for way in (1, -1)]
    )
    totals = {sides[way]: total for way, total in zip((1, -1), totals)}
    ends = [totals[side] for side in range(2)]
    for (_, side), more in coming.items():
        ends[side] = ends[side] + more.astype(F32)
    return jnp.concatenate([end.astype(BF16) for end in ends], axis=1)


def add_pair(own, came):
    def body(*refs):
        for index in range(2):
            refs[4 + index][...] = refs[index][...].astype(F32) + refs[2 + index][...].astype(F32)

    return call(
        body,
        [WHOLE] * 4,
        [WHOLE] * 2,
        [jax.ShapeDtypeStruct(value.shape, F32) for value in own],
        cost=cost(0, 64 * own[0].size),
    )(*own, *came)


def swap(value, bit):
    count = lax.axis_size("tok")
    return lax.ppermute(value, "tok", [(index, index ^ bit) for index in range(count)])


def shards(
    tokens, w_query, w_key, w_value, w_out, fast_gate, fast_up, fast_down, token_rate, head_step
):
    local_heads, head_size, _ = fast_gate.shape
    tok_count = lax.axis_size("tok")
    steps = lax.axis_size("head") // 2
    nets = (fast_gate, fast_up, fast_down)
    rate = token_rate.T
    rate_beside = swap(rate, 1)

    own = split_rows(tokens)
    weights = load([w_key, w_value, w_query])
    chunks = [[piece] for piece in own]
    held = [{1: piece, -1: piece} for piece in own]
    sums, done = None, 0
    for step in range(1, steps + 1):
        after = {2: weights[0], 3: (sums, rate_beside)}.get(step)
        for c in range(CHUNKS):
            last = (1,) if c % 2 == 0 else (-1,)
            held[c] = gather_step(held[c], (1, -1) if step < steps else last, after)
            chunks[c] += held[c].values()
        if step > 1:
            known = [chunk[: 2 * step - 1] for chunk in chunks]
            sums = accumulate(known, done, 2 * step - 1, weights, sums)
            done = 2 * step - 1
    filled = ()
    for c in reversed(range(CHUNKS)):
        filled = finish(c, chunks[c][-1], weights[:2], sums, filled)
    kv, far, near = filled
    query = accumulate(chunks, done, 2 * steps, weights[2:], sums, 2)

    behind = lax.ppermute(far, "tok", [(index, index + 1) for index in range(1, tok_count - 1, 2)])
    beside = swap(far, 1)
    (grads,) = head_grads(kv, rate, *nets)
    grads, travel = head_grads(beside, rate_beside, *nets, grads)
    received = []
    for bit in range(1, tok_count.bit_length() - 1):
        if received:
            travel = grads
            for more in received:
                travel = travel + more.astype(F32)
            travel = travel.astype(BF16)
        received.append(swap(travel, 1 << bit))
    attended, stats = attend_own(query, kv, head_size)
    near, _ = lax.optimization_barrier((near, attended))
    behind_far = lax.ppermute(near, "tok", [(index, index + 1) for index in range(tok_count - 1)])
    attended = attend_earlier(attended, stats, query, (behind, beside), False, head_size)
    mine = renew(grads, received, head_step, *nets, (attended,))
    near = combine_near(query, attended, mine)
    attended = attend_earlier(attended, stats, query, (behind_far,), True, head_size, (near,))
    return ring_reduce(query, attended, swap(mine, 1), near, w_out)


def solution(mesh):
    placed = (
        P("tok", "head"),
        P(None, "head"),
        P(None, "head"),
        P(None, "head"),
        P("head", None),
        P("head", None, None),
        P("head", None, None),
        P("head", None, None),
        P("tok", "head"),
        P("head"),
    )
    return jax.shard_map(
        shards, mesh=mesh, in_specs=placed, out_specs=P(("tok", "head"), None), check_vma=False
    )
```

```python
import functools

import jax
import jax.numpy as jnp
from jax import lax
from jax.experimental import pallas as pl
from jax.experimental.pallas import tpu as pltpu
from jax.sharding import PartitionSpec as P

WINDOW = 512
CHUNKS = 2
F32 = jnp.float32
BF16 = jnp.bfloat16
LOG2E = 1.4426950408889634


def call(body, in_specs, out_specs, out_shape, scratch=(), vmem=8, cost=None, aliases=None):
    return pl.pallas_call(
        body,
        in_specs=in_specs,
        out_specs=out_specs,
        out_shape=out_shape,
        scratch_shapes=list(scratch),
        input_output_aliases=aliases or {},
        cost_estimate=cost,
        compiler_params=pltpu.CompilerParams(vmem_limit_bytes=vmem * 1024 * 1024),
    )


def cost(flops, moved, exps=0):
    return pl.CostEstimate(flops=int(flops), bytes_accessed=int(moved), transcendentals=int(exps))


WHOLE = pl.BlockSpec(memory_space=pltpu.VMEM)
AFTER = pl.BlockSpec(memory_space=pl.ANY)
SCALARS = pl.BlockSpec(memory_space=pltpu.SMEM)
IN_HBM = pl.BlockSpec(memory_space=pltpu.HBM)


def mm(left, right, dims=((1,), (0,))):
    return lax.dot_general(left, right, (dims, ((), ())), preferred_element_type=F32)


def sigmoid(x):
    return 0.5 * jnp.tanh(0.5 * x) + 0.5


def ring_order(count):
    return list(range(0, count, 2)) + list(range(count - 1, 0, -2))


def ring_send(value, step):
    order = ring_order(lax.axis_size("head"))
    count = len(order)
    return lax.ppermute(
        value, "head", [(order[i], order[(i + step) % count]) for i in range(count)]
    )


def ring_offsets():
    steps = lax.axis_size("head") // 2
    return [0] + [way * step for step in range(1, steps) for way in (-1, 1)] + [steps]


def ring_index(offset):
    count = lax.axis_size("head")
    me = lax.axis_index("head")
    at = lax.rem(jnp.where(me % 2 == 0, me // 2, count - 1 - me // 2) + offset + count, count)
    return jnp.where(at < count // 2, 2 * at, 2 * (count - 1 - at) + 1)


def first_head(heads, other=False):
    side = lax.axis_index("tok") % 2
    return (1 - side if other else side) * heads


def hbm(array):
    return pltpu.with_memory_space_constraint(array, pltpu.HBM)


def run_copies(copies, most):
    for index, copy in enumerate(copies):
        if index >= most:
            copies[index - most].wait()
        copy.start()
    for copy in copies[-most:]:
        copy.wait()


def load(arrays):
    count = len(arrays)
    blocks = len(ring_offsets())
    size = arrays[0].shape[0] // blocks

    def body(*refs):
        out_refs, sems = refs[count:-1], refs[-1]
        starts = [pl.multiple_of(ring_index(offset) * size, size) for offset in ring_offsets()]
        run_copies(
            [
                pltpu.make_async_copy(
                    refs[index].at[pl.ds(starts[block], size)],
                    out_refs[index].at[pl.ds(block * size, size)],
                    sems.at[index, block],
                )
                for block in range(blocks)
                for index in range(count)
            ],
            count * blocks,
        )

    return call(
        body,
        [IN_HBM] * count,
        [WHOLE] * count,
        [jax.ShapeDtypeStruct(array.shape, array.dtype) for array in arrays],
        [pltpu.SemaphoreType.DMA((count, blocks))],
        vmem=1,
        cost=cost(0, sum(4 * array.size for array in arrays)),
    )(*[hbm(array) for array in arrays])


def split_rows(tokens):
    rows, width = tokens.shape[0] // CHUNKS, tokens.shape[1]

    def body(in_ref, *refs):
        out_refs, sems = refs[:-1], refs[-1]
        run_copies(
            [
                pltpu.make_async_copy(in_ref.at[pl.ds(c * rows, rows)], out_refs[c], sems.at[c])
                for c in range(CHUNKS)
            ],
            CHUNKS,
        )

    return call(
        body,
        [IN_HBM],
        [WHOLE] * CHUNKS,
        [jax.ShapeDtypeStruct((rows, width), tokens.dtype)] * CHUNKS,
        [pltpu.SemaphoreType.DMA((CHUNKS,))],
        vmem=1,
        cost=cost(0, 4 * tokens.size),
    )(hbm(tokens))


def gather_step(held, ways, after):
    moved = {}
    for way in ways:
        value = held[way]
        if after is not None:
            value, _ = lax.optimization_barrier((value, after))
        moved[way] = ring_send(value, way)
    return moved


def accumulate(chunks, first, last, weights, before=None, lead=0):
    rows, depth = chunks[0][0].shape
    width = weights[0].shape[1]
    parts, span = len(weights), last - first
    total = rows * len(chunks)
    final = last == lax.axis_size("head")
    dtype = BF16 if final else F32
    pieces = [chunk[index] for chunk in chunks for index in range(first, last)]

    def body(*refs):
        piece_refs = refs[: len(pieces)]
        weight_refs = refs[len(pieces) : len(pieces) + parts]
        out_ref, left = refs[-2:]
        for index, ref in enumerate(piece_refs):
            chunk, piece = divmod(index, span)
            left[chunk * rows : (chunk + 1) * rows, piece * depth : (piece + 1) * depth] = ref[...]
        for part in range(parts):
            term = mm(left[...], weight_refs[part][first * depth : last * depth])
            if before is not None:
                term = term + refs[-3][lead + part]
            out_ref[part] = term.astype(dtype)

    aliased = before is not None and not final
    args = [*pieces, *weights] + ([] if before is None else [before])
    return call(
        body,
        [WHOLE] * len(args),
        WHOLE,
        jax.ShapeDtypeStruct((parts, total, width), dtype),
        [pltpu.VMEM((total, span * depth), BF16)],
        vmem=12,
        cost=cost(
            2 * total * span * depth * width * parts,
            2 * span * depth * (total + width * parts) + 8 * total * width * parts,
        ),
        aliases={len(args) - 1: 0} if aliased else None,
    )(*args)


def finish(chunk, piece, weights, sums, filled):
    rows, depth = piece.shape
    width = weights[0].shape[1]
    parts = len(weights)
    where = slice(chunk * rows, (chunk + 1) * rows)

    def body(piece_ref, *refs):
        weight_refs, sum_ref = refs[:parts], refs[parts]
        out_ref, far_ref, near_ref = refs[-3:]
        side = lax.axis_index("tok") % 2
        for part in range(parts):
            term = mm(piece_ref[...], weight_refs[part][-depth:]) + sum_ref[part, where]
            out_ref[part, where] = term.astype(BF16)
            far_ref[part, where] = out_ref[part, where, lanes(1 - side, width // 2)]
            near_ref[part, where] = out_ref[part, where, lanes(side, width // 2)]

    total = sums.shape[1]
    args = [piece, *weights, sums, *filled]
    return call(
        body,
        [WHOLE] * len(args),
        [WHOLE] * 3,
        [
            jax.ShapeDtypeStruct((parts, total, size), BF16)
            for size in (width, width // 2, width // 2)
        ],
        cost=cost(2 * rows * depth * width * parts, 2 * width * parts * (depth + 4 * rows)),
        aliases={len(args) - 3 + index: index for index in range(3)} if filled else None,
    )(*args)


def lanes(head, size):
    return pl.ds(pl.multiple_of(head * size, size), size)


def normed(values):
    values = values.astype(F32)
    scale = lax.rsqrt(jnp.mean(values * values, axis=-1, keepdims=True) + 1e-06)
    return (values * scale).astype(BF16)


def head_grads(kv, rate, fast_gate, fast_up, fast_down, before=None):
    rows = kv.shape[1]
    size, hidden_size = fast_gate.shape[1:]
    count = rate.shape[0]
    heads = count // 2
    whole = kv.shape[2] == count * size

    def body(kv_ref, rate_ref, gate_ref, up_ref, down_ref, *rest):
        rates = rate_ref[...].T
        column = lax.broadcasted_iota(jnp.int32, (rows, count), 1)
        for index in range(heads):
            head = first_head(heads) + index
            mine = jnp.sum(jnp.where(column == head, rates, 0.0), axis=1, keepdims=True)
            lane = lanes(head if whole else index, size)
            knorm = normed(kv_ref[0, :, lane])
            target = (-mine * kv_ref[1, :, lane].astype(F32)).astype(BF16)
            gate_pre = mm(knorm, gate_ref[head].astype(BF16))
            up_pre = mm(knorm, up_ref[head].astype(BF16))
            back = mm(target, down_ref[head].astype(BF16), ((1,), (1,)))
            sigma = sigmoid(gate_pre)
            active = gate_pre * sigma
            first = back * up_pre * (sigma + active * (1.0 - sigma))
            both = jnp.concatenate([first.astype(BF16), (back * active).astype(BF16)], axis=1)
            third = (active * up_pre).astype(BF16)
            pair = mm(knorm, both, ((0,), (0,)))
            terms = (pair[:, :hidden_size], pair[:, hidden_size:], mm(target, third, ((0,), (0,))))
            for part, term in enumerate(terms):
                if before is not None:
                    term = term + rest[0][index, part]
                    rest[-1][index, part] = term.astype(BF16)
                    rest[-2][index, part] = term
                else:
                    rest[-1][index, part] = term

    args = [kv, rate, fast_gate, fast_up, fast_down] + ([] if before is None else [before])
    kinds = [F32] if before is None else [F32, BF16]
    return call(
        body,
        [WHOLE] * len(args),
        [WHOLE] * len(kinds),
        [jax.ShapeDtypeStruct((heads, 3, size, hidden_size), kind) for kind in kinds],
        cost=cost(
            12 * heads * rows * size * hidden_size,
            8 * heads * 3 * size * hidden_size,
            heads * rows * hidden_size,
        ),
    )(*args)


def renew(kept, received, step, fast_gate, fast_up, fast_down, after):
    heads, _, size, hidden_size = kept.shape

    def body(step_ref, kept_ref, gate_ref, up_ref, down_ref, *rest):
        out_ref = rest[-1]
        for index in range(heads):
            head = first_head(heads) + index
            for part in range(3):
                grad = kept_ref[index, part]
                for more in rest[: len(received)]:
                    grad = grad + more[index, part].astype(F32)
                if part < 2:
                    matrix = (gate_ref, up_ref)[part][head]
                    fan = size
                else:
                    matrix = down_ref[head].T
                    fan = hidden_size
                mean_sq = jnp.sum(grad * grad, keepdims=True) / (size * hidden_size)
                scale = step_ref[head] * fan ** (-0.5) * lax.rsqrt(mean_sq + 1e-06)
                out_ref[index, part] = (matrix - scale * grad).astype(BF16)

    return call(
        body,
        [SCALARS] + [WHOLE] * (4 + len(received)) + [AFTER] * len(after),
        WHOLE,
        jax.ShapeDtypeStruct(kept.shape, BF16),
        cost=cost(10 * kept.size, 12 * kept.size),
    )(step, kept, fast_gate, fast_up, fast_down, *received, *after)


def attend_blocks(query, blocks):
    factor = query.shape[-1] ** (-0.5) * LOG2E
    scores = []
    for key, _, allowed in blocks:
        part = mm(query, key, ((1,), (1,))) * factor
        scores.append(part if allowed is None else jnp.where(allowed, part, -1e30))
    tops = [jnp.max(part, axis=-1, keepdims=True) for part in scores]
    top = functools.reduce(jnp.maximum, tops)
    result, total = 0.0, 0.0
    for part, (_, value, _) in zip(scores, blocks):
        weight = jnp.exp2(part - top)
        total = total + jnp.sum(weight, axis=-1, keepdims=True)
        result = result + mm(weight.astype(BF16), value)
    return result, top, total


def halves(rows):
    return [slice(index * rows // 2, (index + 1) * rows // 2) for index in range(2)]


def earlier_blocks(ref, index, lane):
    rows = ref.shape[1]
    row = lax.broadcasted_iota(jnp.int32, (rows // 2, rows // 2), 0)
    col = lax.broadcasted_iota(jnp.int32, (rows // 2, rows // 2), 1)
    blocks = [(ref[0, halves(rows)[index], lane], ref[1, halves(rows)[index], lane], col > row)]
    if index == 0:
        blocks.append((ref[0, halves(rows)[1], lane], ref[1, halves(rows)[1], lane], None))
    return blocks


def attend_own(query, kv, size):
    rows = query.shape[1]
    heads = query.shape[2] // size
    row = (rows // 2, rows // 2)

    def body(q_ref, kv_ref, out_ref, stats_ref):
        alone = lax.axis_index("tok") == 0
        causal = lax.broadcasted_iota(jnp.int32, row, 1) <= lax.broadcasted_iota(jnp.int32, row, 0)
        for index, where in enumerate(halves(rows)):
            for head in range(heads):
                lane = slice(head * size, (head + 1) * size)
                blocks = [
                    (kv_ref[0, keys, lane], kv_ref[1, keys, lane], causal if at == index else None)
                    for at, keys in enumerate(halves(rows)[: index + 1])
                ]
                result, top, total = attend_blocks(q_ref[0, where, lane], blocks)
                out_ref[where, lane] = result / jnp.where(alone, total, 1.0)
                stats_ref[0, where, lane] = jnp.broadcast_to(top, result.shape)
                stats_ref[1, where, lane] = jnp.broadcast_to(total, result.shape)

    return call(
        body,
        [WHOLE] * 2,
        [WHOLE] * 2,
        [
            jax.ShapeDtypeStruct((rows, heads * size), F32),
            jax.ShapeDtypeStruct((2, rows, heads * size), F32),
        ],
        cost=cost(3 * heads * size * rows * rows, 8 * rows * heads * size, heads * rows * rows),
    )(query, kv)


def attend_earlier(summed, stats, query, sources, other, size, after=()):
    rows = query.shape[1]
    heads = next(iter(sources.values())).shape[2] // size

    def body(sum_ref, stats_ref, q_ref, *refs):
        out_ref = refs[-1]
        place = lax.axis_index("tok")

        def add(ref):
            for index, where in enumerate(halves(rows)):
                for at in range(heads):
                    lane = lanes(first_head(heads, other) + at, size)
                    result, top, total = attend_blocks(
                        q_ref[0, where, lane],
                        earlier_blocks(ref, index, slice(at * size, (at + 1) * size)),
                    )
                    before = stats_ref[0, where, lane]
                    both = jnp.maximum(before, top)
                    old, new = jnp.exp2(before - both), jnp.exp2(top - both)
                    total = stats_ref[1, where, lane] * old + total * new
                    out_ref[where, lane] = (sum_ref[where, lane] * old + result * new) / total

        for core, ref in zip(sources, refs):
            pl.when((place > 0) & (place % 2 == core))(functools.partial(add, ref))

    return call(
        body,
        [WHOLE] * (3 + len(sources)) + [AFTER] * len(after),
        WHOLE,
        jax.ShapeDtypeStruct(summed.shape, F32),
        cost=cost(3 * heads * size * rows * rows, 8 * rows * heads * size, heads * rows * rows),
        aliases={0: 0},
    )(summed, stats, query, *sources.values(), *after)


def fast_apply(query, gate, upper, down):
    qnorm = normed(query)
    gate_pre = mm(qnorm, gate)
    hidden = gate_pre * sigmoid(gate_pre) * mm(qnorm, upper)
    return mm(hidden.astype(BF16), down, ((1,), (1,)))


def combine_near(query, attended, nets):
    rows = query.shape[1]
    heads, _, size, hidden_size = nets.shape

    def body(q_ref, attended_ref, net_ref, out_ref):
        for index in range(heads):
            lane = lanes(first_head(heads) + index, size)
            fast = fast_apply(q_ref[0, :, lane], *(net_ref[index, part] for part in range(3)))
            where = slice(index * size, (index + 1) * size)
            out_ref[:, where] = (attended_ref[:, lane] + fast).astype(BF16)

    return call(
        body,
        [WHOLE] * 3,
        WHOLE,
        jax.ShapeDtypeStruct((rows, heads * size), BF16),
        cost=cost(
            6 * heads * rows * size * hidden_size,
            8 * heads * rows * size,
            heads * rows * hidden_size,
        ),
    )(query, attended, nets)


def partial_out(offsets, query, attended, nets, near, w_out, after=()):
    rows = near.shape[0] // lax.axis_size("head")
    heads, _, size, hidden_size = nets.shape
    depth = heads * size
    count = len(offsets)
    width = w_out.shape[1]
    block = width // 8

    def body(q_ref, attended_ref, net_ref, near_ref, w_ref, *refs):
        out_refs, far_ref = refs[len(after) : -1], refs[-1]
        starts = [pl.multiple_of(ring_index(offset) * rows, rows) for offset in offsets]

        def take(ref, lane):
            return jnp.concatenate([ref[pl.ds(start, rows), lane] for start in starts], axis=0)

        for index in range(heads):
            lane = lanes(first_head(heads, True) + index, size)
            fast = fast_apply(
                take(q_ref.at[0], lane), *(net_ref[index, part] for part in range(3))
            )
            where = slice(index * size, (index + 1) * size)
            far_ref[:, where] = (take(attended_ref, lane) + fast).astype(BF16)
        left = take(near_ref, slice(None))
        near_rows = pl.ds(pl.multiple_of(first_head(heads) * size, depth), depth)
        far_rows = pl.ds(pl.multiple_of(first_head(heads, True) * size, depth), depth)
        for column in range(0, width, block):
            result = mm(left, w_ref[near_rows, column : column + block])
            result += mm(far_ref[...], w_ref[far_rows, column : column + block])
            result = result.astype(BF16)
            half, at = divmod(column, width // 2)
            for index in range(count):
                out_refs[2 * index + half][:, at : at + block] = result[
                    index * rows : (index + 1) * rows
                ]

    outs = call(
        body,
        [WHOLE] * 5 + [AFTER] * len(after),
        [WHOLE] * (2 * count),
        [jax.ShapeDtypeStruct((rows, width // 2), BF16)] * (2 * count),
        [pltpu.VMEM((count * rows, depth), BF16)],
        vmem=8,
        cost=cost(4 * count * rows * depth * width, 2 * width * (2 * depth + count * rows)),
    )(query, attended, nets, near, w_out, *after)
    return {offset: tuple(outs[2 * at : 2 * at + 2]) for at, offset in enumerate(offsets)}


def ring_reduce(query, attended, nets, near, w_out):
    steps = lax.axis_size("head") // 2
    signed = [sign * step for step in range(steps - 1, 0, -1) for sign in (1, -1)]
    shared = (query, attended, nets, near, w_out)
    parts = partial_out([steps], *shared) | partial_out(signed[:2], *shared)
    coming = {}
    ordered = ()
    for which in range(2 * steps - 1):
        step, half = steps - (which + 1) // 2, which % 2
        if which % 2 == 0 and 2 <= which <= 2 * (steps - 2):
            later = signed[which : which + 2] + [0] * (which == 2 * (steps - 2))
            parts |= partial_out(later, *shared, tuple(coming.values())[:2])
        terms = []
        for way in (1, -1):
            side = half if way == 1 else 1 - half
            term = parts[steps if step == steps else way * step][side]
            if (way, side) in coming:
                term = (term.astype(F32) + coming[way, side].astype(F32)).astype(BF16)
            terms.append(term)
        ordered = lax.optimization_barrier((*terms, *ordered))[:2]
        for way, term in zip((1, -1), ordered):
            coming[way, half if way == 1 else 1 - half] = ring_send(term, way)
    sides = {1: 1 - half, -1: half}
    totals = add_pair(
        [parts[0][sides[way]] for way in (1, -1)], [coming.pop((way, sides[way])) for way in (1, -1)]
    )
    totals = {sides[way]: total for way, total in zip((1, -1), totals)}
    ends = [totals[side] for side in range(2)]
    for (_, side), more in coming.items():
        ends[side] = ends[side] + more.astype(F32)
    return jnp.concatenate([end.astype(BF16) for end in ends], axis=1)


def add_pair(own, came):
    def body(*refs):
        for index in range(2):
            refs[4 + index][...] = refs[index][...].astype(F32) + refs[2 + index][...].astype(F32)

    return call(
        body,
        [WHOLE] * 4,
        [WHOLE] * 2,
        [jax.ShapeDtypeStruct(value.shape, F32) for value in own],
        cost=cost(0, 64 * own[0].size),
    )(*own, *came)


def swap(value, bit):
    count = lax.axis_size("tok")
    return lax.ppermute(value, "tok", [(index, index ^ bit) for index in range(count)])


def shards(
    tokens, w_query, w_key, w_value, w_out, fast_gate, fast_up, fast_down, token_rate, head_step
):
    local_heads, head_size, _ = fast_gate.shape
    tok_count = lax.axis_size("tok")
    steps = lax.axis_size("head") // 2
    nets = (fast_gate, fast_up, fast_down)
    rate = token_rate.T
    rate_beside = swap(rate, 1)

    own = split_rows(tokens)
    weights = load([w_key, w_value, w_query])
    chunks = [[piece] for piece in own]
    held = [{1: piece, -1: piece} for piece in own]
    sums, done = None, 0
    for step in range(1, steps + 1):
        after = {2: weights[0], 3: (sums, rate_beside)}.get(step)
        for c in range(CHUNKS):
            last = (1,) if c % 2 == 0 else (-1,)
            held[c] = gather_step(held[c], (1, -1) if step < steps else last, after)
            chunks[c] += held[c].values()
        if step > 1:
            known = [chunk[: 2 * step - 1] for chunk in chunks]
            sums = accumulate(known, done, 2 * step - 1, weights, sums)
            done = 2 * step - 1
    filled = ()
    for c in reversed(range(CHUNKS)):
        filled = finish(c, chunks[c][-1], weights[:2], sums, filled)
    kv, far, near = filled
    query = accumulate(chunks, done, 2 * steps, weights[2:], sums, 2)

    behind = lax.ppermute(far, "tok", [(index, index + 1) for index in range(1, tok_count - 1, 2)])
    beside = swap(far, 1)
    (grads,) = head_grads(kv, rate, *nets)
    grads, travel = head_grads(beside, rate_beside, *nets, grads)
    received = []
    for bit in range(1, tok_count.bit_length() - 1):
        if received:
            travel = grads
            for more in received:
                travel = travel + more.astype(F32)
            travel = travel.astype(BF16)
        received.append(swap(travel, 1 << bit))
    attended, stats = attend_own(query, kv, head_size)
    early, _ = lax.optimization_barrier((near, grads))
    late, _ = lax.optimization_barrier((near, attended))
    beside_far = lax.ppermute(early, "tok", [(index, index + 1) for index in range(0, tok_count, 2)])
    behind_far = lax.ppermute(late, "tok", [(index, index + 1) for index in range(1, tok_count - 1, 2)])
    nearer = {0: behind, 1: beside}
    attended = attend_earlier(attended, stats, query, nearer, False, head_size)
    attended = attend_earlier(attended, stats, query, {1: beside_far}, True, head_size)
    mine = renew(grads, received, head_step, *nets, (attended,))
    near = combine_near(query, attended, mine)
    attended = attend_earlier(attended, stats, query, {0: behind_far}, True, head_size, (near,))
    return ring_reduce(query, attended, swap(mine, 1), near, w_out)


def solution(mesh):
    placed = (
        P("tok", "head"),
        P(None, "head"),
        P(None, "head"),
        P(None, "head"),
        P("head", None),
        P("head", None, None),
        P("head", None, None),
        P("head", None, None),
        P("tok", "head"),
        P("head"),
    )
    return jax.shard_map(
        shards, mesh=mesh, in_specs=placed, out_specs=P(("tok", "head"), None), check_vma=False
    )
```

```python
import functools

import jax
import jax.numpy as jnp
from jax import lax
from jax.experimental import pallas as pl
from jax.experimental.pallas import tpu as pltpu
from jax.sharding import PartitionSpec as P

WINDOW = 512
CHUNKS = 2
F32 = jnp.float32
BF16 = jnp.bfloat16
LOG2E = 1.4426950408889634


def call(body, in_specs, out_specs, out_shape, scratch=(), vmem=8, cost=None, aliases=None):
    return pl.pallas_call(
        body,
        in_specs=in_specs,
        out_specs=out_specs,
        out_shape=out_shape,
        scratch_shapes=list(scratch),
        input_output_aliases=aliases or {},
        cost_estimate=cost,
        compiler_params=pltpu.CompilerParams(vmem_limit_bytes=vmem * 1024 * 1024),
    )


def cost(flops, moved, exps=0):
    return pl.CostEstimate(flops=int(flops), bytes_accessed=int(moved), transcendentals=int(exps))


WHOLE = pl.BlockSpec(memory_space=pltpu.VMEM)
AFTER = pl.BlockSpec(memory_space=pl.ANY)
SCALARS = pl.BlockSpec(memory_space=pltpu.SMEM)
IN_HBM = pl.BlockSpec(memory_space=pltpu.HBM)


def mm(left, right, dims=((1,), (0,))):
    return lax.dot_general(left, right, (dims, ((), ())), preferred_element_type=F32)


def sigmoid(x):
    return 0.5 * jnp.tanh(0.5 * x) + 0.5


def ring_order(count):
    return list(range(0, count, 2)) + list(range(count - 1, 0, -2))


def ring_send(value, step):
    order = ring_order(lax.axis_size("head"))
    count = len(order)
    return lax.ppermute(
        value, "head", [(order[i], order[(i + step) % count]) for i in range(count)]
    )


def ring_offsets():
    steps = lax.axis_size("head") // 2
    return [0] + [way * step for step in range(1, steps) for way in (-1, 1)] + [steps]


def ring_index(offset):
    count = lax.axis_size("head")
    me = lax.axis_index("head")
    at = lax.rem(jnp.where(me % 2 == 0, me // 2, count - 1 - me // 2) + offset + count, count)
    return jnp.where(at < count // 2, 2 * at, 2 * (count - 1 - at) + 1)


def first_head(heads, other=False):
    side = lax.axis_index("tok") % 2
    return (1 - side if other else side) * heads


def hbm(array):
    return pltpu.with_memory_space_constraint(array, pltpu.HBM)


def run_copies(copies, most):
    for index, copy in enumerate(copies):
        if index >= most:
            copies[index - most].wait()
        copy.start()
    for copy in copies[-most:]:
        copy.wait()


def load(arrays):
    count = len(arrays)
    blocks = len(ring_offsets())
    size = arrays[0].shape[0] // blocks

    def body(*refs):
        out_refs, sems = refs[count:-1], refs[-1]
        starts = [pl.multiple_of(ring_index(offset) * size, size) for offset in ring_offsets()]
        run_copies(
            [
                pltpu.make_async_copy(
                    refs[index].at[pl.ds(starts[block], size)],
                    out_refs[index].at[pl.ds(block * size, size)],
                    sems.at[index, block],
                )
                for block in range(blocks)
                for index in range(count)
            ],
            count * blocks,
        )

    return call(
        body,
        [IN_HBM] * count,
        [WHOLE] * count,
        [jax.ShapeDtypeStruct(array.shape, array.dtype) for array in arrays],
        [pltpu.SemaphoreType.DMA((count, blocks))],
        vmem=1,
        cost=cost(0, sum(4 * array.size for array in arrays)),
    )(*[hbm(array) for array in arrays])


def split_rows(tokens):
    rows, width = tokens.shape[0] // CHUNKS, tokens.shape[1]

    def body(in_ref, *refs):
        out_refs, sems = refs[:-1], refs[-1]
        run_copies(
            [
                pltpu.make_async_copy(in_ref.at[pl.ds(c * rows, rows)], out_refs[c], sems.at[c])
                for c in range(CHUNKS)
            ],
            CHUNKS,
        )

    return call(
        body,
        [IN_HBM],
        [WHOLE] * CHUNKS,
        [jax.ShapeDtypeStruct((rows, width), tokens.dtype)] * CHUNKS,
        [pltpu.SemaphoreType.DMA((CHUNKS,))],
        vmem=1,
        cost=cost(0, 4 * tokens.size),
    )(hbm(tokens))


def gather_step(held, ways, after):
    moved = {}
    for way in ways:
        value = held[way]
        if after is not None:
            value, _ = lax.optimization_barrier((value, after))
        moved[way] = ring_send(value, way)
    return moved


def accumulate(chunks, first, last, weights, before=None, lead=0):
    rows, depth = chunks[0][0].shape
    width = weights[0].shape[1]
    parts, span = len(weights), last - first
    total = rows * len(chunks)
    final = last == lax.axis_size("head")
    dtype = BF16 if final else F32
    pieces = [chunk[index] for chunk in chunks for index in range(first, last)]

    def body(*refs):
        piece_refs = refs[: len(pieces)]
        weight_refs = refs[len(pieces) : len(pieces) + parts]
        out_ref, left = refs[-2:]
        for index, ref in enumerate(piece_refs):
            chunk, piece = divmod(index, span)
            left[chunk * rows : (chunk + 1) * rows, piece * depth : (piece + 1) * depth] = ref[...]
        for part in range(parts):
            term = mm(left[...], weight_refs[part][first * depth : last * depth])
            if before is not None:
                term = term + refs[-3][lead + part]
            out_ref[part] = term.astype(dtype)

    aliased = before is not None and not final
    args = [*pieces, *weights] + ([] if before is None else [before])
    return call(
        body,
        [WHOLE] * len(args),
        WHOLE,
        jax.ShapeDtypeStruct((parts, total, width), dtype),
        [pltpu.VMEM((total, span * depth), BF16)],
        vmem=12,
        cost=cost(
            2 * total * span * depth * width * parts,
            2 * span * depth * (total + width * parts) + 8 * total * width * parts,
        ),
        aliases={len(args) - 1: 0} if aliased else None,
    )(*args)


def finish(chunk, piece, weights, sums, filled):
    rows, depth = piece.shape
    width = weights[0].shape[1]
    parts = len(weights)
    where = slice(chunk * rows, (chunk + 1) * rows)

    def body(piece_ref, *refs):
        weight_refs, sum_ref = refs[:parts], refs[parts]
        out_ref, far_ref, near_ref = refs[-3:]
        side = lax.axis_index("tok") % 2
        for part in range(parts):
            term = mm(piece_ref[...], weight_refs[part][-depth:]) + sum_ref[part, where]
            out_ref[part, where] = term.astype(BF16)
            far_ref[part, where] = out_ref[part, where, lanes(1 - side, width // 2)]
            near_ref[part, where] = out_ref[part, where, lanes(side, width // 2)]

    total = sums.shape[1]
    args = [piece, *weights, sums, *filled]
    return call(
        body,
        [WHOLE] * len(args),
        [WHOLE] * 3,
        [
            jax.ShapeDtypeStruct((parts, total, size), BF16)
            for size in (width, width // 2, width // 2)
        ],
        cost=cost(2 * rows * depth * width * parts, 2 * width * parts * (depth + 4 * rows)),
        aliases={len(args) - 3 + index: index for index in range(3)} if filled else None,
    )(*args)


def lanes(head, size):
    return pl.ds(pl.multiple_of(head * size, size), size)


def normed(values):
    values = values.astype(F32)
    scale = lax.rsqrt(jnp.mean(values * values, axis=-1, keepdims=True) + 1e-06)
    return (values * scale).astype(BF16)


def head_grads(kv, rate, fast_gate, fast_up, fast_down, before=None):
    rows = kv.shape[1]
    size, hidden_size = fast_gate.shape[1:]
    count = rate.shape[0]
    heads = count // 2
    whole = kv.shape[2] == count * size

    def body(kv_ref, rate_ref, gate_ref, up_ref, down_ref, *rest):
        rates = rate_ref[...].T
        column = lax.broadcasted_iota(jnp.int32, (rows, count), 1)
        for index in range(heads):
            head = first_head(heads) + index
            mine = jnp.sum(jnp.where(column == head, rates, 0.0), axis=1, keepdims=True)
            lane = lanes(head if whole else index, size)
            knorm = normed(kv_ref[0, :, lane])
            target = (-mine * kv_ref[1, :, lane].astype(F32)).astype(BF16)
            gate_pre = mm(knorm, gate_ref[head].astype(BF16))
            up_pre = mm(knorm, up_ref[head].astype(BF16))
            back = mm(target, down_ref[head].astype(BF16), ((1,), (1,)))
            sigma = sigmoid(gate_pre)
            active = gate_pre * sigma
            first = back * up_pre * (sigma + active * (1.0 - sigma))
            both = jnp.concatenate([first.astype(BF16), (back * active).astype(BF16)], axis=1)
            third = (active * up_pre).astype(BF16)
            pair = mm(knorm, both, ((0,), (0,)))
            terms = (pair[:, :hidden_size], pair[:, hidden_size:], mm(target, third, ((0,), (0,))))
            for part, term in enumerate(terms):
                if before is not None:
                    term = term + rest[0][index, part]
                    rest[-1][index, part] = term.astype(BF16)
                    rest[-2][index, part] = term
                else:
                    rest[-1][index, part] = term

    args = [kv, rate, fast_gate, fast_up, fast_down] + ([] if before is None else [before])
    kinds = [F32] if before is None else [F32, BF16]
    return call(
        body,
        [WHOLE] * len(args),
        [WHOLE] * len(kinds),
        [jax.ShapeDtypeStruct((heads, 3, size, hidden_size), kind) for kind in kinds],
        cost=cost(
            12 * heads * rows * size * hidden_size,
            8 * heads * 3 * size * hidden_size,
            heads * rows * hidden_size,
        ),
    )(*args)


def renew(kept, received, step, fast_gate, fast_up, fast_down, after):
    heads, _, size, hidden_size = kept.shape

    def body(step_ref, kept_ref, gate_ref, up_ref, down_ref, *rest):
        out_ref = rest[-1]
        for index in range(heads):
            head = first_head(heads) + index
            for part in range(3):
                grad = kept_ref[index, part]
                for more in rest[: len(received)]:
                    grad = grad + more[index, part].astype(F32)
                if part < 2:
                    matrix = (gate_ref, up_ref)[part][head]
                    fan = size
                else:
                    matrix = down_ref[head].T
                    fan = hidden_size
                mean_sq = jnp.sum(grad * grad, keepdims=True) / (size * hidden_size)
                scale = step_ref[head] * fan ** (-0.5) * lax.rsqrt(mean_sq + 1e-06)
                out_ref[index, part] = (matrix - scale * grad).astype(BF16)

    return call(
        body,
        [SCALARS] + [WHOLE] * (4 + len(received)) + [AFTER] * len(after),
        WHOLE,
        jax.ShapeDtypeStruct(kept.shape, BF16),
        cost=cost(10 * kept.size, 12 * kept.size),
    )(step, kept, fast_gate, fast_up, fast_down, *received, *after)


def attend_blocks(query, blocks):
    factor = query.shape[-1] ** (-0.5) * LOG2E
    scores = []
    for key, _, allowed in blocks:
        part = mm(query, key, ((1,), (1,))) * factor
        scores.append(part if allowed is None else jnp.where(allowed, part, -1e30))
    tops = [jnp.max(part, axis=-1, keepdims=True) for part in scores]
    top = functools.reduce(jnp.maximum, tops)
    result, total = 0.0, 0.0
    for part, (_, value, _) in zip(scores, blocks):
        weight = jnp.exp2(part - top)
        total = total + jnp.sum(weight, axis=-1, keepdims=True)
        result = result + mm(weight.astype(BF16), value)
    return result, top, total


def halves(rows):
    return [slice(index * rows // 2, (index + 1) * rows // 2) for index in range(2)]


def earlier_blocks(ref, index, lane):
    rows = ref.shape[1]
    row = lax.broadcasted_iota(jnp.int32, (rows // 2, rows // 2), 0)
    col = lax.broadcasted_iota(jnp.int32, (rows // 2, rows // 2), 1)
    blocks = [(ref[0, halves(rows)[index], lane], ref[1, halves(rows)[index], lane], col > row)]
    if index == 0:
        blocks.append((ref[0, halves(rows)[1], lane], ref[1, halves(rows)[1], lane], None))
    return blocks


def attend_own(query, kv, size):
    rows = query.shape[1]
    heads = query.shape[2] // size
    row = (rows // 2, rows // 2)

    def body(q_ref, kv_ref, out_ref, stats_ref):
        alone = lax.axis_index("tok") == 0
        causal = lax.broadcasted_iota(jnp.int32, row, 1) <= lax.broadcasted_iota(jnp.int32, row, 0)
        for index, where in enumerate(halves(rows)):
            for head in range(heads):
                lane = slice(head * size, (head + 1) * size)
                blocks = [
                    (kv_ref[0, keys, lane], kv_ref[1, keys, lane], causal if at == index else None)
                    for at, keys in enumerate(halves(rows)[: index + 1])
                ]
                result, top, total = attend_blocks(q_ref[0, where, lane], blocks)
                out_ref[where, lane] = result / jnp.where(alone, total, 1.0)
                stats_ref[0, where, lane] = jnp.broadcast_to(top, result.shape)
                stats_ref[1, where, lane] = jnp.broadcast_to(total, result.shape)

    return call(
        body,
        [WHOLE] * 2,
        [WHOLE] * 2,
        [
            jax.ShapeDtypeStruct((rows, heads * size), F32),
            jax.ShapeDtypeStruct((2, rows, heads * size), F32),
        ],
        cost=cost(3 * heads * size * rows * rows, 8 * rows * heads * size, heads * rows * rows),
    )(query, kv)


def attend_earlier(summed, stats, query, sources, other, size, after=()):
    rows = query.shape[1]
    heads = sources[0].shape[2] // size

    def body(sum_ref, stats_ref, q_ref, *refs):
        out_ref = refs[-1]
        place = lax.axis_index("tok")

        def add(ref):
            for index, where in enumerate(halves(rows)):
                for at in range(heads):
                    lane = lanes(first_head(heads, other) + at, size)
                    result, top, total = attend_blocks(
                        q_ref[0, where, lane],
                        earlier_blocks(ref, index, slice(at * size, (at + 1) * size)),
                    )
                    before = stats_ref[0, where, lane]
                    both = jnp.maximum(before, top)
                    old, new = jnp.exp2(before - both), jnp.exp2(top - both)
                    total = stats_ref[1, where, lane] * old + total * new
                    out_ref[where, lane] = (sum_ref[where, lane] * old + result * new) / total

        if len(sources) == 1:
            pl.when(place > 0)(lambda: add(refs[0]))
        else:
            pl.when((place > 0) & (place % 2 == 0))(lambda: add(refs[0]))
            pl.when(place % 2 == 1)(lambda: add(refs[1]))

    return call(
        body,
        [WHOLE] * (3 + len(sources)) + [AFTER] * len(after),
        WHOLE,
        jax.ShapeDtypeStruct(summed.shape, F32),
        cost=cost(3 * heads * size * rows * rows, 8 * rows * heads * size, heads * rows * rows),
        aliases={0: 0},
    )(summed, stats, query, *sources, *after)


def fast_apply(query, gate, upper, down):
    qnorm = normed(query)
    gate_pre = mm(qnorm, gate)
    hidden = gate_pre * sigmoid(gate_pre) * mm(qnorm, upper)
    return mm(hidden.astype(BF16), down, ((1,), (1,)))


def combine_near(query, attended, nets):
    rows = query.shape[1]
    heads, _, size, hidden_size = nets.shape

    def body(q_ref, attended_ref, net_ref, out_ref):
        for index in range(heads):
            lane = lanes(first_head(heads) + index, size)
            fast = fast_apply(q_ref[0, :, lane], *(net_ref[index, part] for part in range(3)))
            where = slice(index * size, (index + 1) * size)
            out_ref[:, where] = (attended_ref[:, lane] + fast).astype(BF16)

    return call(
        body,
        [WHOLE] * 3,
        WHOLE,
        jax.ShapeDtypeStruct((rows, heads * size), BF16),
        cost=cost(
            6 * heads * rows * size * hidden_size,
            8 * heads * rows * size,
            heads * rows * hidden_size,
        ),
    )(query, attended, nets)


def partial_out(offsets, query, attended, nets, near, w_out, after=()):
    rows = near.shape[0] // lax.axis_size("head")
    heads, _, size, hidden_size = nets.shape
    depth = heads * size
    count = len(offsets)
    width = w_out.shape[1]
    block = width // 8

    def body(q_ref, attended_ref, net_ref, near_ref, w_ref, *refs):
        out_refs, far_ref = refs[len(after) : -1], refs[-1]
        starts = [pl.multiple_of(ring_index(offset) * rows, rows) for offset in offsets]

        def take(ref, lane):
            return jnp.concatenate([ref[pl.ds(start, rows), lane] for start in starts], axis=0)

        for index in range(heads):
            lane = lanes(first_head(heads, True) + index, size)
            fast = fast_apply(
                take(q_ref.at[0], lane), *(net_ref[index, part] for part in range(3))
            )
            where = slice(index * size, (index + 1) * size)
            far_ref[:, where] = (take(attended_ref, lane) + fast).astype(BF16)
        left = take(near_ref, slice(None))
        near_rows = pl.ds(pl.multiple_of(first_head(heads) * size, depth), depth)
        far_rows = pl.ds(pl.multiple_of(first_head(heads, True) * size, depth), depth)
        for column in range(0, width, block):
            result = mm(left, w_ref[near_rows, column : column + block])
            result += mm(far_ref[...], w_ref[far_rows, column : column + block])
            result = result.astype(BF16)
            half, at = divmod(column, width // 2)
            for index in range(count):
                out_refs[2 * index + half][:, at : at + block] = result[
                    index * rows : (index + 1) * rows
                ]

    outs = call(
        body,
        [WHOLE] * 5 + [AFTER] * len(after),
        [WHOLE] * (2 * count),
        [jax.ShapeDtypeStruct((rows, width // 2), BF16)] * (2 * count),
        [pltpu.VMEM((count * rows, depth), BF16)],
        vmem=8,
        cost=cost(4 * count * rows * depth * width, 2 * width * (2 * depth + count * rows)),
    )(query, attended, nets, near, w_out, *after)
    return {offset: tuple(outs[2 * at : 2 * at + 2]) for at, offset in enumerate(offsets)}


def ring_reduce(query, attended, nets, near, w_out):
    steps = lax.axis_size("head") // 2
    signed = [sign * step for step in range(steps - 1, 0, -1) for sign in (1, -1)]
    shared = (query, attended, nets, near, w_out)
    parts = partial_out([steps], *shared) | partial_out(signed[:2], *shared)
    coming = {}
    ordered = ()
    for which in range(2 * steps - 1):
        step, half = steps - (which + 1) // 2, which % 2
        if which % 2 == 0 and 2 <= which <= 2 * (steps - 2):
            later = signed[which : which + 2] + [0] * (which == 2 * (steps - 2))
            parts |= partial_out(later, *shared, tuple(coming.values())[:2])
        terms = []
        for way in (1, -1):
            side = half if way == 1 else 1 - half
            term = parts[steps if step == steps else way * step][side]
            if (way, side) in coming:
                term = (term.astype(F32) + coming[way, side].astype(F32)).astype(BF16)
            terms.append(term)
        terms[0] = lax.optimization_barrier((terms[0], *ordered))[0]
        terms[1] = lax.optimization_barrier((terms[1], terms[0]))[0]
        ordered = terms[1:]
        for way, term in zip((1, -1), terms):
            coming[way, half if way == 1 else 1 - half] = ring_send(term, way)
    sides = {1: 1 - half, -1: half}
    totals = add_pair(
        [parts[0][sides[way]] for way in (1, -1)], [coming.pop((way, sides[way])) for way in (1, -1)]
    )
    totals = {sides[way]: total for way, total in zip((1, -1), totals)}
    ends = [totals[side] for side in range(2)]
    for (_, side), more in coming.items():
        ends[side] = ends[side] + more.astype(F32)
    return jnp.concatenate([end.astype(BF16) for end in ends], axis=1)


def add_pair(own, came):
    def body(*refs):
        for index in range(2):
            refs[4 + index][...] = refs[index][...].astype(F32) + refs[2 + index][...].astype(F32)

    return call(
        body,
        [WHOLE] * 4,
        [WHOLE] * 2,
        [jax.ShapeDtypeStruct(value.shape, F32) for value in own],
        cost=cost(0, 64 * own[0].size),
    )(*own, *came)


def swap(value, bit):
    count = lax.axis_size("tok")
    return lax.ppermute(value, "tok", [(index, index ^ bit) for index in range(count)])


def shards(
    tokens, w_query, w_key, w_value, w_out, fast_gate, fast_up, fast_down, token_rate, head_step
):
    local_heads, head_size, _ = fast_gate.shape
    tok_count = lax.axis_size("tok")
    steps = lax.axis_size("head") // 2
    nets = (fast_gate, fast_up, fast_down)
    rate = token_rate.T
    rate_beside = swap(rate, 1)

    own = split_rows(tokens)
    weights = load([w_key, w_value, w_query])
    chunks = [[piece] for piece in own]
    held = [{1: piece, -1: piece} for piece in own]
    sums, done = None, 0
    for step in range(1, steps + 1):
        after = {2: weights[0], 3: (sums, rate_beside)}.get(step)
        for c in range(CHUNKS):
            last = (1,) if c % 2 == 0 else (-1,)
            held[c] = gather_step(held[c], (1, -1) if step < steps else last, after)
            chunks[c] += held[c].values()
        if step > 1:
            known = [chunk[: 2 * step - 1] for chunk in chunks]
            sums = accumulate(known, done, 2 * step - 1, weights, sums)
            done = 2 * step - 1
    filled = ()
    for c in reversed(range(CHUNKS)):
        filled = finish(c, chunks[c][-1], weights[:2], sums, filled)
    kv, far, near = filled
    query = accumulate(chunks, done, 2 * steps, weights[2:], sums, 2)

    behind = lax.ppermute(far, "tok", [(index, index + 1) for index in range(1, tok_count - 1, 2)])
    beside = swap(far, 1)
    (grads,) = head_grads(kv, rate, *nets)
    grads, travel = head_grads(beside, rate_beside, *nets, grads)
    received = []
    for bit in range(1, tok_count.bit_length() - 1):
        if received:
            travel = grads
            for more in received:
                travel = travel + more.astype(F32)
            travel = travel.astype(BF16)
        received.append(swap(travel, 1 << bit))
    attended, stats = attend_own(query, kv, head_size)
    near, _ = lax.optimization_barrier((near, attended))
    behind_far = lax.ppermute(near, "tok", [(index, index + 1) for index in range(tok_count - 1)])
    attended = attend_earlier(attended, stats, query, (behind, beside), False, head_size)
    mine = renew(grads, received, head_step, *nets, (attended,))
    near = combine_near(query, attended, mine)
    attended = attend_earlier(attended, stats, query, (behind_far,), True, head_size, (near,))
    return ring_reduce(query, attended, swap(mine, 1), near, w_out)


def solution(mesh):
    placed = (
        P("tok", "head"),
        P(None, "head"),
        P(None, "head"),
        P(None, "head"),
        P("head", None),
        P("head", None, None),
        P("head", None, None),
        P("head", None, None),
        P("tok", "head"),
        P("head"),
    )
    return jax.shard_map(
        shards, mesh=mesh, in_specs=placed, out_specs=P(("tok", "head"), None), check_vma=False
    )
```

```python
import functools

import jax
import jax.numpy as jnp
from jax import lax
from jax.experimental import pallas as pl
from jax.experimental.pallas import tpu as pltpu
from jax.sharding import PartitionSpec as P

WINDOW = 512
CHUNKS = 2
F32 = jnp.float32
BF16 = jnp.bfloat16
LOG2E = 1.4426950408889634


def call(body, in_specs, out_specs, out_shape, scratch=(), vmem=8, cost=None, aliases=None):
    return pl.pallas_call(
        body,
        in_specs=in_specs,
        out_specs=out_specs,
        out_shape=out_shape,
        scratch_shapes=list(scratch),
        input_output_aliases=aliases or {},
        cost_estimate=cost,
        compiler_params=pltpu.CompilerParams(vmem_limit_bytes=vmem * 1024 * 1024),
    )


def cost(flops, moved, exps=0):
    return pl.CostEstimate(flops=int(flops), bytes_accessed=int(moved), transcendentals=int(exps))


WHOLE = pl.BlockSpec(memory_space=pltpu.VMEM)
AFTER = pl.BlockSpec(memory_space=pl.ANY)
SCALARS = pl.BlockSpec(memory_space=pltpu.SMEM)
IN_HBM = pl.BlockSpec(memory_space=pltpu.HBM)


def mm(left, right, dims=((1,), (0,))):
    return lax.dot_general(left, right, (dims, ((), ())), preferred_element_type=F32)


def sigmoid(x):
    return 0.5 * jnp.tanh(0.5 * x) + 0.5


def ring_order(count):
    return list(range(0, count, 2)) + list(range(count - 1, 0, -2))


def ring_send(value, step):
    order = ring_order(lax.axis_size("head"))
    count = len(order)
    return lax.ppermute(
        value, "head", [(order[i], order[(i + step) % count]) for i in range(count)]
    )


def ring_offsets():
    steps = lax.axis_size("head") // 2
    return [0] + [way * step for step in range(1, steps) for way in (-1, 1)] + [steps]


def ring_index(offset):
    count = lax.axis_size("head")
    me = lax.axis_index("head")
    at = lax.rem(jnp.where(me % 2 == 0, me // 2, count - 1 - me // 2) + offset + count, count)
    return jnp.where(at < count // 2, 2 * at, 2 * (count - 1 - at) + 1)


def first_head(heads, other=False):
    side = lax.axis_index("tok") % 2
    return (1 - side if other else side) * heads


def hbm(array):
    return pltpu.with_memory_space_constraint(array, pltpu.HBM)


def run_copies(copies, most):
    for index, copy in enumerate(copies):
        if index >= most:
            copies[index - most].wait()
        copy.start()
    for copy in copies[-most:]:
        copy.wait()


def load(arrays):
    count = len(arrays)
    blocks = len(ring_offsets())
    size = arrays[0].shape[0] // blocks

    def body(*refs):
        out_refs, sems = refs[count:-1], refs[-1]
        starts = [pl.multiple_of(ring_index(offset) * size, size) for offset in ring_offsets()]
        run_copies(
            [
                pltpu.make_async_copy(
                    refs[index].at[pl.ds(starts[block], size)],
                    out_refs[index].at[pl.ds(block * size, size)],
                    sems.at[index, block],
                )
                for block in range(blocks)
                for index in range(count)
            ],
            count * blocks,
        )

    return call(
        body,
        [IN_HBM] * count,
        [WHOLE] * count,
        [jax.ShapeDtypeStruct(array.shape, array.dtype) for array in arrays],
        [pltpu.SemaphoreType.DMA((count, blocks))],
        vmem=1,
        cost=cost(0, sum(4 * array.size for array in arrays)),
    )(*[hbm(array) for array in arrays])


def split_rows(tokens):
    rows, width = tokens.shape[0] // CHUNKS, tokens.shape[1]

    def body(in_ref, *refs):
        out_refs, sems = refs[:-1], refs[-1]
        run_copies(
            [
                pltpu.make_async_copy(in_ref.at[pl.ds(c * rows, rows)], out_refs[c], sems.at[c])
                for c in range(CHUNKS)
            ],
            CHUNKS,
        )

    return call(
        body,
        [IN_HBM],
        [WHOLE] * CHUNKS,
        [jax.ShapeDtypeStruct((rows, width), tokens.dtype)] * CHUNKS,
        [pltpu.SemaphoreType.DMA((CHUNKS,))],
        vmem=1,
        cost=cost(0, 4 * tokens.size),
    )(hbm(tokens))


def gather_step(held, ways, after):
    moved = {}
    for way in ways:
        value = held[way]
        if after is not None:
            value, _ = lax.optimization_barrier((value, after))
        moved[way] = ring_send(value, way)
    return moved


def accumulate(chunks, first, last, weights, before=None, lead=0):
    rows, depth = chunks[0][0].shape
    width = weights[0].shape[1]
    parts, span = len(weights), last - first
    total = rows * len(chunks)
    final = last == lax.axis_size("head")
    dtype = BF16 if final else F32
    pieces = [chunk[index] for chunk in chunks for index in range(first, last)]

    def body(*refs):
        piece_refs = refs[: len(pieces)]
        weight_refs = refs[len(pieces) : len(pieces) + parts]
        out_ref, left = refs[-2:]
        for index, ref in enumerate(piece_refs):
            chunk, piece = divmod(index, span)
            left[chunk * rows : (chunk + 1) * rows, piece * depth : (piece + 1) * depth] = ref[...]
        for part in range(parts):
            term = mm(left[...], weight_refs[part][first * depth : last * depth])
            if before is not None:
                term = term + refs[-3][lead + part]
            out_ref[part] = term.astype(dtype)

    aliased = before is not None and not final
    args = [*pieces, *weights] + ([] if before is None else [before])
    return call(
        body,
        [WHOLE] * len(args),
        WHOLE,
        jax.ShapeDtypeStruct((parts, total, width), dtype),
        [pltpu.VMEM((total, span * depth), BF16)],
        vmem=12,
        cost=cost(
            2 * total * span * depth * width * parts,
            2 * span * depth * (total + width * parts) + 8 * total * width * parts,
        ),
        aliases={len(args) - 1: 0} if aliased else None,
    )(*args)


def finish(chunk, piece, weights, sums, filled):
    rows, depth = piece.shape
    width = weights[0].shape[1]
    parts = len(weights)
    where = slice(chunk * rows, (chunk + 1) * rows)

    def body(piece_ref, *refs):
        weight_refs, sum_ref = refs[:parts], refs[parts]
        out_ref, far_ref, near_ref = refs[-3:]
        side = lax.axis_index("tok") % 2
        for part in range(parts):
            term = mm(piece_ref[...], weight_refs[part][-depth:]) + sum_ref[part, where]
            out_ref[part, where] = term.astype(BF16)
            far_ref[part, where] = out_ref[part, where, lanes(1 - side, width // 2)]
            near_ref[part, where] = out_ref[part, where, lanes(side, width // 2)]

    total = sums.shape[1]
    args = [piece, *weights, sums, *filled]
    return call(
        body,
        [WHOLE] * len(args),
        [WHOLE] * 3,
        [
            jax.ShapeDtypeStruct((parts, total, size), BF16)
            for size in (width, width // 2, width // 2)
        ],
        cost=cost(2 * rows * depth * width * parts, 2 * width * parts * (depth + 4 * rows)),
        aliases={len(args) - 3 + index: index for index in range(3)} if filled else None,
    )(*args)


def lanes(head, size):
    return pl.ds(pl.multiple_of(head * size, size), size)


def normed(values):
    values = values.astype(F32)
    scale = lax.rsqrt(jnp.mean(values * values, axis=-1, keepdims=True) + 1e-06)
    return (values * scale).astype(BF16)


def head_grads(kv, rate, fast_gate, fast_up, fast_down, before=None):
    rows = kv.shape[1]
    size, hidden_size = fast_gate.shape[1:]
    count = rate.shape[0]
    heads = count // 2
    whole = kv.shape[2] == count * size

    def body(kv_ref, rate_ref, gate_ref, up_ref, down_ref, *rest):
        rates = rate_ref[...].T
        column = lax.broadcasted_iota(jnp.int32, (rows, count), 1)
        for index in range(heads):
            head = first_head(heads) + index
            mine = jnp.sum(jnp.where(column == head, rates, 0.0), axis=1, keepdims=True)
            lane = lanes(head if whole else index, size)
            knorm = normed(kv_ref[0, :, lane])
            target = (-mine * kv_ref[1, :, lane].astype(F32)).astype(BF16)
            gate_pre = mm(knorm, gate_ref[head].astype(BF16))
            up_pre = mm(knorm, up_ref[head].astype(BF16))
            back = mm(target, down_ref[head].astype(BF16), ((1,), (1,)))
            sigma = sigmoid(gate_pre)
            active = gate_pre * sigma
            first = back * up_pre * (sigma + active * (1.0 - sigma))
            both = jnp.concatenate([first.astype(BF16), (back * active).astype(BF16)], axis=1)
            third = (active * up_pre).astype(BF16)
            pair = mm(knorm, both, ((0,), (0,)))
            terms = (pair[:, :hidden_size], pair[:, hidden_size:], mm(target, third, ((0,), (0,))))
            for part, term in enumerate(terms):
                if before is not None:
                    term = term + rest[0][index, part]
                    rest[-1][index, part] = term.astype(BF16)
                    rest[-2][index, part] = term
                else:
                    rest[-1][index, part] = term

    args = [kv, rate, fast_gate, fast_up, fast_down] + ([] if before is None else [before])
    kinds = [F32] if before is None else [F32, BF16]
    return call(
        body,
        [WHOLE] * len(args),
        [WHOLE] * len(kinds),
        [jax.ShapeDtypeStruct((heads, 3, size, hidden_size), kind) for kind in kinds],
        cost=cost(
            12 * heads * rows * size * hidden_size,
            8 * heads * 3 * size * hidden_size,
            heads * rows * hidden_size,
        ),
    )(*args)


def renew(kept, received, step, fast_gate, fast_up, fast_down, after):
    heads, _, size, hidden_size = kept.shape

    def body(step_ref, kept_ref, gate_ref, up_ref, down_ref, *rest):
        out_ref = rest[-1]
        for index in range(heads):
            head = first_head(heads) + index
            for part in range(3):
                grad = kept_ref[index, part]
                for more in rest[: len(received)]:
                    grad = grad + more[index, part].astype(F32)
                if part < 2:
                    matrix = (gate_ref, up_ref)[part][head]
                    fan = size
                else:
                    matrix = down_ref[head].T
                    fan = hidden_size
                mean_sq = jnp.sum(grad * grad, keepdims=True) / (size * hidden_size)
                scale = step_ref[head] * fan ** (-0.5) * lax.rsqrt(mean_sq + 1e-06)
                out_ref[index, part] = (matrix - scale * grad).astype(BF16)

    return call(
        body,
        [SCALARS] + [WHOLE] * (4 + len(received)) + [AFTER] * len(after),
        WHOLE,
        jax.ShapeDtypeStruct(kept.shape, BF16),
        cost=cost(10 * kept.size, 12 * kept.size),
    )(step, kept, fast_gate, fast_up, fast_down, *received, *after)


def attend_blocks(query, blocks):
    factor = query.shape[-1] ** (-0.5) * LOG2E
    scores = []
    for key, _, allowed in blocks:
        part = mm(query, key, ((1,), (1,))) * factor
        scores.append(part if allowed is None else jnp.where(allowed, part, -1e30))
    tops = [jnp.max(part, axis=-1, keepdims=True) for part in scores]
    top = functools.reduce(jnp.maximum, tops)
    result, total = 0.0, 0.0
    for part, (_, value, _) in zip(scores, blocks):
        weight = jnp.exp2(part - top)
        total = total + jnp.sum(weight, axis=-1, keepdims=True)
        result = result + mm(weight.astype(BF16), value)
    return result, top, total


def halves(rows):
    return [slice(index * rows // 2, (index + 1) * rows // 2) for index in range(2)]


def earlier_blocks(ref, index, lane):
    rows = ref.shape[1]
    row = lax.broadcasted_iota(jnp.int32, (rows // 2, rows // 2), 0)
    col = lax.broadcasted_iota(jnp.int32, (rows // 2, rows // 2), 1)
    blocks = [(ref[0, halves(rows)[index], lane], ref[1, halves(rows)[index], lane], col > row)]
    if index == 0:
        blocks.append((ref[0, halves(rows)[1], lane], ref[1, halves(rows)[1], lane], None))
    return blocks


def attend_own(query, kv, size):
    rows = query.shape[1]
    heads = query.shape[2] // size
    row = (rows // 2, rows // 2)

    def body(q_ref, kv_ref, out_ref, stats_ref):
        alone = lax.axis_index("tok") == 0
        causal = lax.broadcasted_iota(jnp.int32, row, 1) <= lax.broadcasted_iota(jnp.int32, row, 0)
        for index, where in enumerate(halves(rows)):
            for head in range(heads):
                lane = slice(head * size, (head + 1) * size)
                blocks = [
                    (kv_ref[0, keys, lane], kv_ref[1, keys, lane], causal if at == index else None)
                    for at, keys in enumerate(halves(rows)[: index + 1])
                ]
                result, top, total = attend_blocks(q_ref[0, where, lane], blocks)
                out_ref[where, lane] = result / jnp.where(alone, total, 1.0)
                stats_ref[0, where, lane] = jnp.broadcast_to(top, result.shape)
                stats_ref[1, where, lane] = jnp.broadcast_to(total, result.shape)

    return call(
        body,
        [WHOLE] * 2,
        [WHOLE] * 2,
        [
            jax.ShapeDtypeStruct((rows, heads * size), F32),
            jax.ShapeDtypeStruct((2, rows, heads * size), F32),
        ],
        cost=cost(3 * heads * size * rows * rows, 8 * rows * heads * size, heads * rows * rows),
    )(query, kv)


def attend_earlier(summed, stats, query, sources, other, size, after=()):
    rows = query.shape[1]
    heads = sources[0].shape[2] // size

    def body(sum_ref, stats_ref, q_ref, *refs):
        out_ref = refs[-1]
        place = lax.axis_index("tok")

        def add(ref):
            for index, where in enumerate(halves(rows)):
                for at in range(heads):
                    lane = lanes(first_head(heads, other) + at, size)
                    result, top, total = attend_blocks(
                        q_ref[0, where, lane],
                        earlier_blocks(ref, index, slice(at * size, (at + 1) * size)),
                    )
                    before = stats_ref[0, where, lane]
                    both = jnp.maximum(before, top)
                    old, new = jnp.exp2(before - both), jnp.exp2(top - both)
                    total = stats_ref[1, where, lane] * old + total * new
                    out_ref[where, lane] = (sum_ref[where, lane] * old + result * new) / total

        if len(sources) == 1:
            pl.when(place > 0)(lambda: add(refs[0]))
        else:
            pl.when((place > 0) & (place % 2 == 0))(lambda: add(refs[0]))
            pl.when(place % 2 == 1)(lambda: add(refs[1]))

    return call(
        body,
        [WHOLE] * (3 + len(sources)) + [AFTER] * len(after),
        WHOLE,
        jax.ShapeDtypeStruct(summed.shape, F32),
        cost=cost(3 * heads * size * rows * rows, 8 * rows * heads * size, heads * rows * rows),
        aliases={0: 0},
    )(summed, stats, query, *sources, *after)


def fast_apply(query, gate, upper, down):
    qnorm = normed(query)
    gate_pre = mm(qnorm, gate)
    hidden = gate_pre * sigmoid(gate_pre) * mm(qnorm, upper)
    return mm(hidden.astype(BF16), down, ((1,), (1,)))


def combine_near(query, attended, nets):
    rows = query.shape[1]
    heads, _, size, hidden_size = nets.shape

    def body(q_ref, attended_ref, net_ref, out_ref):
        for index in range(heads):
            lane = lanes(first_head(heads) + index, size)
            fast = fast_apply(q_ref[0, :, lane], *(net_ref[index, part] for part in range(3)))
            where = slice(index * size, (index + 1) * size)
            out_ref[:, where] = (attended_ref[:, lane] + fast).astype(BF16)

    return call(
        body,
        [WHOLE] * 3,
        WHOLE,
        jax.ShapeDtypeStruct((rows, heads * size), BF16),
        cost=cost(
            6 * heads * rows * size * hidden_size,
            8 * heads * rows * size,
            heads * rows * hidden_size,
        ),
    )(query, attended, nets)


def partial_out(offsets, query, attended, nets, near, w_out, after=()):
    rows = near.shape[0] // lax.axis_size("head")
    heads, _, size, hidden_size = nets.shape
    depth = heads * size
    count = len(offsets)
    width = w_out.shape[1]
    block = width // 8

    def body(q_ref, attended_ref, net_ref, near_ref, w_ref, *refs):
        out_refs, far_ref = refs[len(after) : -1], refs[-1]
        starts = [pl.multiple_of(ring_index(offset) * rows, rows) for offset in offsets]

        def take(ref, lane):
            return jnp.concatenate([ref[pl.ds(start, rows), lane] for start in starts], axis=0)

        for index in range(heads):
            lane = lanes(first_head(heads, True) + index, size)
            fast = fast_apply(
                take(q_ref.at[0], lane), *(net_ref[index, part] for part in range(3))
            )
            where = slice(index * size, (index + 1) * size)
            far_ref[:, where] = (take(attended_ref, lane) + fast).astype(BF16)
        left = take(near_ref, slice(None))
        near_rows = pl.ds(pl.multiple_of(first_head(heads) * size, depth), depth)
        far_rows = pl.ds(pl.multiple_of(first_head(heads, True) * size, depth), depth)
        for column in range(0, width, block):
            result = mm(left, w_ref[near_rows, column : column + block])
            result += mm(far_ref[...], w_ref[far_rows, column : column + block])
            result = result.astype(BF16)
            half, at = divmod(column, width // 2)
            for index in range(count):
                out_refs[2 * index + half][:, at : at + block] = result[
                    index * rows : (index + 1) * rows
                ]

    outs = call(
        body,
        [WHOLE] * 5 + [AFTER] * len(after),
        [WHOLE] * (2 * count),
        [jax.ShapeDtypeStruct((rows, width // 2), BF16)] * (2 * count),
        [pltpu.VMEM((count * rows, depth), BF16)],
        vmem=8,
        cost=cost(4 * count * rows * depth * width, 2 * width * (2 * depth + count * rows)),
    )(query, attended, nets, near, w_out, *after)
    return {offset: tuple(outs[2 * at : 2 * at + 2]) for at, offset in enumerate(offsets)}


def ring_reduce(query, attended, nets, near, w_out):
    steps = lax.axis_size("head") // 2
    signed = [sign * step for step in range(steps - 1, 0, -1) for sign in (1, -1)]
    shared = (query, attended, nets, near, w_out)
    parts = partial_out([steps], *shared) | partial_out(signed[:2], *shared)
    coming = {}
    ordered = ()
    for which in range(2 * steps - 1):
        step, half = steps - (which + 1) // 2, which % 2
        if which % 2 == 0 and 2 <= which <= 2 * (steps - 2):
            later = signed[which : which + 2] + [0] * (which == 2 * (steps - 2))
            parts |= partial_out(later, *shared, tuple(coming.values())[:2])
        terms = []
        for way in (1, -1):
            side = half if way == 1 else 1 - half
            term = parts[steps if step == steps else way * step][side]
            if (way, side) in coming:
                term = (term.astype(F32) + coming[way, side].astype(F32)).astype(BF16)
            terms.append(term)
        terms[0] = lax.optimization_barrier((terms[0], *ordered))[0]
        terms[1] = lax.optimization_barrier((terms[1], terms[0]))[0]
        ordered = terms[1:]
        for way, term in zip((1, -1), terms):
            coming[way, half if way == 1 else 1 - half] = ring_send(term, way)
    sides = {1: 1 - half, -1: half}
    totals = add_pair(
        [parts[0][sides[way]] for way in (1, -1)], [coming.pop((way, sides[way])) for way in (1, -1)]
    )
    totals = {sides[way]: total for way, total in zip((1, -1), totals)}
    ends = [totals[side] for side in range(2)]
    for (_, side), more in coming.items():
        ends[side] = ends[side] + more.astype(F32)
    return jnp.concatenate([end.astype(BF16) for end in ends], axis=1)


def add_pair(own, came):
    def body(*refs):
        for index in range(2):
            refs[4 + index][...] = refs[index][...].astype(F32) + refs[2 + index][...].astype(F32)

    return call(
        body,
        [WHOLE] * 4,
        [WHOLE] * 2,
        [jax.ShapeDtypeStruct(value.shape, F32) for value in own],
        cost=cost(0, 64 * own[0].size),
    )(*own, *came)


def swap(value, bit):
    count = lax.axis_size("tok")
    return lax.ppermute(value, "tok", [(index, index ^ bit) for index in range(count)])


def shards(
    tokens, w_query, w_key, w_value, w_out, fast_gate, fast_up, fast_down, token_rate, head_step
):
    local_heads, head_size, _ = fast_gate.shape
    tok_count = lax.axis_size("tok")
    steps = lax.axis_size("head") // 2
    nets = (fast_gate, fast_up, fast_down)
    rate = token_rate.T
    rate_beside = swap(rate, 1)

    own = split_rows(tokens)
    weights = load([w_key, w_value, w_query])
    chunks = [[piece] for piece in own]
    held = [{1: piece, -1: piece} for piece in own]
    sums, done = None, 0
    for step in range(1, steps + 1):
        for c in range(CHUNKS):
            last = (1,) if c % 2 == 0 else (-1,)
            after = {(2, 0): weights[0], (2, 1): weights[0], (3, 1): (sums, rate_beside)}.get((step, c))
            held[c] = gather_step(held[c], (1, -1) if step < steps else last, after)
            chunks[c] += held[c].values()
        if step > 1:
            known = [chunk[: 2 * step - 1] for chunk in chunks]
            if step < steps:
                ahead = (known[0][done], *chunks[0][2 * step - 1 :])
                known[0][done] = lax.optimization_barrier(ahead)[0]
            sums = accumulate(known, done, 2 * step - 1, weights, sums)
            done = 2 * step - 1
    filled = ()
    for c in reversed(range(CHUNKS)):
        filled = finish(c, chunks[c][-1], weights[:2], sums, filled)
    kv, far, near = filled
    query = accumulate(chunks, done, 2 * steps, weights[2:], sums, 2)

    behind = lax.ppermute(far, "tok", [(index, index + 1) for index in range(1, tok_count - 1, 2)])
    beside = swap(far, 1)
    (grads,) = head_grads(kv, rate, *nets)
    grads, travel = head_grads(beside, rate_beside, *nets, grads)
    received = []
    for bit in range(1, tok_count.bit_length() - 1):
        if received:
            travel = grads
            for more in received:
                travel = travel + more.astype(F32)
            travel = travel.astype(BF16)
        received.append(swap(travel, 1 << bit))
    attended, stats = attend_own(query, kv, head_size)
    near, _ = lax.optimization_barrier((near, attended))
    behind_far = lax.ppermute(near, "tok", [(index, index + 1) for index in range(tok_count - 1)])
    attended = attend_earlier(attended, stats, query, (behind, beside), False, head_size)
    mine = renew(grads, received, head_step, *nets, (attended,))
    near = combine_near(query, attended, mine)
    attended = attend_earlier(attended, stats, query, (behind_far,), True, head_size, (near,))
    return ring_reduce(query, attended, swap(mine, 1), near, w_out)


def solution(mesh):
    placed = (
        P("tok", "head"),
        P(None, "head"),
        P(None, "head"),
        P(None, "head"),
        P("head", None),
        P("head", None, None),
        P("head", None, None),
        P("head", None, None),
        P("tok", "head"),
        P("head"),
    )
    return jax.shard_map(
        shards, mesh=mesh, in_specs=placed, out_specs=P(("tok", "head"), None), check_vma=False
    )
```
